256 devices in a mesh: gx: 8 (over x, core), gy: 32 (over y, z).
Axes of the slice: x: 4, y: 4, z: 8, core: 2. Of those that a mesh axis runs over, the one named last changes fastest.
Arguments:
- forcing: float32 [8, 32, 256, 512], P('gx', 'gy'), may hold values from -26 to 26
- element_order: int32 [8, 32, 256], P('gx', 'gy'), may hold values from 0 to 255, each once within a row
- diffusivity: float32 [8, 32, 256], P('gx', 'gy'), may hold values from 0.3 to 3
- reaction: float32 [8, 32, 256], P('gx', 'gy'), may hold values from 0.02 to 0.2
- leaf_factor: float32 [8, 32, 153, 256], P('gx', 'gy'), may hold values from -0.21875 to 0.21875
- column_factor: float32 [8, 32, 425, 256], P('gx', 'gy'), may hold values from -1 to 1, as said below
- top_factor: float32 [8, 32, 425, 256], P('gx', 'gy'), may hold values from -1 to 1, as said below
Outputs:
- pressure: float32 [8, 32, 256, 512], P('gx', 'gy')
- residual: float32 [8, 32, 256, 512], P('gx', 'gy')
The draws below stay inside these ranges and needn't reach their ends.
Inputs may be any that keep to these rules, and one draw needn't show every extreme that they name: Each device's element_order holds every structured index of its 256 elements once. `column_factor`: devices that touch the same global vertex hold equal rows for it; rows of vertices with local offset vx = 0 or vx = 4 are zero. `top_factor`: devices that touch the same global vertex hold equal rows for it.
All inputs are finite; a program needn't handle non-finite values.
Results may differ from the reference program's by a relative error of at most 0.0014.
Values sent between devices are 32-bit elements; how exact they have to be, the bound alone decides.
No kernel may reach another device: no remote copies, remote signals or barrier semaphores. Data moves between devices by JAX's collectives and lax.ppermute only.
A program may use at most 128 MiB of HBM per device.

```python
import math
import jax
import jax.numpy as jnp
import numpy as np
from jax import lax

NP = 8
EX = 4
EY = 4
EZ = 16
LEAF = 256
SEP = 256
ELEMS = 256
INNER = 153
N_GX = 8
N_GY = 32


def draw_forcing(key, part):
    key_value, key_scale = jax.random.split(key)
    elements = EX * EY * EZ
    shape_all = (N_GX, N_GY, elements, NP * NP * NP)
    device = (jnp.arange(N_GX)[:, None] * N_GY + jnp.arange(N_GY)[None, :]).astype(jnp.float32)
    rising = 0.5 + 1.5 * device / max(N_GX * N_GY - 1, 1)
    spread = jnp.exp(jax.random.uniform(key_scale, (N_GX, N_GY, elements, 1), jnp.float32, -1.15, 1.15))
    values = jnp.clip(jax.random.normal(key_value, shape_all, jnp.float32), -4.0, 4.0)
    return values * rising[:, :, None, None] * spread


def factor_rows(key, salt, zero_planes):
    vertex_x = jnp.arange(EX + 1)
    vertex_y = jnp.arange(EY + 1)
    global_x = (jnp.arange(N_GX)[:, None, None, None, None] * EX + vertex_x[None, None, :, None, None]) % (EX * N_GX)
    global_y = (jnp.arange(N_GY)[None, :, None, None, None] * EY + vertex_y[None, None, None, :, None]) % (EY * N_GY)
    level = jnp.arange(EZ + 1)[None, None, None, None, :]
    row_ids = (global_x * (EY * N_GY) + global_y) * (EZ + 1) + level
    row_ids = jnp.broadcast_to(row_ids, (N_GX, N_GY, EX + 1, EY + 1, EZ + 1)).reshape(-1).astype(jnp.int32)
    base = jax.random.fold_in(key, salt)

    def one_row(row_at):
        row_key = jax.random.fold_in(base, row_at)
        key_value = jax.random.fold_in(row_key, 0)
        return jnp.clip(jax.random.normal(key_value, (SEP,), jnp.float32), -4.0, 4.0)
    rows = jax.vmap(one_row)(row_ids).reshape(N_GX, N_GY, EX + 1, EY + 1, EZ + 1, SEP)
    if zero_planes:
        planes = jnp.arange(EX + 1)
        keeper = ((planes > 0) & (planes < EX)).astype(jnp.float32)
        rows = rows * keeper[None, None, :, None, None, None]
    return rows.reshape(N_GX, N_GY, (EX + 1) * (EY + 1) * (EZ + 1), SEP)


def draw_column_factor(key, part):
    return factor_rows(key, 11, True) * (3.0 * SEP) ** (-0.5) * N_GY ** (-0.25)


def draw_top_factor(key, part):
    return factor_rows(key, 13, False) * (3.0 * SEP) ** (-0.5) * (N_GX * N_GY) ** (-0.25)


def block_scale(rng, dims, cuts, smallest, top_value):
    gain, own = 1.0, jax.random.fold_in(rng, 6)
    for dim, shards_of in cuts:
        draws = jnp.exp(jax.random.uniform(jax.random.fold_in(own, dim), (shards_of,), jnp.float32, smallest / len(cuts), top_value / len(cuts)))
        gain = gain * jnp.repeat(draws, dims[dim] // shards_of).reshape([-1 if axis == dim else 1 for axis in range(len(dims))])
    return gain


def gaussian(stream_key, shape, scale, limit, cuts=(), held_as=jnp.bfloat16):
    gain = block_scale(stream_key, shape, cuts, -0.22, 0.18) if cuts else 1.0
    result = jax.random.normal(stream_key, shape, jnp.float32) * scale * gain
    return jnp.minimum(jnp.maximum(result, -limit), limit).astype(held_as)


def setup_inputs(seed: int = 0) -> dict:
    splits = jax.random.split(jax.random.key(seed), 8)
    forcing = draw_forcing(jax.random.fold_in(splits[7], 71), 0)
    element_order = jax.vmap(lambda own: jax.random.permutation(own, ELEMS))(jax.random.split(splits[1], N_GX * N_GY)).reshape((N_GX, N_GY, ELEMS)).astype(jnp.int32)
    diffusivity = jnp.clip(jnp.exp(math.log(3.0) - 2.3025851 * jax.random.uniform(splits[2], (N_GX, N_GY, ELEMS), jnp.float32) ** block_scale(splits[2], (N_GX, N_GY, ELEMS), ((0, 8), (1, 32)), -0.2, 0.2)), 0.3, 3.0)
    reaction = jnp.clip(jnp.exp(math.log(0.2) - 2.3025851 * jax.random.uniform(splits[3], (N_GX, N_GY, ELEMS), jnp.float32) ** block_scale(splits[3], (N_GX, N_GY, ELEMS), ((0, 8), (1, 32)), -0.2, 0.2)), 0.02, 0.2)
    leaf_factor = gaussian(splits[4], (N_GX, N_GY, INNER, LEAF), (3 * LEAF) ** -0.5, 0.21875, ((0, 8), (1, 32)), jnp.float32)
    column_factor = draw_column_factor(jax.random.fold_in(splits[7], 71), 0)
    top_factor = draw_top_factor(jax.random.fold_in(splits[7], 71), 0)
    return {"forcing": forcing, "element_order": element_order, "diffusivity": diffusivity, "reaction": reaction, "leaf_factor": leaf_factor, "column_factor": column_factor, "top_factor": top_factor}


def legendre_columns(points, degree):
    columns_table = np.zeros((points.shape[0], degree + 1))
    columns_table[:, 0] = 1.0
    columns_table[:, 1] = points
    for level_at in range(2, degree + 1):
        columns_table[:, level_at] = ((2 * level_at - 1) * points * columns_table[:, level_at - 1] - (level_at - 1) * columns_table[:, level_at - 2]) / level_at
    return columns_table

def jacobi_eigen(symmetric, npoints):
    matrix_work = symmetric.copy()
    vectors = np.eye(npoints)
    for sweep_at in range(15):
        for first_at in range(npoints):
            for second_at in range(first_at + 1, npoints):
                off_value = matrix_work[first_at, second_at]
                gap_value = matrix_work[second_at, second_at] - matrix_work[first_at, first_at]
                root_value = np.sqrt(gap_value * gap_value + 4.0 * off_value * off_value)
                sign_value = np.where(gap_value >= 0.0, 1.0, -1.0)
                denominator = np.abs(gap_value) + root_value
                safe_denominator = np.where(denominator > 0.0, denominator, 1.0)
                tangent = sign_value * 2.0 * off_value / safe_denominator
                cosine_value = 1.0 / np.sqrt(1.0 + tangent * tangent)
                sine_value = tangent * cosine_value
                rotation = np.eye(npoints)
                rotation[first_at, first_at] = cosine_value
                rotation[second_at, second_at] = cosine_value
                rotation[first_at, second_at] = sine_value
                rotation[second_at, first_at] = -sine_value
                matrix_work = rotation.T @ matrix_work @ rotation
                vectors = vectors @ rotation
    eigvals = np.array([matrix_work[place_at, place_at] for place_at in range(npoints)])
    return (eigvals, vectors)

def gll_tables(npoints):
    degree = npoints - 1
    estimate = -np.cos(np.pi * np.arange(npoints) / degree)
    for newton_at in range(100):
        columns_table = legendre_columns(estimate, degree)
        estimate = estimate - (estimate * columns_table[:, degree] - columns_table[:, degree - 1]) / (npoints * columns_table[:, degree])
    points = estimate
    values = legendre_columns(points, degree)[:, degree]
    weights = 2.0 / (degree * (degree + 1) * values ** 2)
    derivative = np.zeros((npoints, npoints))
    for row_at in range(npoints):
        for column_at in range(npoints):
            if row_at != column_at:
                derivative[row_at, column_at] = values[row_at] / values[column_at] / (points[row_at] - points[column_at])
    derivative[0, 0] = -degree * (degree + 1) / 4.0
    derivative[degree, degree] = degree * (degree + 1) / 4.0
    stiffness = derivative.T @ (weights[:, None] * derivative)
    inv_root = 1.0 / np.sqrt(weights)
    symmetric = inv_root[:, None] * stiffness * inv_root[None, :]
    eigvals, eigvecs = jacobi_eigen(0.5 * (symmetric + symmetric.T), npoints)
    modes = inv_root[:, None] * eigvecs
    return (points, weights, stiffness, eigvals, modes)

def build_tables():
    points, weights, stiffness, eigvals, modes = gll_tables(8)
    massmat = weights[:, None] * np.eye(8)
    filler = np.ones(8)
    stiff_full = np.kron(np.kron(stiffness, massmat), massmat) + np.kron(np.kron(massmat, stiffness), massmat) + np.kron(np.kron(massmat, massmat), stiffness)
    mass_full = np.kron(np.kron(weights, weights), weights)
    eigen_full = np.kron(np.kron(eigvals, filler), filler) + np.kron(np.kron(filler, eigvals), filler) + np.kron(np.kron(filler, filler), eigvals)
    shape_full = np.kron(np.kron(modes, modes), modes)
    linear = np.stack([(1.0 - points) / 2.0, (1.0 + points) / 2.0], 1)
    trilinear = np.kron(np.kron(linear, linear), linear)
    return tuple((jnp.asarray(table, dtype=jnp.float32) for table in (stiff_full, mass_full, eigen_full, shape_full, trilinear)))

def weight_table():
    node_index = jnp.arange(NP * NP * NP, dtype=jnp.int32)
    index_x = node_index // (NP * NP)
    index_y = node_index // NP % NP
    index_z = node_index % NP
    count_x = jnp.where((index_x == 0) | (index_x == NP - 1), 2.0, 1.0)
    count_y = jnp.where((index_y == 0) | (index_y == NP - 1), 2.0, 1.0)
    layer_index = jnp.arange(EZ, dtype=jnp.int32)[:, None]
    count_z = jnp.where((index_z[None, :] == 0) & (layer_index > 0) | (index_z[None, :] == NP - 1) & (layer_index < EZ - 1), 2.0, 1.0)
    multiplicity = count_x[None, :] * count_y[None, :] * count_z
    weight = jnp.broadcast_to(1.0 / multiplicity, (EX * EY, EZ, NP * NP * NP)).reshape(EX * EY * EZ, NP * NP * NP)
    return weight.astype(jnp.float32)

def pair_sum(extended, direction):
    length = extended.shape[direction] - 2
    middle = lax.slice_in_dim(extended, 1, length + 1, axis=direction)
    preceding = lax.slice_in_dim(extended, 0, length, axis=direction)
    following = lax.slice_in_dim(extended, 2, length + 2, axis=direction)
    position = lax.broadcasted_iota(jnp.int32, middle.shape, direction) % NP
    return middle + jnp.where(position == 0, preceding, 0.0) + jnp.where(position == NP - 1, following, 0.0)

def assemble_all(element_field):
    lattice = element_field.reshape(N_GX, N_GY, EX, EY, EZ, NP, NP, NP).transpose(0, 2, 5, 1, 3, 6, 4, 7)
    lattice = lattice.reshape(N_GX * EX * NP, N_GY * EY * NP, EZ * NP)
    extended = jnp.concatenate([lattice[-1:], lattice, lattice[:1]], 0)
    lattice = pair_sum(extended, 0)
    extended = jnp.concatenate([lattice[:, -1:], lattice, lattice[:, :1]], 1)
    lattice = pair_sum(extended, 1)
    padded = jnp.pad(lattice, ((0, 0), (0, 0), (1, 1)))
    lattice = pair_sum(padded, 2)
    lattice = lattice.reshape(N_GX, EX, NP, N_GY, EY, NP, EZ, NP).transpose(0, 3, 1, 4, 6, 2, 5, 7)
    return lattice.reshape(N_GX, N_GY, EX * EY * EZ, NP * NP * NP)

def table_product(element_field, table):
    leading = element_field.shape[:-1]
    flat = element_field.reshape(-1, element_field.shape[-1])
    product = jnp.dot(flat, table, precision=lax.Precision.HIGHEST, preferred_element_type=jnp.float32)
    return product.reshape(leading + (table.shape[1],))

def reference(forcing, element_order, diffusivity, reaction, leaf_factor, column_factor, top_factor):
    stiff_table, mass_table, eigen_table, shape_table, linear_table = build_tables()
    inverse = jnp.argsort(element_order, axis=-1).astype(jnp.int32)
    source = jnp.take_along_axis(forcing, inverse[..., None], axis=2)
    diffusion_local = jnp.take_along_axis(diffusivity, inverse, axis=2)[..., None]
    reaction_local = jnp.take_along_axis(reaction, inverse, axis=2)[..., None]
    weight = weight_table()
    reciprocal = 1.0 / (diffusion_local * eigen_table + reaction_local)
    column_own = column_factor.reshape(N_GX, N_GY, EX + 1, EY + 1, EZ + 1, SEP)[:, :, :EX, :EY].reshape(N_GX, N_GY, EX * EY * (EZ + 1), SEP)
    top_own = top_factor.reshape(N_GX, N_GY, EX + 1, EY + 1, EZ + 1, SEP)[:, :, :EX, :EY].reshape(N_GX, N_GY, EX * EY * (EZ + 1), SEP)
    highest = lax.Precision.HIGHEST

    def inner(former, latter):
        return jnp.sum(former * latter * weight)

    def operate(element_field):
        element_term = table_product(element_field, stiff_table) * diffusion_local + element_field * (mass_table * reaction_local)
        return assemble_all(element_term)

    def coarse(residue):
        corner = table_product(residue * weight, linear_table)
        corner = corner.reshape(N_GX, N_GY, EX, EY, EZ, 8).transpose(0, 2, 1, 3, 4, 5).reshape(N_GX * EX, N_GY * EY, EZ, 8)
        vertex = jnp.zeros((N_GX * EX, N_GY * EY, EZ + 1), jnp.float32)
        for shift_x in (0, 1):
            for shift_y in (0, 1):
                for shift_z in (0, 1):
                    piece = jnp.pad(corner[..., shift_x * 4 + shift_y * 2 + shift_z], ((0, 0), (0, 0), (shift_z, 1 - shift_z)))
                    vertex = vertex + jnp.roll(jnp.roll(piece, shift_x, 0), shift_y, 1)
        owned = vertex.reshape(N_GX, EX, N_GY, EY, EZ + 1).transpose(0, 2, 1, 3, 4)
        interior = owned[:, :, 1:, 1:, :].reshape(N_GX, N_GY, -1)
        owned_flat = owned.reshape(N_GX, N_GY, -1)
        leaf_coeffs = jnp.einsum('gavl,gav->gal', leaf_factor, interior, precision=highest)
        column_coeffs = jnp.einsum('gavs,gav->gs', column_own, owned_flat, precision=highest)
        top_coeffs = jnp.einsum('gavs,gav->s', top_own, owned_flat, precision=highest)
        solved = jnp.einsum('gavs,gs->gav', column_own, column_coeffs, precision=highest) + jnp.einsum('gavs,s->gav', top_own, top_coeffs, precision=highest)
        solved = solved.reshape(N_GX, N_GY, EX, EY, EZ + 1)
        leaf_part = jnp.einsum('gavl,gal->gav', leaf_factor, leaf_coeffs, precision=highest).reshape(N_GX, N_GY, EX - 1, EY - 1, EZ + 1)
        solved = solved.at[:, :, 1:, 1:, :].add(leaf_part)
        global_vertex = solved.transpose(0, 2, 1, 3, 4).reshape(N_GX * EX, N_GY * EY, EZ + 1)
        gathered = []
        for shift_x in (0, 1):
            for shift_y in (0, 1):
                for shift_z in (0, 1):
                    moved = jnp.roll(jnp.roll(global_vertex, -shift_x, 0), -shift_y, 1)
                    gathered.append(moved[:, :, shift_z:shift_z + EZ])
        corner_values = jnp.stack(gathered, -1)
        corner_values = corner_values.reshape(N_GX, EX, N_GY, EY, EZ, 8).transpose(0, 2, 1, 3, 4, 5).reshape(N_GX, N_GY, EX * EY * EZ, 8)
        return table_product(corner_values, linear_table.T)

    def precondition(residue):
        spectral = table_product(residue, shape_table) * reciprocal
        smooth = assemble_all(table_product(spectral, shape_table.T)) * weight
        return smooth + coarse(residue)
    assembled = assemble_all(source)
    beta_norm = jnp.sqrt(inner(assembled, assembled))
    basis_one = assembled / beta_norm
    search_one = precondition(basis_one)
    image_one = operate(search_one)
    first_diag = inner(image_one, basis_one)
    remainder = image_one - first_diag * basis_one
    first_sub = jnp.sqrt(inner(remainder, remainder))
    basis_two = remainder / first_sub
    search_two = precondition(basis_two)
    image_two = operate(search_two)
    second_top = inner(image_two, basis_one)
    second_diag = inner(image_two, basis_two)
    remainder = image_two - second_top * basis_one - second_diag * basis_two
    second_sub = jnp.sqrt(inner(remainder, remainder))
    first_norm = jnp.sqrt(first_diag * first_diag + first_sub * first_sub)
    cosine = first_diag / first_norm
    sine_part = first_sub / first_norm
    rotated = cosine * second_top + sine_part * second_diag
    lowered = cosine * second_diag - sine_part * second_top
    second_norm = jnp.sqrt(lowered * lowered + second_sub * second_sub)
    factor_two = -(lowered / second_norm) * sine_part * beta_norm / second_norm
    factor_one = (cosine * beta_norm - rotated * factor_two) / first_norm
    pressure_field = factor_one * search_one + factor_two * search_two
    residual_field = assembled - factor_one * image_one - factor_two * image_two
    pressure = jnp.take_along_axis(pressure_field, element_order[..., None], axis=2)
    residual = jnp.take_along_axis(residual_field, element_order[..., None], axis=2)
    return (pressure, residual)
```

```python
import jax
import jax.numpy as jnp
import numpy as np
from jax import lax
from jax.experimental import pallas as pl
from jax.experimental.pallas import tpu as pltpu
from jax.sharding import PartitionSpec as P

NP = 8
EX = 4
EY = 4
EZ = 16
ROWS = EX * EY * EZ
NODES = NP * NP * NP
LEVELS = EZ + 1
F32 = jnp.float32
BF16 = jnp.bfloat16


def legendre_columns(points, degree):
    columns_table = np.zeros((points.shape[0], degree + 1))
    columns_table[:, 0] = 1.0
    columns_table[:, 1] = points
    for level_at in range(2, degree + 1):
        columns_table[:, level_at] = (
            (2 * level_at - 1) * points * columns_table[:, level_at - 1]
            - (level_at - 1) * columns_table[:, level_at - 2]
        ) / level_at
    return columns_table


def jacobi_eigen(symmetric, npoints):
    matrix_work = symmetric.copy()
    vectors = np.eye(npoints)
    for sweep_at in range(15):
        for first_at in range(npoints):
            for second_at in range(first_at + 1, npoints):
                off_value = matrix_work[first_at, second_at]
                gap_value = matrix_work[second_at, second_at] - matrix_work[first_at, first_at]
                root_value = np.sqrt(gap_value * gap_value + 4.0 * off_value * off_value)
                sign_value = np.where(gap_value >= 0.0, 1.0, -1.0)
                denominator = np.abs(gap_value) + root_value
                safe_denominator = np.where(denominator > 0.0, denominator, 1.0)
                tangent = sign_value * 2.0 * off_value / safe_denominator
                cosine_value = 1.0 / np.sqrt(1.0 + tangent * tangent)
                sine_value = tangent * cosine_value
                rotation = np.eye(npoints)
                rotation[first_at, first_at] = cosine_value
                rotation[second_at, second_at] = cosine_value
                rotation[first_at, second_at] = sine_value
                rotation[second_at, first_at] = -sine_value
                matrix_work = rotation.T @ matrix_work @ rotation
                vectors = vectors @ rotation
    eigvals = np.array([matrix_work[place_at, place_at] for place_at in range(npoints)])
    return (eigvals, vectors)


def gll_tables(npoints):
    degree = npoints - 1
    estimate = -np.cos(np.pi * np.arange(npoints) / degree)
    for newton_at in range(100):
        columns_table = legendre_columns(estimate, degree)
        estimate = estimate - (
            estimate * columns_table[:, degree] - columns_table[:, degree - 1]
        ) / (npoints * columns_table[:, degree])
    values = legendre_columns(estimate, degree)[:, degree]
    weights = 2.0 / (degree * (degree + 1) * values**2)
    derivative = np.zeros((npoints, npoints))
    for row_at in range(npoints):
        for column_at in range(npoints):
            if row_at != column_at:
                derivative[row_at, column_at] = (
                    values[row_at] / values[column_at] / (estimate[row_at] - estimate[column_at])
                )
    derivative[0, 0] = -degree * (degree + 1) / 4.0
    derivative[degree, degree] = degree * (degree + 1) / 4.0
    stiffness = derivative.T @ (weights[:, None] * derivative)
    inv_root = 1.0 / np.sqrt(weights)
    symmetric = inv_root[:, None] * stiffness * inv_root[None, :]
    eigvals, eigvecs = jacobi_eigen(0.5 * (symmetric + symmetric.T), npoints)
    modes = inv_root[:, None] * eigvecs
    return (estimate, weights, stiffness, eigvals, modes)


def split_pair(table):
    high = table.astype(np.float32).astype(jnp.bfloat16)
    low = (table.astype(np.float32) - high.astype(np.float32)).astype(jnp.bfloat16)
    return np.stack([high, low])


def build_tables():
    points, weights, stiffness, eigvals, modes = gll_tables(8)
    massmat = weights[:, None] * np.eye(8)
    filler = np.ones(8)
    stiff_full = (
        np.kron(np.kron(stiffness, massmat), massmat)
        + np.kron(np.kron(massmat, stiffness), massmat)
        + np.kron(np.kron(massmat, massmat), stiffness)
    )
    mass_full = np.kron(np.kron(weights, weights), weights)
    eigen_full = (
        np.kron(np.kron(eigvals, filler), filler)
        + np.kron(np.kron(filler, eigvals), filler)
        + np.kron(np.kron(filler, filler), eigvals)
    )
    shape_full = np.kron(np.kron(modes, modes), modes)
    linear = np.stack([(1.0 - points) / 2.0, (1.0 + points) / 2.0], 1)
    trilinear = np.kron(np.kron(linear, linear), linear)
    ends = np.where((np.arange(8) == 0) | (np.arange(8) == 7), 0.5, 1.0)
    share = np.kron(np.kron(ends, ends), ends)
    rows = np.zeros((8, NODES), np.float32)
    rows[0], rows[1], rows[2] = eigen_full, mass_full, share
    loads = np.zeros((NODES, 128))
    loads[:, :8] = trilinear
    return (
        jnp.asarray(split_pair(stiff_full)),
        jnp.asarray(split_pair(shape_full)),
        jnp.asarray(split_pair(loads)),
        jnp.asarray(split_pair(loads.T)),
        jnp.asarray(rows),
    )


def lanes(width=128):
    return lax.broadcasted_iota(jnp.int32, (1, width), 1)


def halves(x):
    high = x.astype(BF16)
    return high, (x - high.astype(F32)).astype(BF16)


def product(x, table, contract=0):
    high, low = halves(x)
    dims = (((1,), (contract,)), ((), ()))

    def dot(p, q):
        return lax.dot_general(p, q, dims, preferred_element_type=F32)

    return dot(high, table[0]) + (dot(low, table[0]) + dot(high, table[1]))


def permuted(chooser, x):
    high, rest = x.astype(BF16), x
    rest = rest - high.astype(F32)
    mid = rest.astype(BF16)
    low = (rest - mid.astype(F32)).astype(BF16)

    def dot(q):
        return jnp.dot(chooser, q, preferred_element_type=F32)

    return dot(high) + (dot(mid) + dot(low))


def columns(x):
    return [x[:, 128 * c : 128 * c + 128] for c in range(4)]


def weight_of(share):
    lane = lanes(NODES) % NP
    level = lax.broadcasted_iota(jnp.int32, (ROWS, 1), 0) % EZ
    end = ((lane == 0) & (level == 0)) | ((lane == NP - 1) & (level == EZ - 1))
    return jnp.where(end, 2.0 * share, share)


def assemble_inside(cols):
    lane = lanes()
    zero = jnp.zeros((64, 128), F32)
    up = jnp.where(lane < 64, pltpu.roll(cols[3], 64, 1)[:192], 0.0)
    down = jnp.where(lane >= 64, pltpu.roll(cols[0], 64, 1)[64:], 0.0)
    cols = [
        cols[0] + jnp.concatenate([zero, up], 0),
        cols[1],
        cols[2],
        cols[3] + jnp.concatenate([down, zero], 0),
    ]
    row_y = lane // NP % NP
    row_z = lane % NP
    level = lax.broadcasted_iota(jnp.int32, (ROWS, 1), 0) % EZ
    from_below = (row_z == 0) & (level > 0)
    from_above = (row_z == NP - 1) & (level < EZ - 1)
    edge = jnp.zeros((EX, 1, EZ, 128), F32)
    result = []
    for col in cols:
        up = jnp.where(row_y == 0, pltpu.roll(col, 72, 1), 0.0).reshape(EX, EY, EZ, 128)
        down = jnp.where(row_y == NP - 1, pltpu.roll(col, 56, 1), 0.0).reshape(EX, EY, EZ, 128)
        col = (
            col
            + jnp.concatenate([edge, up[:, : EY - 1]], 1).reshape(ROWS, 128)
            + jnp.concatenate([down[:, 1:], edge], 1).reshape(ROWS, 128)
        )
        up = pltpu.roll(pltpu.roll(col, 121, 1), 1, 0)
        down = pltpu.roll(pltpu.roll(col, 7, 1), ROWS - 1, 0)
        result.append(col + jnp.where(from_below, up, 0.0) + jnp.where(from_above, down, 0.0))
    return result


def write_faces(cols, part_ref, face_x_ref, face_y_ref):
    row_y = lanes() // NP % NP
    for c in range(4):
        part_ref[:, 128 * c : 128 * c + 128] = cols[c]
    face_x_ref[0] = cols[0][:64]
    face_x_ref[1] = cols[3][192:]
    low = jnp.zeros((64, 128), F32)
    high = jnp.zeros((64, 128), F32)
    for c in range(4):
        blocks = cols[c].reshape(EX, EY, EZ, 128)
        first = jnp.where(row_y == 0, blocks[:, 0].reshape(64, 128), 0.0)
        last = jnp.where(row_y == NP - 1, blocks[:, EY - 1].reshape(64, 128), 0.0)
        low = low + (pltpu.roll(first, 8 * c, 1) if c else first)
        high = high + pltpu.roll(last, (72 + 8 * c) % 128, 1)
    face_y_ref[0] = low
    face_y_ref[1] = high


def edge_kernel(face_y_ref, before_ref, after_ref, out_low_ref, out_high_ref):
    lane = lanes()
    first = lane < 8
    last = (lane >= 88) & (lane < 96)
    out_low_ref[...] = face_y_ref[0]
    out_high_ref[...] = face_y_ref[1]
    out_low_ref[0:16] += jnp.where(first, pltpu.roll(before_ref[0:16], 64, 1), 0.0)
    out_high_ref[0:16] += jnp.where(first, pltpu.roll(before_ref[48:64], 8, 1), 0.0)
    out_low_ref[48:64] += jnp.where(last, pltpu.roll(after_ref[0:16], 88, 1), 0.0)
    out_high_ref[48:64] += jnp.where(last, pltpu.roll(after_ref[48:64], 32, 1), 0.0)


def finish(part_ref, before_x_ref, after_x_ref, before_y_ref, after_y_ref):
    lane = lanes()
    row_y = lane // NP % NP
    rest = jnp.zeros((192, 128), F32)
    before = jnp.where(lane < 64, pltpu.roll(before_x_ref[...], 64, 1), 0.0)
    after = jnp.where(lane >= 64, pltpu.roll(after_x_ref[...], 64, 1), 0.0)
    before_y, after_y = before_y_ref[...], after_y_ref[...]
    hole = jnp.zeros((EX, EY - 2, EZ, 128), F32)
    result = []
    for c in range(4):
        col = part_ref[:, 128 * c : 128 * c + 128]
        if c == 0:
            col = col + jnp.concatenate([before, rest], 0)
        if c == 3:
            col = col + jnp.concatenate([rest, after], 0)
        low = pltpu.roll(before_y, (128 - 8 * c) % 128, 1) if c else before_y
        low = jnp.where(row_y == 0, low, 0.0).reshape(EX, 1, EZ, 128)
        high = jnp.where(row_y == NP - 1, pltpu.roll(after_y, 56 - 8 * c, 1), 0.0)
        high = high.reshape(EX, 1, EZ, 128)
        result.append(col + jnp.concatenate([low, hole, high], 1).reshape(ROWS, 128))
    return jnp.concatenate(result, 1)


def factor_rows(ref, at, count):
    if at < count - 1:
        return ref[pl.ds(LEVELS * at, 24), :]
    return pltpu.roll(ref[pl.ds(LEVELS * count - 24, 24), :], LEVELS, 0)


def loads_of(unassembled, loads, leaf_ref, column_ref, top_ref, coeff_ref, leaf_out_ref):
    corner = product(unassembled, loads)
    lane = lanes()
    pad = jnp.zeros((8, 128), F32)
    lifted = []
    for at in range(EX * EY):
        piece = corner[16 * at : 16 * at + 16]
        same = jnp.concatenate([jnp.where(lane % 2 == 0, piece, 0.0), pad], 0)
        above = jnp.concatenate([jnp.where(lane % 2 == 1, piece, 0.0), pad], 0)
        lifted.append(same + pltpu.roll(above, 1, 0))
    top_sum = jnp.zeros((24, 256), F32)
    column_sum = jnp.zeros((24, 256), F32)
    leaf_sum = jnp.zeros((24, 256), F32)
    for vx in range(EX + 1):
        for vy in range(EY + 1):
            total = jnp.zeros((24, 128), F32)
            for sx in (0, 1):
                for sy in (0, 1):
                    if 0 <= vx - sx < EX and 0 <= vy - sy < EY:
                        piece = lifted[(vx - sx) * EY + vy - sy]
                        total = total + jnp.where(lane // 2 == sx * 2 + sy, piece, 0.0)
            vertex = jnp.sum(total, axis=1, keepdims=True)
            at = vx * (EY + 1) + vy
            top_sum = top_sum + factor_rows(top_ref, at, 25) * vertex
            if 0 < vx < EX:
                column_sum = column_sum + factor_rows(column_ref, at, 25) * vertex
                if 0 < vy < EY:
                    leaf_sum = leaf_sum + factor_rows(leaf_ref, (vx - 1) * 3 + vy - 1, 9) * vertex
    coeff_ref[...] = jnp.zeros((8, 128), F32)
    for at, total in ((0, top_sum), (4, column_sum)):
        total = jnp.sum(total, axis=0, keepdims=True)
        coeff_ref[at : at + 1] = total[:, :128]
        coeff_ref[at + 1 : at + 2] = total[:, 128:]
    leaf_out_ref[...] = jnp.sum(leaf_sum, axis=0, keepdims=True)


def coarse_of(coeffs, leaf_coeffs, spread, leaf_ref, column_ref, top_ref):
    lane = lanes()
    top = jnp.concatenate([coeffs[0:1], coeffs[1:2]], 1)
    column = jnp.concatenate([coeffs[4:5], coeffs[5:6]], 1)
    around = []
    for vx in range(EX + 1):
        for vy in range(EY + 1):
            at = vx * (EY + 1) + vy
            total = factor_rows(top_ref, at, 25) * top
            if 0 < vx < EX:
                total = total + factor_rows(column_ref, at, 25) * column
                if 0 < vy < EY:
                    total = total + factor_rows(leaf_ref, (vx - 1) * 3 + vy - 1, 9) * leaf_coeffs
            vertex = jnp.sum(total, axis=1, keepdims=True)
            same = jnp.broadcast_to(vertex, (24, 128))
            around.append(jnp.where(lane % 2 == 0, same, pltpu.roll(same, 23, 0))[:16])
    corners = []
    for ex in range(EX):
        for ey in range(EY):
            value = jnp.zeros((16, 128), F32)
            for sx in (0, 1):
                for sy in (0, 1):
                    piece = around[(ex + sx) * (EY + 1) + ey + sy]
                    value = jnp.where(lane // 2 == sx * 2 + sy, piece, value)
            corners.append(value)
    return product(jnp.concatenate(corners, 0), spread)


def start_kernel(
    order_ref, forcing_ref, diffusivity_ref, reaction_ref, leaf_ref, column_ref, top_ref, loads_ref,
    part_ref, face_x_ref, face_y_ref, coeff_ref, leaf_out_ref, pair_ref,
):
    slot = lax.broadcasted_iota(jnp.int32, (ROWS, ROWS), 0)
    chooser = (order_ref[...] == slot).astype(F32)
    diffusion = jnp.sum(chooser * diffusivity_ref[...], axis=1, keepdims=True)
    reacting = jnp.sum(chooser * reaction_ref[...], axis=1, keepdims=True)
    lane = lanes()
    pair_ref[...] = jnp.where(lane == 0, diffusion, reacting)
    source = permuted(chooser.astype(BF16), forcing_ref[...])
    write_faces(assemble_inside(columns(source)), part_ref, face_x_ref, face_y_ref)
    loads_of(source, loads_ref[...], leaf_ref, column_ref, top_ref, coeff_ref, leaf_out_ref)


def smooth_kernel(
    part_ref, before_x_ref, after_x_ref, before_y_ref, after_y_ref, pair_ref, shape_ref, rows_ref,
    field_ref, out_ref, face_x_ref, face_y_ref,
):
    field = finish(part_ref, before_x_ref, after_x_ref, before_y_ref, after_y_ref)
    field_ref[...] = field
    pair = pair_ref[...]
    scale = 1.0 / (pair[:, 0:1] * rows_ref[0:1] + pair[:, 1:2])
    table = shape_ref[...]
    smoothed = product(product(field, table) * scale, table, 1)
    write_faces(assemble_inside(columns(smoothed)), out_ref, face_x_ref, face_y_ref)


def stiffness_of(field, pair, stiff_ref, rows_ref):
    return product(field, stiff_ref[...]) * pair[:, 0:1] + field * (rows_ref[1:2] * pair[:, 1:2])


def total_of(x):
    return jnp.sum(jnp.sum(x, axis=0, keepdims=True), axis=1, keepdims=True)


def numbers_row(values):
    lane = lanes()
    row = jnp.zeros((1, 128), F32)
    for at, value in enumerate(values):
        row = jnp.where(lane == at, value, row)
    return row


def first_kernel(
    part_ref, before_x_ref, after_x_ref, before_y_ref, after_y_ref, pair_ref, stiff_ref, rows_ref,
    loads_ref, spread_ref, leaf_ref, column_ref, top_ref, coeff_in_ref, leaf_in_ref, source_ref,
    search_ref, out_ref, face_x_ref, face_y_ref, coeff_ref, leaf_out_ref,
):
    weight = weight_of(rows_ref[2:3])
    smoothed = finish(part_ref, before_x_ref, after_x_ref, before_y_ref, after_y_ref)
    search = smoothed * weight + coarse_of(
        coeff_in_ref[...], leaf_in_ref[...], spread_ref[...], leaf_ref, column_ref, top_ref
    )
    search_ref[...] = search
    image = stiffness_of(search, pair_ref[...], stiff_ref, rows_ref)
    write_faces(assemble_inside(columns(image)), out_ref, face_x_ref, face_y_ref)
    loads_of(image, loads_ref[...], leaf_ref, column_ref, top_ref, coeff_ref, leaf_out_ref)
    source = source_ref[...]
    coeff_ref[2:3] = numbers_row(
        [total_of(source * source * weight), total_of(image * source), total_of(image * image)]
    )


def second_kernel(
    part_ref, before_x_ref, after_x_ref, before_y_ref, after_y_ref, pair_ref, stiff_ref, rows_ref,
    spread_ref, leaf_ref, column_ref, top_ref, coeff_in_ref, leaf_in_ref, source_ref, search_ref,
    image_ref,
    second_ref, out_ref, face_x_ref, face_y_ref, sums_ref,
):
    weight = weight_of(rows_ref[2:3])
    coeffs = coeff_in_ref[...]
    norm, along, size = coeffs[2:3, 0:1], coeffs[2:3, 1:2], coeffs[2:3, 2:3]
    overlap = along / norm
    scale = 1.0 / jnp.sqrt(size)
    smoothed = finish(part_ref, before_x_ref, after_x_ref, before_y_ref, after_y_ref)
    whole = smoothed * weight + coarse_of(
        coeffs, leaf_in_ref[...], spread_ref[...], leaf_ref, column_ref, top_ref
    )
    second = (whole - overlap * search_ref[...]) * scale
    second_ref[...] = second
    source = source_ref[...]
    basis = (image_ref[...] - overlap * source) * scale
    image = stiffness_of(second, pair_ref[...], stiff_ref, rows_ref)
    write_faces(assemble_inside(columns(image)), out_ref, face_x_ref, face_y_ref)
    sums_ref[...] = numbers_row(
        [total_of(basis * basis * weight), total_of(image * source), total_of(image * basis)]
    )


def last_kernel(
    part_ref, before_x_ref, after_x_ref, before_y_ref, after_y_ref, rows_ref, sums_in_ref,
    image_ref, sums_ref,
):
    image = finish(part_ref, before_x_ref, after_x_ref, before_y_ref, after_y_ref)
    image_ref[...] = image
    square = total_of(image * image * weight_of(rows_ref[2:3]))
    sums_ref[...] = jnp.where(lanes() == 3, square, sums_in_ref[...])


def end_kernel(
    order_ref, sums_ref, coeff_ref, source_ref, search_one_ref, image_one_ref, search_two_ref,
    image_two_ref,
    pressure_ref, residual_ref,
):
    sums = jnp.sum(sums_ref[...], axis=0, keepdims=True)
    squared, dot_source, dot_basis, dot_self = (sums[:, at : at + 1] for at in range(4))
    coeffs = coeff_ref[...]
    norm, along, size = coeffs[2:3, 0:1], coeffs[2:3, 1:2], coeffs[2:3, 2:3]
    beta = jnp.sqrt(norm)
    basis_norm = jnp.sqrt(squared)
    first_diag = along / norm
    first_sub = basis_norm * jnp.sqrt(size) / beta
    second_top = dot_source / (beta * basis_norm)
    second_diag = dot_basis / squared
    second_sub_squared = jnp.maximum(
        dot_self / squared - second_top * second_top - second_diag * second_diag, 0.0
    )
    first_norm = jnp.sqrt(first_diag * first_diag + first_sub * first_sub)
    cosine = first_diag / first_norm
    sine_part = first_sub / first_norm
    rotated = cosine * second_top + sine_part * second_diag
    lowered = cosine * second_diag - sine_part * second_top
    second_norm = jnp.sqrt(lowered * lowered + second_sub_squared)
    factor_two = -(lowered / second_norm) * sine_part * beta / second_norm
    factor_one = (cosine * beta - rotated * factor_two) / first_norm
    step_one = factor_one / beta
    step_two = factor_two / basis_norm
    slot = lax.broadcasted_iota(jnp.int32, (ROWS, ROWS), 0)
    chooser = (order_ref[...] == slot).astype(F32).T.astype(BF16)
    pressure_ref[...] = permuted(
        chooser, step_one * search_one_ref[...] + step_two * search_two_ref[...]
    )
    residual_ref[...] = permuted(
        chooser, source_ref[...] - step_one * image_one_ref[...] - step_two * image_two_ref[...]
    )


FIELD = jax.ShapeDtypeStruct((ROWS, NODES), F32)
FACES = jax.ShapeDtypeStruct((2, 64, 128), F32)
FACE = jax.ShapeDtypeStruct((64, 128), F32)
COEFFS = jax.ShapeDtypeStruct((8, 128), F32)
LEAVES = jax.ShapeDtypeStruct((1, 256), F32)
NUMBERS = jax.ShapeDtypeStruct((1, 128), F32)
PAIRS = jax.ShapeDtypeStruct((ROWS, 128), F32)


def run(kernel, outs, *args):
    vmem = pl.BlockSpec(memory_space=pltpu.VMEM)
    return pl.pallas_call(
        kernel,
        out_shape=outs,
        in_specs=[vmem] * len(args),
        out_specs=tuple(vmem for _ in outs),
        compiler_params=pltpu.CompilerParams(vmem_limit_bytes=24 * 2**20),
    )(*args)


def neighbours(low, high, axis):
    peers = lax.axis_size(axis)
    up = [(i, (i + 1) % peers) for i in range(peers)]
    down = [(j, i) for i, j in up]
    return lax.ppermute(high, axis, up), lax.ppermute(low, axis, down)


def exchanged(face_x, face_y):
    before_x, after_x = neighbours(face_x[0], face_x[1], "gx")
    low, high = run(edge_kernel, (FACE, FACE), face_y, before_x, after_x)
    before_y, after_y = neighbours(low, high, "gy")
    return before_x, after_x, before_y, after_y


def summed(coeffs):
    shared = lax.psum(coeffs[:4], "gx")
    mine = jnp.concatenate([shared, coeffs[4:]], 0)
    peers = lax.axis_size("gy")
    spread = jnp.broadcast_to(mine[None], (peers, 8, 128))
    return jnp.sum(lax.all_to_all(spread, "gy", 0, 0), 0)


def per_device(
    forcing, element_order, diffusivity, reaction, leaf_factor, column_factor, top_factor
):
    stiff, shape, loads, spread, rows = build_tables()
    factors = (leaf_factor[0, 0], column_factor[0, 0], top_factor[0, 0])
    order = element_order[0]
    part, face_x, face_y, coeffs, leaves, pair = run(
        start_kernel,
        (FIELD, FACES, FACES, COEFFS, LEAVES, PAIRS),
        order, forcing[0, 0], diffusivity[0], reaction[0], *factors, loads,
    )
    coeffs = summed(coeffs)
    source, part, face_x, face_y = run(
        smooth_kernel, (FIELD, FIELD, FACES, FACES), part, *exchanged(face_x, face_y), pair, shape, rows
    )
    search_one, part, face_x, face_y, coeffs, leaves = run(
        first_kernel,
        (FIELD, FIELD, FACES, FACES, COEFFS, LEAVES),
        part, *exchanged(face_x, face_y), pair, stiff, rows, loads, spread, *factors, coeffs, leaves,
        source,
    )
    coeffs = summed(coeffs)
    image_one, part, face_x, face_y = run(
        smooth_kernel, (FIELD, FIELD, FACES, FACES), part, *exchanged(face_x, face_y), pair, shape, rows
    )
    search_two, part, face_x, face_y, sums = run(
        second_kernel,
        (FIELD, FIELD, FACES, FACES, NUMBERS),
        part, *exchanged(face_x, face_y), pair, stiff, rows, spread, *factors, coeffs, leaves, source,
        search_one, image_one,
    )
    image_two, sums = run(
        last_kernel, (FIELD, NUMBERS), part, *exchanged(face_x, face_y), rows, sums
    )
    peers = lax.axis_size(("gx", "gy"))
    sums = lax.all_to_all(jnp.broadcast_to(sums, (peers, 128)), ("gx", "gy"), 0, 0, tiled=True)
    pressure, residual = run(
        end_kernel, (FIELD, FIELD),
        order, sums, coeffs, source, search_one, image_one, search_two, image_two,
    )
    return (pressure[None, None], residual[None, None])


def solution(mesh):
    field = P("gx", "gy", None, None)
    row = P("gx", "gy", None)
    return jax.shard_map(
        per_device,
        mesh=mesh,
        in_specs=(field, row, row, row, field, field, field),
        out_specs=(field, field),
        check_vma=False,
    )
```

```python
import jax
import jax.numpy as jnp
import numpy as np
from jax import lax
from jax.experimental import pallas as pl
from jax.experimental.pallas import tpu as pltpu
from jax.sharding import PartitionSpec as P

NP = 8
EX = 4
EY = 4
EZ = 16
ROWS = EX * EY * EZ
NODES = NP * NP * NP
LEVELS = EZ + 1
F32 = jnp.float32
BF16 = jnp.bfloat16


def legendre_columns(points, degree):
    columns_table = np.zeros((points.shape[0], degree + 1))
    columns_table[:, 0] = 1.0
    columns_table[:, 1] = points
    for level_at in range(2, degree + 1):
        columns_table[:, level_at] = (
            (2 * level_at - 1) * points * columns_table[:, level_at - 1]
            - (level_at - 1) * columns_table[:, level_at - 2]
        ) / level_at
    return columns_table


def jacobi_eigen(symmetric, npoints):
    matrix_work = symmetric.copy()
    vectors = np.eye(npoints)
    for sweep_at in range(15):
        for first_at in range(npoints):
            for second_at in range(first_at + 1, npoints):
                off_value = matrix_work[first_at, second_at]
                gap_value = matrix_work[second_at, second_at] - matrix_work[first_at, first_at]
                root_value = np.sqrt(gap_value * gap_value + 4.0 * off_value * off_value)
                sign_value = np.where(gap_value >= 0.0, 1.0, -1.0)
                denominator = np.abs(gap_value) + root_value
                safe_denominator = np.where(denominator > 0.0, denominator, 1.0)
                tangent = sign_value * 2.0 * off_value / safe_denominator
                cosine_value = 1.0 / np.sqrt(1.0 + tangent * tangent)
                sine_value = tangent * cosine_value
                rotation = np.eye(npoints)
                rotation[first_at, first_at] = cosine_value
                rotation[second_at, second_at] = cosine_value
                rotation[first_at, second_at] = sine_value
                rotation[second_at, first_at] = -sine_value
                matrix_work = rotation.T @ matrix_work @ rotation
                vectors = vectors @ rotation
    eigvals = np.array([matrix_work[place_at, place_at] for place_at in range(npoints)])
    return (eigvals, vectors)


def gll_tables(npoints):
    degree = npoints - 1
    estimate = -np.cos(np.pi * np.arange(npoints) / degree)
    for newton_at in range(100):
        columns_table = legendre_columns(estimate, degree)
        estimate = estimate - (
            estimate * columns_table[:, degree] - columns_table[:, degree - 1]
        ) / (npoints * columns_table[:, degree])
    values = legendre_columns(estimate, degree)[:, degree]
    weights = 2.0 / (degree * (degree + 1) * values**2)
    derivative = np.zeros((npoints, npoints))
    for row_at in range(npoints):
        for column_at in range(npoints):
            if row_at != column_at:
                derivative[row_at, column_at] = (
                    values[row_at] / values[column_at] / (estimate[row_at] - estimate[column_at])
                )
    derivative[0, 0] = -degree * (degree + 1) / 4.0
    derivative[degree, degree] = degree * (degree + 1) / 4.0
    stiffness = derivative.T @ (weights[:, None] * derivative)
    inv_root = 1.0 / np.sqrt(weights)
    symmetric = inv_root[:, None] * stiffness * inv_root[None, :]
    eigvals, eigvecs = jacobi_eigen(0.5 * (symmetric + symmetric.T), npoints)
    modes = inv_root[:, None] * eigvecs
    return (estimate, weights, stiffness, eigvals, modes)


def split_pair(table):
    high = table.astype(np.float32).astype(jnp.bfloat16)
    low = (table.astype(np.float32) - high.astype(np.float32)).astype(jnp.bfloat16)
    return np.stack([high, low])


def build_tables():
    points, weights, stiffness, eigvals, modes = gll_tables(8)
    massmat = weights[:, None] * np.eye(8)
    filler = np.ones(8)
    stiff_full = (
        np.kron(np.kron(stiffness, massmat), massmat)
        + np.kron(np.kron(massmat, stiffness), massmat)
        + np.kron(np.kron(massmat, massmat), stiffness)
    )
    mass_full = np.kron(np.kron(weights, weights), weights)
    eigen_full = (
        np.kron(np.kron(eigvals, filler), filler)
        + np.kron(np.kron(filler, eigvals), filler)
        + np.kron(np.kron(filler, filler), eigvals)
    )
    shape_full = np.kron(np.kron(modes, modes), modes)
    linear = np.stack([(1.0 - points) / 2.0, (1.0 + points) / 2.0], 1)
    trilinear = np.kron(np.kron(linear, linear), linear)
    ends = np.where((np.arange(8) == 0) | (np.arange(8) == 7), 0.5, 1.0)
    share = np.kron(np.kron(ends, ends), ends)
    rows = np.zeros((8, NODES), np.float32)
    rows[0], rows[1], rows[2] = eigen_full, mass_full, share
    loads = np.zeros((NODES, 128))
    loads[:, :8] = trilinear
    return (
        jnp.asarray(split_pair(stiff_full)),
        jnp.asarray(split_pair(shape_full)),
        jnp.asarray(split_pair(loads)),
        jnp.asarray(split_pair(loads.T)),
        jnp.asarray(rows),
    )


def lanes(width=128):
    return lax.broadcasted_iota(jnp.int32, (1, width), 1)


def halves(x):
    high = x.astype(BF16)
    return high, (x - high.astype(F32)).astype(BF16)


def product(x, table, contract=0):
    high, low = halves(x)
    dims = (((1,), (contract,)), ((), ()))

    def dot(p, q):
        return lax.dot_general(p, q, dims, preferred_element_type=F32)

    return dot(high, table[0]) + (dot(low, table[0]) + dot(high, table[1]))


def permuted(chooser, x):
    high, rest = x.astype(BF16), x
    rest = rest - high.astype(F32)
    mid = rest.astype(BF16)
    low = (rest - mid.astype(F32)).astype(BF16)

    def dot(q):
        return jnp.dot(chooser, q, preferred_element_type=F32)

    return dot(high) + (dot(mid) + dot(low))


def columns(x):
    return [x[:, 128 * c : 128 * c + 128] for c in range(4)]


def weight_of(share):
    lane = lanes(NODES) % NP
    level = lax.broadcasted_iota(jnp.int32, (ROWS, 1), 0) % EZ
    end = ((lane == 0) & (level == 0)) | ((lane == NP - 1) & (level == EZ - 1))
    return jnp.where(end, 2.0 * share, share)


def first_plane(x):
    return jnp.where(lanes() < 64, roll_lanes(x, 64), 0.0)


def last_plane(x):
    return jnp.where(lanes() >= 64, roll_lanes(x, 64), 0.0)


def first_row(x):
    return jnp.where(lanes() // NP % NP == 0, roll_lanes(x, 72), 0.0)


def last_row(x):
    return jnp.where(lanes() // NP % NP == NP - 1, roll_lanes(x, 56), 0.0)


def roll_lanes(x, shift):
    return pltpu.roll(x.reshape(-1, 128), shift, 1).reshape(x.shape)


def sum_levels(col):
    rows = col.shape[0]
    row_z = lanes() % NP
    level = lax.broadcasted_iota(jnp.int32, (rows, 1), 0) % EZ
    up = pltpu.roll(pltpu.roll(col, 121, 1), 1, 0)
    down = pltpu.roll(pltpu.roll(col, 7, 1), rows - 1, 0)
    return (
        col
        + jnp.where((row_z == 0) & (level > 0), up, 0.0)
        + jnp.where((row_z == NP - 1) & (level < EZ - 1), down, 0.0)
    )


def blocks(col, length=EY):
    return col.reshape(-1, length, EZ, 128)


def assemble_inside(cols):
    cols = [blocks(col) for col in cols]
    edge = jnp.zeros((1, EY, EZ, 128), F32)
    cols = [
        cols[0] + jnp.concatenate([edge, first_plane(cols[3][: EX - 1])], 0),
        cols[1],
        cols[2],
        cols[3] + jnp.concatenate([last_plane(cols[0][1:]), edge], 0),
    ]
    edge = jnp.zeros((EX, 1, EZ, 128), F32)
    result = []
    for col in cols:
        col = (
            col
            + jnp.concatenate([edge, first_row(col[:, : EY - 1])], 1)
            + jnp.concatenate([last_row(col[:, 1:]), edge], 1)
        )
        result.append(sum_levels(col.reshape(ROWS, 128)))
    return result


def joined_x(own, left, right):
    own, left, right = list(own), list(left), list(right)
    low, high = own[0], own[3]
    tail = jnp.zeros_like(low[1:])
    own[0] = low + jnp.concatenate([first_plane(left[3]), tail], 0)
    own[3] = high + jnp.concatenate([tail, last_plane(right[0])], 0)
    left[3] = left[3] + last_plane(low[:1])
    right[0] = right[0] + first_plane(high[EX - 1 :])
    return [jnp.concatenate(parts, 0) for parts in zip(left, own, right)]


def joined_y(middle, below, above):
    first, last = middle[:, :1], middle[:, EY - 1 :]
    hole = jnp.zeros_like(middle[:, 1 : EY - 1])
    middle = middle + jnp.concatenate([first_row(below), hole, last_row(above)], 1)
    return jnp.concatenate([below + last_row(first), middle, above + first_row(last)], 1)


def assemble_wide(cols):
    cols = [
        cols[0][1:-1] + first_plane(cols[3][:-2]),
        cols[1][1:-1],
        cols[2][1:-1],
        cols[3][1:-1] + last_plane(cols[0][2:]),
    ]
    return [
        sum_levels((col[:, 1:-1] + first_row(col[:, :-2]) + last_row(col[:, 2:])).reshape(ROWS, 128))
        for col in cols
    ]


def write_faces(cols, part_ref, face_left_ref, face_right_ref, face_y_ref):
    row_y = lanes() // NP % NP
    for c in range(4):
        part_ref[:, 128 * c : 128 * c + 128] = cols[c]
    face_left_ref[...] = cols[0][:64]
    face_right_ref[...] = cols[3][192:]
    low = jnp.zeros((64, 128), F32)
    high = jnp.zeros((64, 128), F32)
    for c in range(4):
        split = cols[c].reshape(EX, EY, EZ, 128)
        first = jnp.where(row_y == 0, split[:, 0].reshape(64, 128), 0.0)
        last = jnp.where(row_y == NP - 1, split[:, EY - 1].reshape(64, 128), 0.0)
        low = low + (pltpu.roll(first, 8 * c, 1) if c else first)
        high = high + pltpu.roll(last, (72 + 8 * c) % 128, 1)
    face_y_ref[0] = low
    face_y_ref[1] = high


def write_planes(cols, part_ref, left_ref, right_ref):
    for c in range(4):
        at = slice(128 * c, 128 * c + 128)
        part_ref[:, at] = cols[c]
        left_ref[:, at] = cols[c][:64]
        right_ref[:, at] = cols[c][192:]


def edge_kernel(face_y_ref, before_ref, after_ref, out_low_ref, out_high_ref):
    lane = lanes()
    first = lane < 8
    last = (lane >= 88) & (lane < 96)
    out_low_ref[...] = face_y_ref[0]
    out_high_ref[...] = face_y_ref[1]
    out_low_ref[0:16] += jnp.where(first, pltpu.roll(before_ref[0:16], 64, 1), 0.0)
    out_high_ref[0:16] += jnp.where(first, pltpu.roll(before_ref[48:64], 8, 1), 0.0)
    out_low_ref[48:64] += jnp.where(last, pltpu.roll(after_ref[0:16], 88, 1), 0.0)
    out_high_ref[48:64] += jnp.where(last, pltpu.roll(after_ref[48:64], 32, 1), 0.0)


def finish(part_ref, before_x_ref, after_x_ref, before_y_ref, after_y_ref):
    lane = lanes()
    row_y = lane // NP % NP
    rest = jnp.zeros((192, 128), F32)
    before = jnp.where(lane < 64, pltpu.roll(before_x_ref[...], 64, 1), 0.0)
    after = jnp.where(lane >= 64, pltpu.roll(after_x_ref[...], 64, 1), 0.0)
    before_y, after_y = before_y_ref[...], after_y_ref[...]
    hole = jnp.zeros((EX, EY - 2, EZ, 128), F32)
    result = []
    for c in range(4):
        col = part_ref[:, 128 * c : 128 * c + 128]
        if c == 0:
            col = col + jnp.concatenate([before, rest], 0)
        if c == 3:
            col = col + jnp.concatenate([rest, after], 0)
        low = pltpu.roll(before_y, (128 - 8 * c) % 128, 1) if c else before_y
        low = jnp.where(row_y == 0, low, 0.0).reshape(EX, 1, EZ, 128)
        high = jnp.where(row_y == NP - 1, pltpu.roll(after_y, 56 - 8 * c, 1), 0.0)
        high = high.reshape(EX, 1, EZ, 128)
        result.append(col + jnp.concatenate([low, hole, high], 1).reshape(ROWS, 128))
    return jnp.concatenate(result, 1)


def factor_rows(ref, at, count):
    if at < count - 1:
        return ref[pl.ds(LEVELS * at, 24), :]
    return pltpu.roll(ref[pl.ds(LEVELS * count - 24, 24), :], LEVELS, 0)


def loads_of(unassembled, loads, leaf_ref, column_ref, top_ref, coeff_ref, leaf_out_ref, numbers):
    corner = product(unassembled, loads)
    lane = lanes()
    pad = jnp.zeros((8, 128), F32)
    lifted = []
    for at in range(EX * EY):
        piece = corner[16 * at : 16 * at + 16]
        same = jnp.concatenate([jnp.where(lane % 2 == 0, piece, 0.0), pad], 0)
        above = jnp.concatenate([jnp.where(lane % 2 == 1, piece, 0.0), pad], 0)
        lifted.append(same + pltpu.roll(above, 1, 0))
    top_sum = jnp.zeros((24, 256), F32)
    column_sum = jnp.zeros((24, 256), F32)
    leaf_sum = jnp.zeros((24, 256), F32)
    for vx in range(EX + 1):
        for vy in range(EY + 1):
            total = jnp.zeros((24, 128), F32)
            for sx in (0, 1):
                for sy in (0, 1):
                    if 0 <= vx - sx < EX and 0 <= vy - sy < EY:
                        piece = lifted[(vx - sx) * EY + vy - sy]
                        total = total + jnp.where(lane // 2 == sx * 2 + sy, piece, 0.0)
            vertex = jnp.sum(total, axis=1, keepdims=True)
            at = vx * (EY + 1) + vy
            top_sum = top_sum + factor_rows(top_ref, at, 25) * vertex
            if 0 < vx < EX:
                column_sum = column_sum + factor_rows(column_ref, at, 25) * vertex
                if 0 < vy < EY:
                    leaf_sum = leaf_sum + factor_rows(leaf_ref, (vx - 1) * 3 + vy - 1, 9) * vertex
    row = lax.broadcasted_iota(jnp.int32, (8, 1), 0)
    coeffs = jnp.where(row == 2, numbers, 0.0)
    for at, total in ((0, top_sum), (4, column_sum)):
        total = jnp.sum(total, axis=0, keepdims=True)
        coeffs = jnp.where(row == at, total[:, :128], coeffs)
        coeffs = jnp.where(row == at + 1, total[:, 128:], coeffs)
    coeff_ref[...] = jnp.broadcast_to(coeffs[None], coeff_ref.shape)
    leaf_out_ref[...] = jnp.sum(leaf_sum, axis=0, keepdims=True)


def coarse_of(coeffs, leaf_coeffs, spread, leaf_ref, column_ref, top_ref):
    lane = lanes()
    top = jnp.concatenate([coeffs[0:1], coeffs[1:2]], 1)
    column = jnp.concatenate([coeffs[4:5], coeffs[5:6]], 1)
    around = []
    for vx in range(EX + 1):
        for vy in range(EY + 1):
            at = vx * (EY + 1) + vy
            total = factor_rows(top_ref, at, 25) * top
            if 0 < vx < EX:
                total = total + factor_rows(column_ref, at, 25) * column
                if 0 < vy < EY:
                    total = total + factor_rows(leaf_ref, (vx - 1) * 3 + vy - 1, 9) * leaf_coeffs
            vertex = jnp.sum(total, axis=1, keepdims=True)
            same = jnp.broadcast_to(vertex, (24, 128))
            around.append(jnp.where(lane % 2 == 0, same, pltpu.roll(same, 23, 0))[:16])
    corners = []
    for ex in range(EX):
        for ey in range(EY):
            value = jnp.zeros((16, 128), F32)
            for sx in (0, 1):
                for sy in (0, 1):
                    piece = around[(ex + sx) * (EY + 1) + ey + sy]
                    value = jnp.where(lane // 2 == sx * 2 + sy, piece, value)
            corners.append(value)
    return product(jnp.concatenate(corners, 0), spread)


def total_of(x):
    return jnp.sum(jnp.sum(x, axis=0, keepdims=True), axis=1, keepdims=True)


def numbers_row(values):
    lane = lanes()
    row = jnp.zeros((1, 128), F32)
    for at, value in enumerate(values):
        row = jnp.where(lane == at, value, row)
    return row


def start_kernel(
    order, forcing, diffusivity, reaction, loads, leaf, column, top,
    part_ref, left_ref, right_ref, coeff_ref, leaf_out_ref, pair_ref,
):
    slot = lax.broadcasted_iota(jnp.int32, (ROWS, ROWS), 0)
    chooser = (order()[...] == slot).astype(F32)
    diffusion = jnp.sum(chooser * diffusivity()[...], axis=1, keepdims=True)
    reacting = jnp.sum(chooser * reaction()[...], axis=1, keepdims=True)
    pair = jnp.where(lanes() == 0, diffusion, reacting)
    pair_ref[...] = pair
    left_ref[:, NODES:] = pair[:64]
    right_ref[:, NODES:] = pair[192:]
    source = permuted(chooser.astype(BF16), forcing()[...])
    write_planes(assemble_inside(columns(source)), part_ref, left_ref, right_ref)
    loads_of(
        source, loads()[...], leaf(), column(), top(), coeff_ref, leaf_out_ref, numbers_row([])
    )


def rows_of_plane(ref, c, plane):
    return blocks(ref[:, 128 * c : 128 * c + 128])[:, plane : plane + 1]


def middle_kernel(part_ref, left_ref, right_ref, own_ref, gathered_ref, *refs):
    with_pair = len(refs) == 4
    low_ref, high_ref, spread_ref = refs[-3:]
    row = lax.broadcasted_iota(jnp.int32, (8, 1), 0)
    coeffs = jnp.where(row < 4, jnp.sum(gathered_ref[...], axis=0), own_ref[0])
    spread_ref[...] = jnp.broadcast_to(coeffs[None], spread_ref.shape)
    for plane, out_ref in ((0, low_ref), (EY - 1, high_ref)):
        sides = [
            [rows_of_plane(ref, c, plane) for c in range(4)] for ref in (part_ref, left_ref, right_ref)
        ]
        for c, col in enumerate(joined_x(*sides)):
            out_ref[:, 128 * c : 128 * c + 128] = col.reshape(-1, 128)
        if with_pair:
            sides = [rows_of_plane(left_ref, 4, plane), rows_of_plane(refs[0], 0, plane)]
            sides.append(rows_of_plane(right_ref, 4, plane))
            out_ref[:, NODES:] = jnp.concatenate(sides, 0).reshape(-1, 128)


def wide_field(part_ref, left_ref, right_ref, below_ref, above_ref):
    sides = [
        [blocks(ref[:, 128 * c : 128 * c + 128]) for c in range(4)]
        for ref in (part_ref, left_ref, right_ref)
    ]
    result = []
    for c, middle in enumerate(joined_x(*sides)):
        at = slice(128 * c, 128 * c + 128)
        result.append(joined_y(middle, blocks(below_ref[:, at], 1), blocks(above_ref[:, at], 1)))
    return result


def inner_rows(cols):
    return jnp.concatenate([col[1:-1, 1:-1].reshape(ROWS, 128) for col in cols], 1)


def smoothed_of(cols, pair, shape, rows):
    wide = jnp.concatenate([col.reshape(-1, 128) for col in cols], 1)
    scale = 1.0 / (pair[:, 0:1] * rows[0:1] + pair[:, 1:2])
    table = shape()[...]
    modes = product(wide, table) * scale
    back = product(modes, table, 1)
    return assemble_wide([blocks(col, EY + 2) for col in columns(back)])


def stiffness_of(field, pair, stiff, rows):
    return product(field, stiff()[...]) * pair[:, 0:1] + field * (rows[1:2] * pair[:, 1:2])


def first_kernel(
    part_ref, left_ref, right_ref, below_ref, above_ref, pair_ref, gathered_ref, leaf_in_ref,
    rows, shape, spread, leaf, column, top, stiff, loads,
    source_out, search_out, wide_pair_out, out_ref, left_out_ref, right_out_ref, coeff_ref,
    leaf_out_ref,
):
    rows = rows()[...]
    weight = weight_of(rows[2:3])
    field = wide_field(part_ref, left_ref, right_ref, below_ref, above_ref)
    source = inner_rows(field)
    source_out.ref[...] = source
    source_out.send()
    own = pair_ref[...]
    at = slice(NODES, NODES + 128)
    wide_pair = jnp.concatenate([blocks(left_ref[:, at]), blocks(own), blocks(right_ref[:, at])], 0)
    wide_pair = jnp.concatenate(
        [blocks(below_ref[:, at], 1), wide_pair, blocks(above_ref[:, at], 1)], 1
    ).reshape(-1, 128)
    wide_pair_out.ref[...] = wide_pair
    wide_pair_out.send()
    coeffs = jnp.sum(gathered_ref[...], axis=0)
    smoothed = smoothed_of(field, wide_pair, shape, rows)
    search = jnp.concatenate(smoothed, 1) * weight + coarse_of(
        coeffs, leaf_in_ref[...], spread()[...], leaf(), column(), top()
    )
    search_out.ref[...] = search
    search_out.send()
    image = stiffness_of(search, own, stiff, rows)
    write_planes(assemble_inside(columns(image)), out_ref, left_out_ref, right_out_ref)
    numbers = numbers_row(
        [total_of(source * source * weight), total_of(image * source), total_of(image * image)]
    )
    loads_of(image, loads()[...], leaf(), column(), top(), coeff_ref, leaf_out_ref, numbers)


def second_kernel(
    part_ref, left_ref, right_ref, below_ref, above_ref, pair_ref, gathered_ref, leaf_in_ref,
    rows, wide_pair, shape, spread, leaf, column, top, search, source, stiff,
    image_out, second_out, out_ref, face_left_ref, face_right_ref, face_y_ref, sums_ref, total_ref,
):
    rows = rows()[...]
    weight = weight_of(rows[2:3])
    coeffs = jnp.sum(gathered_ref[...], axis=0)
    total_ref[...] = coeffs
    norm, along, size = coeffs[2:3, 0:1], coeffs[2:3, 1:2], coeffs[2:3, 2:3]
    overlap = along / norm
    scale = 1.0 / jnp.sqrt(size)
    field = wide_field(part_ref, left_ref, right_ref, below_ref, above_ref)
    first = inner_rows(field)
    image_out.ref[...] = first
    image_out.send()
    smoothed = smoothed_of(field, wide_pair()[...], shape, rows)
    whole = jnp.concatenate(smoothed, 1) * weight + coarse_of(
        coeffs, leaf_in_ref[...], spread()[...], leaf(), column(), top()
    )
    second = (whole - overlap * search()[...]) * scale
    second_out.ref[...] = second
    second_out.send()
    source = source()[...]
    image = stiffness_of(second, pair_ref[...], stiff, rows)
    write_faces(assemble_inside(columns(image)), out_ref, face_left_ref, face_right_ref, face_y_ref)
    basis = (first - overlap * source) * scale
    sums_ref[...] = numbers_row(
        [total_of(basis * basis * weight), total_of(image * source), total_of(image * basis)]
    )


def chooser_back(order_ref):
    slot = lax.broadcasted_iota(jnp.int32, (ROWS, ROWS), 0)
    return (order_ref[...] == slot).astype(F32).T.astype(BF16)


def last_kernel(
    part_ref, before_x_ref, after_x_ref, before_y_ref, after_y_ref, sums_in_ref, rows,
    image_ref, sums_ref,
):
    image = finish(part_ref, before_x_ref, after_x_ref, before_y_ref, after_y_ref)
    image_ref[...] = image
    square = total_of(image * image * weight_of(rows()[2:3]))
    sums = jnp.where(lanes() == 3, square, sums_in_ref[...])
    sums_ref[...] = jnp.broadcast_to(sums, sums_ref.shape)


def end_kernel(
    sums_ref, coeff_ref, image_two_ref, order, search_one, search_two, source, image_one,
    pressure_out, residual_out,
):
    sums = jnp.sum(sums_ref[...], axis=0, keepdims=True)
    squared, dot_source, dot_basis, dot_self = (sums[:, at : at + 1] for at in range(4))
    coeffs = coeff_ref[...]
    norm, along, size = coeffs[2:3, 0:1], coeffs[2:3, 1:2], coeffs[2:3, 2:3]
    beta = jnp.sqrt(norm)
    basis_norm = jnp.sqrt(squared)
    first_diag = along / norm
    first_sub = basis_norm * jnp.sqrt(size) / beta
    second_top = dot_source / (beta * basis_norm)
    second_diag = dot_basis / squared
    second_sub_squared = jnp.maximum(
        dot_self / squared - second_top * second_top - second_diag * second_diag, 0.0
    )
    first_norm = jnp.sqrt(first_diag * first_diag + first_sub * first_sub)
    cosine = first_diag / first_norm
    sine_part = first_sub / first_norm
    rotated = cosine * second_top + sine_part * second_diag
    lowered = cosine * second_diag - sine_part * second_top
    second_norm = jnp.sqrt(lowered * lowered + second_sub_squared)
    factor_two = -(lowered / second_norm) * sine_part * beta / second_norm
    factor_one = (cosine * beta - rotated * factor_two) / first_norm
    step_one = factor_one / beta
    step_two = factor_two / basis_norm
    chooser = chooser_back(order())
    pressure_out.ref[...] = permuted(
        chooser, step_one * search_one()[...] + step_two * search_two()[...]
    )
    pressure_out.send()
    residual_out.ref[...] = permuted(
        chooser, source()[...] - step_one * image_one()[...] - step_two * image_two_ref[...]
    )
    residual_out.send()


class Far:
    def __init__(self, value):
        self.value = value


class Fetch:
    def __init__(self, source, target, sem):
        self.copy, self.target, self.waiting = pltpu.make_async_copy(source, target, sem), target, True
        self.copy.start()

    def __call__(self):
        if self.waiting:
            self.copy.wait()
            self.waiting = False
        return self.target


class Store:
    def __init__(self, ref, target, sem):
        self.ref, self.copy = ref, pltpu.make_async_copy(ref, target, sem)

    def send(self):
        self.copy.start()


def shaped(*shape):
    return jax.ShapeDtypeStruct(shape, F32)


def run(kernel, outs, *args):
    vmem, far = pl.BlockSpec(memory_space=pltpu.VMEM), pl.BlockSpec(memory_space=pl.ANY)
    far_in = [isinstance(arg, Far) for arg in args]
    far_out = [isinstance(out, Far) for out in outs]
    args = [arg.value if isinstance(arg, Far) else arg for arg in args]
    outs = [out.value if isinstance(out, Far) else out for out in outs]
    moved = [arg for arg, out_of in zip(args, far_in) if out_of]
    moved += [out for out, out_of in zip(outs, far_out) if out_of]
    count = len(moved)

    def body(*refs):
        ins, rest = refs[: len(args)], refs[len(args) :]
        results, scratch = rest[: len(outs)], rest[len(outs) :]
        at, given, stores = 0, [], []
        for ref, is_far in zip(ins, far_in):
            if is_far:
                ref = Fetch(ref, scratch[at], scratch[count].at[at])
                at += 1
            given.append(ref)
        for ref, is_far in zip(results, far_out):
            if is_far:
                ref = Store(scratch[at], ref, scratch[count].at[at])
                stores.append(ref)
                at += 1
            given.append(ref)
        kernel(*given)
        for store in stores:
            store.copy.wait()

    scratch = [pltpu.VMEM(item.shape, item.dtype) for item in moved]
    if count:
        scratch.append(pltpu.SemaphoreType.DMA((count,)))
    return pl.pallas_call(
        body,
        out_shape=tuple(outs),
        in_specs=[far if is_far else vmem for is_far in far_in],
        out_specs=tuple(far if is_far else vmem for is_far in far_out),
        scratch_shapes=scratch,
        compiler_params=pltpu.CompilerParams(vmem_limit_bytes=LIMIT),
    )(*args)


LIMIT = 28 * 2**20
FIELD = shaped(ROWS, NODES)
FACES = shaped(2, 64, 128)
FACE = shaped(64, 128)
PAIRS = shaped(ROWS, 128)


def neighbours(low, high, axis):
    peers = lax.axis_size(axis)
    up = [(i, (i + 1) % peers) for i in range(peers)]
    down = [(j, i) for i, j in up]
    return lax.ppermute(high, axis, up), lax.ppermute(low, axis, down)


def surrounded(part, left, right, coeffs, pair=None):
    wide, across = left.shape[1], (EX + 2) * EZ
    before, after = neighbours(left, right, "gx")
    gathered = lax.all_to_all(coeffs, "gx", 0, 0)
    more = () if pair is None else (pair,)
    low, high, spread = run(
        middle_kernel,
        (shaped(across, wide), shaped(across, wide), shaped(lax.axis_size("gy"), 8, 128)),
        part, before, after, coeffs, gathered, *more,
    )
    below, above = neighbours(low, high, "gy")
    return part, before, after, below, above, lax.all_to_all(spread, "gy", 0, 0)


def per_device(
    forcing, element_order, diffusivity, reaction, leaf_factor, column_factor, top_factor
):
    stiff, shape, loads, spread, rows = (Far(table) for table in build_tables())
    factors = tuple(Far(factor[0, 0]) for factor in (leaf_factor, column_factor, top_factor))
    order = Far(element_order[0])
    coarse = (shaped(lax.axis_size("gx"), 8, 128), shaped(1, 256))
    part, left, right, coeffs, leaves, pair = run(
        start_kernel,
        (FIELD, shaped(64, NODES + 128), shaped(64, NODES + 128), *coarse, PAIRS),
        order, Far(forcing[0, 0]), Far(diffusivity[0]), Far(reaction[0]), loads, *factors,
    )
    *around, gathered = surrounded(part, left, right, coeffs, pair)
    source, search_one, wide_pair, part, left, right, coeffs, leaves = run(
        first_kernel,
        (
            Far(FIELD), Far(FIELD), Far(shaped((EX + 2) * (EY + 2) * EZ, 128)),
            FIELD, shaped(64, NODES), shaped(64, NODES), *coarse,
        ),
        *around, pair, gathered, leaves, rows, shape, spread, *factors, stiff, loads,
    )
    *around, gathered = surrounded(part, left, right, coeffs)
    image_one, search_two, part, face_left, face_right, face_y, sums, coeffs = run(
        second_kernel,
        (Far(FIELD), Far(FIELD), FIELD, FACE, FACE, FACES, shaped(1, 128), shaped(8, 128)),
        *around, pair, gathered, leaves, rows, Far(wide_pair), shape, spread, *factors,
        Far(search_one), Far(source), stiff,
    )
    before_x, after_x = neighbours(face_left, face_right, "gx")
    low, high = run(edge_kernel, (FACE, FACE), face_y, before_x, after_x)
    before_y, after_y = neighbours(low, high, "gy")
    peers = lax.axis_size(("gx", "gy"))
    image_two, sums = run(
        last_kernel, (FIELD, shaped(peers, 128)),
        part, before_x, after_x, before_y, after_y, sums, rows,
    )
    sums = lax.all_to_all(sums, ("gx", "gy"), 0, 0, tiled=True)
    pressure, residual = run(
        end_kernel, (Far(FIELD), Far(FIELD)),
        sums, coeffs, image_two, order, Far(search_one), Far(search_two), Far(source), Far(image_one),
    )
    return (pressure[None, None], residual[None, None])


def solution(mesh):
    field = P("gx", "gy", None, None)
    row = P("gx", "gy", None)
    return jax.shard_map(
        per_device,
        mesh=mesh,
        in_specs=(field, row, row, row, field, field, field),
        out_specs=(field, field),
        check_vma=False,
    )
```

```python
import jax
import jax.numpy as jnp
import numpy as np
from jax import lax
from jax.experimental import pallas as pl
from jax.experimental.pallas import tpu as pltpu
from jax.sharding import Mesh, PartitionSpec as P

NP = 8
EX = 4
EY = 4
EZ = 16
ROWS = EX * EY * EZ
NODES = NP * NP * NP
LEVELS = EZ + 1
F32 = jnp.float32
BF16 = jnp.bfloat16


def legendre_columns(points, degree):
    columns_table = np.zeros((points.shape[0], degree + 1))
    columns_table[:, 0] = 1.0
    columns_table[:, 1] = points
    for level_at in range(2, degree + 1):
        columns_table[:, level_at] = (
            (2 * level_at - 1) * points * columns_table[:, level_at - 1]
            - (level_at - 1) * columns_table[:, level_at - 2]
        ) / level_at
    return columns_table


def jacobi_eigen(symmetric, npoints):
    matrix_work = symmetric.copy()
    vectors = np.eye(npoints)
    for sweep_at in range(15):
        for first_at in range(npoints):
            for second_at in range(first_at + 1, npoints):
                off_value = matrix_work[first_at, second_at]
                gap_value = matrix_work[second_at, second_at] - matrix_work[first_at, first_at]
                root_value = np.sqrt(gap_value * gap_value + 4.0 * off_value * off_value)
                sign_value = np.where(gap_value >= 0.0, 1.0, -1.0)
                denominator = np.abs(gap_value) + root_value
                safe_denominator = np.where(denominator > 0.0, denominator, 1.0)
                tangent = sign_value * 2.0 * off_value / safe_denominator
                cosine_value = 1.0 / np.sqrt(1.0 + tangent * tangent)
                sine_value = tangent * cosine_value
                rotation = np.eye(npoints)
                rotation[first_at, first_at] = cosine_value
                rotation[second_at, second_at] = cosine_value
                rotation[first_at, second_at] = sine_value
                rotation[second_at, first_at] = -sine_value
                matrix_work = rotation.T @ matrix_work @ rotation
                vectors = vectors @ rotation
    eigvals = np.array([matrix_work[place_at, place_at] for place_at in range(npoints)])
    return (eigvals, vectors)


def gll_tables(npoints):
    degree = npoints - 1
    estimate = -np.cos(np.pi * np.arange(npoints) / degree)
    for newton_at in range(100):
        columns_table = legendre_columns(estimate, degree)
        estimate = estimate - (
            estimate * columns_table[:, degree] - columns_table[:, degree - 1]
        ) / (npoints * columns_table[:, degree])
    values = legendre_columns(estimate, degree)[:, degree]
    weights = 2.0 / (degree * (degree + 1) * values**2)
    derivative = np.zeros((npoints, npoints))
    for row_at in range(npoints):
        for column_at in range(npoints):
            if row_at != column_at:
                derivative[row_at, column_at] = (
                    values[row_at] / values[column_at] / (estimate[row_at] - estimate[column_at])
                )
    derivative[0, 0] = -degree * (degree + 1) / 4.0
    derivative[degree, degree] = degree * (degree + 1) / 4.0
    stiffness = derivative.T @ (weights[:, None] * derivative)
    inv_root = 1.0 / np.sqrt(weights)
    symmetric = inv_root[:, None] * stiffness * inv_root[None, :]
    eigvals, eigvecs = jacobi_eigen(0.5 * (symmetric + symmetric.T), npoints)
    modes = inv_root[:, None] * eigvecs
    return (estimate, weights, stiffness, eigvals, modes)


def split_pair(table):
    high = table.astype(np.float32).astype(jnp.bfloat16)
    low = (table.astype(np.float32) - high.astype(np.float32)).astype(jnp.bfloat16)
    return np.stack([high, low])


def build_tables():
    points, weights, stiffness, eigvals, modes = gll_tables(8)
    massmat = weights[:, None] * np.eye(8)
    filler = np.ones(8)
    stiff_full = (
        np.kron(np.kron(stiffness, massmat), massmat)
        + np.kron(np.kron(massmat, stiffness), massmat)
        + np.kron(np.kron(massmat, massmat), stiffness)
    )
    mass_full = np.kron(np.kron(weights, weights), weights)
    eigen_full = (
        np.kron(np.kron(eigvals, filler), filler)
        + np.kron(np.kron(filler, eigvals), filler)
        + np.kron(np.kron(filler, filler), eigvals)
    )
    shape_full = np.kron(np.kron(modes, modes), modes)
    linear = np.stack([(1.0 - points) / 2.0, (1.0 + points) / 2.0], 1)
    trilinear = np.kron(np.kron(linear, linear), linear)
    ends = np.where((np.arange(8) == 0) | (np.arange(8) == 7), 0.5, 1.0)
    share = np.kron(np.kron(ends, ends), ends)
    rows = np.zeros((8, NODES), np.float32)
    rows[0], rows[1], rows[2] = eigen_full, mass_full, share
    loads = np.zeros((NODES, 128))
    loads[:, :8] = trilinear
    return (
        jnp.asarray(split_pair(stiff_full)),
        jnp.asarray(split_pair(shape_full)),
        jnp.asarray(split_pair(loads)),
        jnp.asarray(split_pair(loads.T)),
        jnp.asarray(rows),
    )


def lanes(width=128):
    return lax.broadcasted_iota(jnp.int32, (1, width), 1)


def halves(x):
    high = x.astype(BF16)
    return high, (x - high.astype(F32)).astype(BF16)


def product(x, table, contract=0):
    high, low = halves(x)
    dims = (((1,), (contract,)), ((), ()))

    def dot(p, q):
        return lax.dot_general(p, q, dims, preferred_element_type=F32)

    return dot(high, table[0]) + (dot(low, table[0]) + dot(high, table[1]))


def permuted(chooser, x):
    high, rest = x.astype(BF16), x
    rest = rest - high.astype(F32)
    mid = rest.astype(BF16)
    low = (rest - mid.astype(F32)).astype(BF16)

    def dot(q):
        return jnp.dot(chooser, q, preferred_element_type=F32)

    return dot(high) + (dot(mid) + dot(low))


def columns(x):
    return [x[:, 128 * c : 128 * c + 128] for c in range(4)]


def weight_of(share):
    lane = lanes(NODES) % NP
    level = lax.broadcasted_iota(jnp.int32, (ROWS, 1), 0) % EZ
    end = ((lane == 0) & (level == 0)) | ((lane == NP - 1) & (level == EZ - 1))
    return jnp.where(end, 2.0 * share, share)


def first_plane(x):
    return jnp.where(lanes() < 64, roll_lanes(x, 64), 0.0)


def last_plane(x):
    return jnp.where(lanes() >= 64, roll_lanes(x, 64), 0.0)


def first_row(x):
    return jnp.where(lanes() // NP % NP == 0, roll_lanes(x, 72), 0.0)


def last_row(x):
    return jnp.where(lanes() // NP % NP == NP - 1, roll_lanes(x, 56), 0.0)


def roll_lanes(x, shift):
    return pltpu.roll(x.reshape(-1, 128), shift, 1).reshape(x.shape)


def sum_levels(col):
    rows = col.shape[0]
    row_z = lanes() % NP
    level = lax.broadcasted_iota(jnp.int32, (rows, 1), 0) % EZ
    up = pltpu.roll(pltpu.roll(col, 121, 1), 1, 0)
    down = pltpu.roll(pltpu.roll(col, 7, 1), rows - 1, 0)
    return (
        col
        + jnp.where((row_z == 0) & (level > 0), up, 0.0)
        + jnp.where((row_z == NP - 1) & (level < EZ - 1), down, 0.0)
    )


def blocks(col, length=EY):
    return col.reshape(-1, length, EZ, 128)


def assemble_inside(cols):
    cols = [blocks(col) for col in cols]
    edge = jnp.zeros((1, EY, EZ, 128), F32)
    cols = [
        cols[0] + jnp.concatenate([edge, first_plane(cols[3][: EX - 1])], 0),
        cols[1],
        cols[2],
        cols[3] + jnp.concatenate([last_plane(cols[0][1:]), edge], 0),
    ]
    edge = jnp.zeros((EX, 1, EZ, 128), F32)
    result = []
    for col in cols:
        col = (
            col
            + jnp.concatenate([edge, first_row(col[:, : EY - 1])], 1)
            + jnp.concatenate([last_row(col[:, 1:]), edge], 1)
        )
        result.append(sum_levels(col.reshape(ROWS, 128)))
    return result


def joined_x(own, left, right):
    own, left, right = list(own), list(left), list(right)
    low, high = own[0], own[3]
    tail = jnp.zeros_like(low[1:])
    own[0] = low + jnp.concatenate([first_plane(left[3]), tail], 0)
    own[3] = high + jnp.concatenate([tail, last_plane(right[0])], 0)
    left[3] = left[3] + last_plane(low[:1])
    right[0] = right[0] + first_plane(high[EX - 1 :])
    return [jnp.concatenate(parts, 0) for parts in zip(left, own, right)]


def joined_y(middle, below, above):
    first, last = middle[:, :1], middle[:, EY - 1 :]
    hole = jnp.zeros_like(middle[:, 1 : EY - 1])
    middle = middle + jnp.concatenate([first_row(below), hole, last_row(above)], 1)
    return jnp.concatenate([below + last_row(first), middle, above + first_row(last)], 1)


def assemble_wide(cols):
    cols = [
        cols[0][1:-1] + first_plane(cols[3][:-2]),
        cols[1][1:-1],
        cols[2][1:-1],
        cols[3][1:-1] + last_plane(cols[0][2:]),
    ]
    return [
        sum_levels((col[:, 1:-1] + first_row(col[:, :-2]) + last_row(col[:, 2:])).reshape(ROWS, 128))
        for col in cols
    ]


def write_faces(cols, part_ref, face_left_ref, face_right_ref, face_y_ref):
    row_y = lanes() // NP % NP
    for c in range(4):
        part_ref[:, 128 * c : 128 * c + 128] = cols[c]
    face_left_ref[...] = cols[0][:64]
    face_right_ref[...] = cols[3][192:]
    low = jnp.zeros((64, 128), F32)
    high = jnp.zeros((64, 128), F32)
    for c in range(4):
        split = cols[c].reshape(EX, EY, EZ, 128)
        first = jnp.where(row_y == 0, split[:, 0].reshape(64, 128), 0.0)
        last = jnp.where(row_y == NP - 1, split[:, EY - 1].reshape(64, 128), 0.0)
        low = low + (pltpu.roll(first, 8 * c, 1) if c else first)
        high = high + pltpu.roll(last, (72 + 8 * c) % 128, 1)
    face_y_ref[0] = low
    face_y_ref[1] = high


def write_planes(cols, part_ref, left_ref, right_ref):
    for c in range(4):
        at = slice(128 * c, 128 * c + 128)
        part_ref[:, at] = cols[c]
        left_ref[:, at] = cols[c][:64]
        right_ref[:, at] = cols[c][192:]


def edge_kernel(face_y_ref, before_ref, after_ref, out_low_ref, out_high_ref):
    lane = lanes()
    first = lane < 8
    last = (lane >= 88) & (lane < 96)
    out_low_ref[...] = face_y_ref[0]
    out_high_ref[...] = face_y_ref[1]
    out_low_ref[0:16] += jnp.where(first, pltpu.roll(before_ref[0:16], 64, 1), 0.0)
    out_high_ref[0:16] += jnp.where(first, pltpu.roll(before_ref[48:64], 8, 1), 0.0)
    out_low_ref[48:64] += jnp.where(last, pltpu.roll(after_ref[0:16], 88, 1), 0.0)
    out_high_ref[48:64] += jnp.where(last, pltpu.roll(after_ref[48:64], 32, 1), 0.0)


def finish(part_ref, before_x_ref, after_x_ref, before_y_ref, after_y_ref):
    lane = lanes()
    row_y = lane // NP % NP
    rest = jnp.zeros((192, 128), F32)
    before = jnp.where(lane < 64, pltpu.roll(before_x_ref[...], 64, 1), 0.0)
    after = jnp.where(lane >= 64, pltpu.roll(after_x_ref[...], 64, 1), 0.0)
    before_y, after_y = before_y_ref[...], after_y_ref[...]
    hole = jnp.zeros((EX, EY - 2, EZ, 128), F32)
    result = []
    for c in range(4):
        col = part_ref[:, 128 * c : 128 * c + 128]
        if c == 0:
            col = col + jnp.concatenate([before, rest], 0)
        if c == 3:
            col = col + jnp.concatenate([rest, after], 0)
        low = pltpu.roll(before_y, (128 - 8 * c) % 128, 1) if c else before_y
        low = jnp.where(row_y == 0, low, 0.0).reshape(EX, 1, EZ, 128)
        high = jnp.where(row_y == NP - 1, pltpu.roll(after_y, 56 - 8 * c, 1), 0.0)
        high = high.reshape(EX, 1, EZ, 128)
        result.append(col + jnp.concatenate([low, hole, high], 1).reshape(ROWS, 128))
    return jnp.concatenate(result, 1)


def factor_rows(ref, at, count):
    if at < count - 1:
        return ref[pl.ds(LEVELS * at, 24), :]
    return pltpu.roll(ref[pl.ds(LEVELS * count - 24, 24), :], LEVELS, 0)


def loads_of(unassembled, loads, leaf_ref, column_ref, top_ref, coeff_ref, leaf_out_ref, numbers):
    corner = product(unassembled, loads)
    lane = lanes()
    pad = jnp.zeros((8, 128), F32)
    lifted = []
    for at in range(EX * EY):
        piece = corner[16 * at : 16 * at + 16]
        same = jnp.concatenate([jnp.where(lane % 2 == 0, piece, 0.0), pad], 0)
        above = jnp.concatenate([jnp.where(lane % 2 == 1, piece, 0.0), pad], 0)
        lifted.append(same + pltpu.roll(above, 1, 0))
    top_sum = jnp.zeros((24, 256), F32)
    column_sum = jnp.zeros((24, 256), F32)
    leaf_sum = jnp.zeros((24, 256), F32)
    for vx in range(EX + 1):
        for vy in range(EY + 1):
            total = jnp.zeros((24, 128), F32)
            for sx in (0, 1):
                for sy in (0, 1):
                    if 0 <= vx - sx < EX and 0 <= vy - sy < EY:
                        piece = lifted[(vx - sx) * EY + vy - sy]
                        total = total + jnp.where(lane // 2 == sx * 2 + sy, piece, 0.0)
            vertex = jnp.sum(total, axis=1, keepdims=True)
            at = vx * (EY + 1) + vy
            top_sum = top_sum + factor_rows(top_ref, at, 25) * vertex
            if 0 < vx < EX:
                column_sum = column_sum + factor_rows(column_ref, at, 25) * vertex
                if 0 < vy < EY:
                    leaf_sum = leaf_sum + factor_rows(leaf_ref, (vx - 1) * 3 + vy - 1, 9) * vertex
    row = lax.broadcasted_iota(jnp.int32, (4, 1), 0)
    coeffs = jnp.where(row == 1, numbers, 0.0)
    coeffs = jnp.where(row == 0, jnp.sum(top_sum, axis=0, keepdims=True), coeffs)
    coeffs = jnp.where(row == 2, jnp.sum(column_sum, axis=0, keepdims=True), coeffs)
    coeff_ref[...] = jnp.broadcast_to(coeffs[None], coeff_ref.shape)
    leaf_out_ref[...] = jnp.sum(leaf_sum, axis=0, keepdims=True)


def coarse_of(coeffs, leaf_coeffs, spread, leaf_ref, column_ref, top_ref):
    lane = lanes()
    top, column = coeffs[0:1], coeffs[2:3]
    around = []
    for vx in range(EX + 1):
        for vy in range(EY + 1):
            at = vx * (EY + 1) + vy
            total = factor_rows(top_ref, at, 25) * top
            if 0 < vx < EX:
                total = total + factor_rows(column_ref, at, 25) * column
                if 0 < vy < EY:
                    total = total + factor_rows(leaf_ref, (vx - 1) * 3 + vy - 1, 9) * leaf_coeffs
            vertex = jnp.sum(total, axis=1, keepdims=True)
            same = jnp.broadcast_to(vertex, (24, 128))
            around.append(jnp.where(lane % 2 == 0, same, pltpu.roll(same, 23, 0))[:16])
    corners = []
    for ex in range(EX):
        for ey in range(EY):
            value = jnp.zeros((16, 128), F32)
            for sx in (0, 1):
                for sy in (0, 1):
                    piece = around[(ex + sx) * (EY + 1) + ey + sy]
                    value = jnp.where(lane // 2 == sx * 2 + sy, piece, value)
            corners.append(value)
    return product(jnp.concatenate(corners, 0), spread)


def total_of(x):
    return jnp.sum(jnp.sum(x, axis=0, keepdims=True), axis=1, keepdims=True)


def numbers_row(values, width=256):
    lane = lanes(width)
    row = jnp.zeros((1, width), F32)
    for at, value in enumerate(values):
        row = jnp.where(lane == at, value, row)
    return row


def start_kernel(
    order, forcing, diffusivity, reaction, leaf, column, top, loads_ref,
    part_ref, left_ref, right_ref, coeff_ref, leaf_out_ref, pair_ref, order_ref, *factor_refs,
):
    slot = lax.broadcasted_iota(jnp.int32, (ROWS, ROWS), 0)
    order_ref[...] = order()[...]
    chooser = (order_ref[...] == slot).astype(F32)
    diffusion = jnp.sum(chooser * diffusivity()[...], axis=1, keepdims=True)
    reacting = jnp.sum(chooser * reaction()[...], axis=1, keepdims=True)
    pair = jnp.where(lanes() == 0, diffusion, reacting)
    pair_ref[...] = pair
    left_ref[:, NODES:] = pair[:64]
    right_ref[:, NODES:] = pair[192:]
    source = permuted(chooser.astype(BF16), forcing()[...])
    write_planes(assemble_inside(columns(source)), part_ref, left_ref, right_ref)
    factors = [leaf(), column(), top()]
    loads_of(source, loads_ref[...], *factors, coeff_ref, leaf_out_ref, numbers_row([]))
    for ref, factor in zip(factor_refs, factors):
        ref[...] = factor[...]


def rows_of_plane(ref, c, plane):
    return blocks(ref[:, 128 * c : 128 * c + 128])[:, plane : plane + 1]


def middle_kernel(part_ref, left_ref, right_ref, gathered_ref, *refs):
    with_pair = len(refs) == 4
    low_ref, high_ref, spread_ref = refs[-3:]
    row = lax.broadcasted_iota(jnp.int32, (4, 1), 0)
    halves_of, me = gathered_ref.shape[0] // lax.axis_size("gx"), lax.axis_index("gx")
    gathered = gathered_ref[...]
    source = lax.broadcasted_iota(jnp.int32, (gathered.shape[0], 1, 1), 0) // halves_of
    mine = jnp.sum(jnp.where(source == me, gathered, 0.0), axis=0)
    coeffs = jnp.where(row < 2, jnp.sum(gathered, axis=0), mine)
    spread_ref[...] = jnp.broadcast_to(coeffs[None], spread_ref.shape)
    for plane, out_ref in ((0, low_ref), (EY - 1, high_ref)):
        sides = [
            [rows_of_plane(ref, c, plane) for c in range(4)] for ref in (part_ref, left_ref, right_ref)
        ]
        for c, col in enumerate(joined_x(*sides)):
            out_ref[:, 128 * c : 128 * c + 128] = col.reshape(-1, 128)
        if with_pair:
            sides = [rows_of_plane(left_ref, 4, plane), rows_of_plane(refs[0], 0, plane)]
            sides.append(rows_of_plane(right_ref, 4, plane))
            out_ref[:, NODES:] = jnp.concatenate(sides, 0).reshape(-1, 128)


def wide_field(part_ref, left_ref, right_ref, below_ref, above_ref):
    sides = [
        [blocks(ref[:, 128 * c : 128 * c + 128]) for c in range(4)]
        for ref in (part_ref, left_ref, right_ref)
    ]
    result = []
    for c, middle in enumerate(joined_x(*sides)):
        at = slice(128 * c, 128 * c + 128)
        result.append(joined_y(middle, blocks(below_ref[:, at], 1), blocks(above_ref[:, at], 1)))
    return result


def inner_rows(cols):
    return jnp.concatenate([col[1:-1, 1:-1].reshape(ROWS, 128) for col in cols], 1)


def smoothed_of(cols, pair, shape, rows):
    wide = jnp.concatenate([col.reshape(-1, 128) for col in cols], 1)
    scale = 1.0 / (pair[:, 0:1] * rows[0:1] + pair[:, 1:2])
    table = shape[...]
    modes = product(wide, table) * scale
    back = product(modes, table, 1)
    return assemble_wide([blocks(col, EY + 2) for col in columns(back)])


def stiffness_of(field, pair, stiff, rows):
    return product(field, stiff[...]) * pair[:, 0:1] + field * (rows[1:2] * pair[:, 1:2])


def first_kernel(
    part_ref, left_ref, right_ref, below_ref, above_ref, pair_ref, gathered_ref, leaf_in_ref,
    rows_ref, shape, spread, leaf, column, top, stiff, loads,
    source_out, search_out, wide_pair_out, out_ref, left_out_ref, right_out_ref, coeff_ref,
    leaf_out_ref,
):
    rows = rows_ref[...]
    weight = weight_of(rows[2:3])
    field = wide_field(part_ref, left_ref, right_ref, below_ref, above_ref)
    source = inner_rows(field)
    source_out[...] = source
    own = pair_ref[...]
    at = slice(NODES, NODES + 128)
    wide_pair = jnp.concatenate([blocks(left_ref[:, at]), blocks(own), blocks(right_ref[:, at])], 0)
    wide_pair = jnp.concatenate(
        [blocks(below_ref[:, at], 1), wide_pair, blocks(above_ref[:, at], 1)], 1
    ).reshape(-1, 128)
    wide_pair_out[...] = wide_pair
    coeffs = jnp.sum(gathered_ref[...], axis=0)
    smoothed = smoothed_of(field, wide_pair, shape, rows)
    search = jnp.concatenate(smoothed, 1) * weight + coarse_of(
        coeffs, leaf_in_ref[...], spread[...], leaf, column, top
    )
    search_out[...] = search
    image = stiffness_of(search, own, stiff, rows)
    write_planes(assemble_inside(columns(image)), out_ref, left_out_ref, right_out_ref)
    numbers = numbers_row(
        [total_of(source * source * weight), total_of(image * source), total_of(image * image)]
    )
    loads_of(image, loads[...], leaf, column, top, coeff_ref, leaf_out_ref, numbers)


def second_kernel(
    part_ref, left_ref, right_ref, below_ref, above_ref, pair_ref, gathered_ref, leaf_in_ref,
    rows_ref, wide_pair, shape, spread, leaf, column, top, search, source, stiff,
    image_out, second_out, out_ref, face_left_ref, face_right_ref, face_y_ref, sums_ref, total_ref,
):
    rows = rows_ref[...]
    weight = weight_of(rows[2:3])
    coeffs = jnp.sum(gathered_ref[...], axis=0)
    total_ref[...] = coeffs
    norm, along, size = coeffs[1:2, 0:1], coeffs[1:2, 1:2], coeffs[1:2, 2:3]
    overlap = along / norm
    scale = 1.0 / jnp.sqrt(size)
    field = wide_field(part_ref, left_ref, right_ref, below_ref, above_ref)
    first = inner_rows(field)
    image_out[...] = first
    smoothed = smoothed_of(field, wide_pair[...], shape, rows)
    whole = jnp.concatenate(smoothed, 1) * weight + coarse_of(
        coeffs, leaf_in_ref[...], spread[...], leaf, column, top
    )
    second = (whole - overlap * search[...]) * scale
    second_out[...] = second
    source = source[...]
    image = stiffness_of(second, pair_ref[...], stiff, rows)
    write_faces(assemble_inside(columns(image)), out_ref, face_left_ref, face_right_ref, face_y_ref)
    basis = (first - overlap * source) * scale
    sums_ref[...] = numbers_row(
        [total_of(basis * basis * weight), total_of(image * source), total_of(image * basis)], 128
    )


def chooser_back(order_ref):
    slot = lax.broadcasted_iota(jnp.int32, (ROWS, ROWS), 0)
    return (order_ref[...] == slot).astype(F32).T.astype(BF16)


def last_kernel(
    part_ref, before_x_ref, after_x_ref, before_y_ref, after_y_ref, sums_in_ref, rows,
    image_ref, sums_ref,
):
    image = finish(part_ref, before_x_ref, after_x_ref, before_y_ref, after_y_ref)
    image_ref[...] = image
    square = total_of(image * image * weight_of(rows[2:3]))
    sums = jnp.where(lanes() == 3, square, sums_in_ref[...])
    sums_ref[...] = jnp.broadcast_to(sums, sums_ref.shape)


def end_kernel(
    sums_ref, coeff_ref, image_two_ref, order, search_one, search_two, source, image_one,
    pressure_out, residual_out,
):
    sums = jnp.sum(sums_ref[...], axis=0, keepdims=True)
    squared, dot_source, dot_basis, dot_self = (sums[:, at : at + 1] for at in range(4))
    coeffs = coeff_ref[...]
    norm, along, size = coeffs[1:2, 0:1], coeffs[1:2, 1:2], coeffs[1:2, 2:3]
    beta = jnp.sqrt(norm)
    basis_norm = jnp.sqrt(squared)
    first_diag = along / norm
    first_sub = basis_norm * jnp.sqrt(size) / beta
    second_top = dot_source / (beta * basis_norm)
    second_diag = dot_basis / squared
    second_sub_squared = jnp.maximum(
        dot_self / squared - second_top * second_top - second_diag * second_diag, 0.0
    )
    first_norm = jnp.sqrt(first_diag * first_diag + first_sub * first_sub)
    cosine = first_diag / first_norm
    sine_part = first_sub / first_norm
    rotated = cosine * second_top + sine_part * second_diag
    lowered = cosine * second_diag - sine_part * second_top
    second_norm = jnp.sqrt(lowered * lowered + second_sub_squared)
    factor_two = -(lowered / second_norm) * sine_part * beta / second_norm
    factor_one = (cosine * beta - rotated * factor_two) / first_norm
    step_one = factor_one / beta
    step_two = factor_two / basis_norm
    chooser = chooser_back(order)
    pressure_out.ref[...] = permuted(
        chooser, step_one * search_one[...] + step_two * search_two[...]
    )
    pressure_out.send()
    residual_out.ref[...] = permuted(
        chooser, source[...] - step_one * image_one[...] - step_two * image_two_ref[...]
    )
    residual_out.send()


class Far:
    def __init__(self, value):
        self.value = value


class Fetch:
    def __init__(self, source, target, sem):
        self.copy, self.target, self.waiting = pltpu.make_async_copy(source, target, sem), target, True
        self.copy.start()

    def __call__(self):
        if self.waiting:
            self.copy.wait()
            self.waiting = False
        return self.target


class Store:
    def __init__(self, ref, target, sem):
        self.ref, self.copy = ref, pltpu.make_async_copy(ref, target, sem)

    def send(self):
        self.copy.start()


def shaped(*shape):
    return jax.ShapeDtypeStruct(shape, F32)


def run(kernel, outs, *args):
    vmem, far = pl.BlockSpec(memory_space=pltpu.VMEM), pl.BlockSpec(memory_space=pltpu.HBM)
    far_in = [isinstance(arg, Far) for arg in args]
    far_out = [isinstance(out, Far) for out in outs]
    args = [arg.value if isinstance(arg, Far) else arg for arg in args]
    outs = [out.value if isinstance(out, Far) else out for out in outs]
    moved = [arg for arg, out_of in zip(args, far_in) if out_of]
    moved += [out for out, out_of in zip(outs, far_out) if out_of]
    count = len(moved)

    def body(*refs):
        ins, rest = refs[: len(args)], refs[len(args) :]
        results, scratch = rest[: len(outs)], rest[len(outs) :]
        at, given, stores = 0, [], []
        for ref, is_far in zip(ins, far_in):
            if is_far:
                ref = Fetch(ref, scratch[at], scratch[count].at[at])
                at += 1
            given.append(ref)
        for ref, is_far in zip(results, far_out):
            if is_far:
                ref = Store(scratch[at], ref, scratch[count].at[at])
                stores.append(ref)
                at += 1
            given.append(ref)
        kernel(*given)
        for store in stores:
            store.copy.wait()

    scratch = [pltpu.VMEM(item.shape, item.dtype) for item in moved]
    if count:
        scratch.append(pltpu.SemaphoreType.DMA((count,)))
    return pl.pallas_call(
        body,
        out_shape=tuple(outs),
        in_specs=[far if is_far else vmem for is_far in far_in],
        out_specs=tuple(far if is_far else vmem for is_far in far_out),
        scratch_shapes=scratch,
        compiler_params=pltpu.CompilerParams(vmem_limit_bytes=LIMIT),
    )(*args)


LIMIT = 28 * 2**20
GY = ("gh", "gl")
NEAR = ("gx", "gh")
FIELD = shaped(ROWS, NODES)
FACES = shaped(2, 64, 128)
FACE = shaped(64, 128)
PAIRS = shaped(ROWS, 128)


def neighbours(low, high, axis):
    peers = lax.axis_size(axis)
    up = [(i, (i + 1) % peers) for i in range(peers)]
    down = [(j, i) for i, j in up]
    return lax.ppermute(high, axis, up), lax.ppermute(low, axis, down)


def surrounded(part, left, right, coeffs, pair=None):
    wide, across = left.shape[1], (EX + 2) * EZ
    before, after = neighbours(left, right, "gx")
    gathered = lax.all_to_all(coeffs, NEAR, 0, 0)
    more = () if pair is None else (pair,)
    low, high, spread = run(
        middle_kernel,
        (shaped(across, wide), shaped(across, wide), shaped(lax.axis_size("gl"), 4, 256)),
        part, before, after, gathered, *more,
    )
    below, above = neighbours(low, high, GY)
    return part, before, after, below, above, lax.all_to_all(spread, "gl", 0, 0)


def per_device(
    forcing, element_order, diffusivity, reaction, leaf_factor, column_factor, top_factor
):
    stiff, shape, loads, spread, rows = build_tables()
    factors = [factor[0, 0] for factor in (leaf_factor, column_factor, top_factor)]
    coarse = (shaped(lax.axis_size(NEAR), 4, 256), shaped(1, 256))
    part, left, right, coeffs, leaves, pair, order, *factors = run(
        start_kernel,
        (
            FIELD, shaped(64, NODES + 128), shaped(64, NODES + 128), *coarse, PAIRS,
            jax.ShapeDtypeStruct((1, ROWS), jnp.int32), *(shaped(*item.shape) for item in factors),
        ),
        Far(element_order[0]), Far(forcing[0, 0]), Far(diffusivity[0]), Far(reaction[0]),
        *(Far(item) for item in factors), loads,
    )
    *around, gathered = surrounded(part, left, right, coeffs, pair)
    source, search_one, wide_pair, part, left, right, coeffs, leaves = run(
        first_kernel,
        (
            FIELD, FIELD, shaped((EX + 2) * (EY + 2) * EZ, 128), FIELD, shaped(64, NODES), shaped(64, NODES), *coarse,
        ),
        *around, pair, gathered, leaves, rows, shape, spread, *factors, stiff, loads,
    )
    *around, gathered = surrounded(part, left, right, coeffs)
    image_one, search_two, part, face_left, face_right, face_y, sums, coeffs = run(
        second_kernel,
        (FIELD, FIELD, FIELD, FACE, FACE, FACES, shaped(1, 128), shaped(4, 256)),
        *around, pair, gathered, leaves, rows, wide_pair, shape, spread, *factors,
        search_one, source, stiff,
    )
    before_x, after_x = neighbours(face_left, face_right, "gx")
    low, high = run(edge_kernel, (FACE, FACE), face_y, before_x, after_x)
    before_y, after_y = neighbours(low, high, GY)
    peers = lax.axis_size(("gx", *GY))
    image_two, sums = run(
        last_kernel, (FIELD, shaped(peers, 128)),
        part, before_x, after_x, before_y, after_y, sums, rows,
    )
    sums = lax.all_to_all(sums, ("gx", *GY), 0, 0, tiled=True)
    pressure, residual = run(
        end_kernel, (Far(FIELD), Far(FIELD)),
        sums, coeffs, image_two, order, search_one, search_two, source, image_one,
    )
    return (pressure[None, None], residual[None, None])


def solution(mesh):
    count_x, count_y = mesh.devices.shape
    mesh = Mesh(mesh.devices.reshape(count_x, 2, count_y // 2), ("gx", *GY))
    field = P("gx", GY, None, None)
    row = P("gx", GY, None)
    return jax.shard_map(
        per_device,
        mesh=mesh,
        in_specs=(field, row, row, row, field, field, field),
        out_specs=(field, field),
        check_vma=False,
    )
```

```python
import jax
import jax.numpy as jnp
import numpy as np
from jax import lax
from jax.experimental import pallas as pl
from jax.experimental.pallas import tpu as pltpu
from jax.sharding import Mesh, PartitionSpec as P

NP = 8
EX = 4
EY = 4
EZ = 16
ROWS = EX * EY * EZ
NODES = NP * NP * NP
LEVELS = EZ + 1
F32 = jnp.float32
BF16 = jnp.bfloat16


def legendre_columns(points, degree):
    columns_table = np.zeros((points.shape[0], degree + 1))
    columns_table[:, 0] = 1.0
    columns_table[:, 1] = points
    for level_at in range(2, degree + 1):
        columns_table[:, level_at] = (
            (2 * level_at - 1) * points * columns_table[:, level_at - 1]
            - (level_at - 1) * columns_table[:, level_at - 2]
        ) / level_at
    return columns_table


def jacobi_eigen(symmetric, npoints):
    matrix_work = symmetric.copy()
    vectors = np.eye(npoints)
    for sweep_at in range(15):
        for first_at in range(npoints):
            for second_at in range(first_at + 1, npoints):
                off_value = matrix_work[first_at, second_at]
                gap_value = matrix_work[second_at, second_at] - matrix_work[first_at, first_at]
                root_value = np.sqrt(gap_value * gap_value + 4.0 * off_value * off_value)
                sign_value = np.where(gap_value >= 0.0, 1.0, -1.0)
                denominator = np.abs(gap_value) + root_value
                safe_denominator = np.where(denominator > 0.0, denominator, 1.0)
                tangent = sign_value * 2.0 * off_value / safe_denominator
                cosine_value = 1.0 / np.sqrt(1.0 + tangent * tangent)
                sine_value = tangent * cosine_value
                rotation = np.eye(npoints)
                rotation[first_at, first_at] = cosine_value
                rotation[second_at, second_at] = cosine_value
                rotation[first_at, second_at] = sine_value
                rotation[second_at, first_at] = -sine_value
                matrix_work = rotation.T @ matrix_work @ rotation
                vectors = vectors @ rotation
    eigvals = np.array([matrix_work[place_at, place_at] for place_at in range(npoints)])
    return (eigvals, vectors)


def gll_tables(npoints):
    degree = npoints - 1
    estimate = -np.cos(np.pi * np.arange(npoints) / degree)
    for newton_at in range(100):
        columns_table = legendre_columns(estimate, degree)
        estimate = estimate - (
            estimate * columns_table[:, degree] - columns_table[:, degree - 1]
        ) / (npoints * columns_table[:, degree])
    values = legendre_columns(estimate, degree)[:, degree]
    weights = 2.0 / (degree * (degree + 1) * values**2)
    derivative = np.zeros((npoints, npoints))
    for row_at in range(npoints):
        for column_at in range(npoints):
            if row_at != column_at:
                derivative[row_at, column_at] = (
                    values[row_at] / values[column_at] / (estimate[row_at] - estimate[column_at])
                )
    derivative[0, 0] = -degree * (degree + 1) / 4.0
    derivative[degree, degree] = degree * (degree + 1) / 4.0
    stiffness = derivative.T @ (weights[:, None] * derivative)
    inv_root = 1.0 / np.sqrt(weights)
    symmetric = inv_root[:, None] * stiffness * inv_root[None, :]
    eigvals, eigvecs = jacobi_eigen(0.5 * (symmetric + symmetric.T), npoints)
    modes = inv_root[:, None] * eigvecs
    return (estimate, weights, stiffness, eigvals, modes)


def split_pair(table):
    high = table.astype(np.float32).astype(jnp.bfloat16)
    low = (table.astype(np.float32) - high.astype(np.float32)).astype(jnp.bfloat16)
    return np.stack([high, low])


def build_tables():
    points, weights, stiffness, eigvals, modes = gll_tables(8)
    massmat = weights[:, None] * np.eye(8)
    filler = np.ones(8)
    stiff_full = (
        np.kron(np.kron(stiffness, massmat), massmat)
        + np.kron(np.kron(massmat, stiffness), massmat)
        + np.kron(np.kron(massmat, massmat), stiffness)
    )
    mass_full = np.kron(np.kron(weights, weights), weights)
    eigen_full = (
        np.kron(np.kron(eigvals, filler), filler)
        + np.kron(np.kron(filler, eigvals), filler)
        + np.kron(np.kron(filler, filler), eigvals)
    )
    linear = np.stack([(1.0 - points) / 2.0, (1.0 + points) / 2.0], 1)
    trilinear = np.kron(np.kron(linear, linear), linear)
    even_first = np.argsort([np.sign(modes[0, m]) != np.sign(modes[7, m]) for m in range(8)], kind="stable")
    first = np.kron(np.kron(modes[:4, even_first], modes), modes)
    shape_full = np.stack([first[:, :256], first[:, 256:]])
    eigen_full = eigen_full.reshape(8, 64)[even_first].reshape(-1)
    tiles = stiff_full.reshape(8, 64, 8, 64)
    near, mirrored = tiles[:4, :, :4], tiles[:4, :, :3:-1]
    stiff_full = np.stack([near + mirrored, near - mirrored]).reshape(2, 256, 256) / 2.0
    ends = np.where((np.arange(8) == 0) | (np.arange(8) == 7), 0.5, 1.0)
    share = np.kron(np.kron(ends, ends), ends)
    rows = np.zeros((8, NODES), np.float32)
    rows[0], rows[1], rows[2] = eigen_full, mass_full, share
    loads = np.zeros((NODES, 128))
    loads[:, :8] = trilinear
    return (
        jnp.asarray(split_pair(stiff_full)),
        jnp.asarray(split_pair(shape_full)),
        jnp.asarray(split_pair(loads)),
        jnp.asarray(split_pair(loads.T)),
        jnp.asarray(rows),
    )


def lanes(width=128):
    return lax.broadcasted_iota(jnp.int32, (1, width), 1)


def halves(x):
    high = x.astype(BF16)
    return high, (x - high.astype(F32)).astype(BF16)


def product(x, table, contract=0):
    high, low = halves(x)
    dims = (((1,), (contract,)), ((), ()))

    def dot(p, q):
        return lax.dot_general(p, q, dims, preferred_element_type=F32)

    return dot(high, table[0]) + (dot(low, table[0]) + dot(high, table[1]))


def fold(cols):
    far, near = pltpu.roll(cols[3], 64, 1), pltpu.roll(cols[2], 64, 1)
    even = jnp.concatenate([cols[0] + far, cols[1] + near], 1)
    return even, jnp.concatenate([cols[0] - far, cols[1] - near], 1)


def unfold(even, odd):
    total, rest = even + odd, even - odd
    last, third = pltpu.roll(rest[:, :128], 64, 1), pltpu.roll(rest[:, 128:], 64, 1)
    return [total[:, :128], total[:, 128:], third, last]


def part_of(table, at):
    return table[0, at], table[1, at]


def permuted(chooser, x):
    high, rest = x.astype(BF16), x
    rest = rest - high.astype(F32)
    mid = rest.astype(BF16)
    low = (rest - mid.astype(F32)).astype(BF16)

    def dot(q):
        return jnp.dot(chooser, q, preferred_element_type=F32)

    return dot(high) + (dot(mid) + dot(low))


def columns(x):
    return [x[:, 128 * c : 128 * c + 128] for c in range(4)]


def weight_of(share):
    lane = lanes(NODES) % NP
    level = lax.broadcasted_iota(jnp.int32, (ROWS, 1), 0) % EZ
    end = ((lane == 0) & (level == 0)) | ((lane == NP - 1) & (level == EZ - 1))
    return jnp.where(end, 2.0 * share, share)


def first_plane(x):
    return jnp.where(lanes() < 64, roll_lanes(x, 64), 0.0)


def last_plane(x):
    return jnp.where(lanes() >= 64, roll_lanes(x, 64), 0.0)


def first_row(x):
    return jnp.where(lanes() // NP % NP == 0, roll_lanes(x, 72), 0.0)


def last_row(x):
    return jnp.where(lanes() // NP % NP == NP - 1, roll_lanes(x, 56), 0.0)


def roll_lanes(x, shift):
    return pltpu.roll(x.reshape(-1, 128), shift, 1).reshape(x.shape)


def sum_levels(col):
    rows = col.shape[0]
    row_z = lanes() % NP
    level = lax.broadcasted_iota(jnp.int32, (rows, 1), 0) % EZ
    up = pltpu.roll(pltpu.roll(col, 121, 1), 1, 0)
    down = pltpu.roll(pltpu.roll(col, 7, 1), rows - 1, 0)
    return (
        col
        + jnp.where((row_z == 0) & (level > 0), up, 0.0)
        + jnp.where((row_z == NP - 1) & (level < EZ - 1), down, 0.0)
    )


def blocks(col, length=EY):
    return col.reshape(-1, length, EZ, 128)


def assemble_inside(cols):
    cols = [blocks(col) for col in cols]
    edge = jnp.zeros((1, EY, EZ, 128), F32)
    cols = [
        cols[0] + jnp.concatenate([edge, first_plane(cols[3][: EX - 1])], 0),
        cols[1],
        cols[2],
        cols[3] + jnp.concatenate([last_plane(cols[0][1:]), edge], 0),
    ]
    edge = jnp.zeros((EX, 1, EZ, 128), F32)
    result = []
    for col in cols:
        col = (
            col
            + jnp.concatenate([edge, first_row(col[:, : EY - 1])], 1)
            + jnp.concatenate([last_row(col[:, 1:]), edge], 1)
        )
        result.append(sum_levels(col.reshape(ROWS, 128)))
    return result


def joined_x(middle, left, right):
    middle, left, right = list(middle), list(left), list(right)
    low, high = middle[0], middle[3]
    hole = jnp.zeros_like(low[1:])
    middle[0] = low + jnp.concatenate([first_plane(left[3]), hole], 0)
    middle[3] = high + jnp.concatenate([hole, last_plane(right[0])], 0)
    left[3] = left[3] + last_plane(low[:1])
    right[0] = right[0] + first_plane(high[EX - 1 :])
    return [jnp.concatenate(parts, 0) for parts in zip(left, middle, right)]


def joined_y(middle, below, above):
    first, last = middle[:, :1], middle[:, EY - 1 :]
    hole = jnp.zeros_like(middle[:, 1 : EY - 1])
    middle = middle + jnp.concatenate([first_row(below), hole, last_row(above)], 1)
    return jnp.concatenate([below + last_row(first), middle, above + first_row(last)], 1)


def assemble_wide(cols):
    cols = [
        cols[0][1:-1] + first_plane(cols[3][:-2]),
        cols[1][1:-1],
        cols[2][1:-1],
        cols[3][1:-1] + last_plane(cols[0][2:]),
    ]
    return [
        sum_levels((col[:, 1:-1] + first_row(col[:, :-2]) + last_row(col[:, 2:])).reshape(ROWS, 128))
        for col in cols
    ]


def write_faces(cols, part_ref, face_left_ref, face_right_ref, face_low_ref, face_high_ref):
    row_y = lanes() // NP % NP
    for c in range(4):
        part_ref[:, 128 * c : 128 * c + 128] = cols[c]
    face_left_ref[...] = cols[0][:64]
    face_right_ref[...] = cols[3][192:]
    low = jnp.zeros((64, 128), F32)
    high = jnp.zeros((64, 128), F32)
    for c in range(4):
        split = cols[c].reshape(EX, EY, EZ, 128)
        first = jnp.where(row_y == 0, split[:, 0].reshape(64, 128), 0.0)
        last = jnp.where(row_y == NP - 1, split[:, EY - 1].reshape(64, 128), 0.0)
        low = low + (pltpu.roll(first, 8 * c, 1) if c else first)
        high = high + pltpu.roll(last, (72 + 8 * c) % 128, 1)
    face_low_ref[...] = low
    face_high_ref[...] = high


def write_planes(cols, part_ref, below_ref, above_ref):
    for c in range(4):
        at = slice(128 * c, 128 * c + 128)
        part_ref[:, at] = cols[c]
        below_ref[:, at] = blocks(cols[c])[:, 0].reshape(64, 128)
        above_ref[:, at] = blocks(cols[c])[:, EY - 1].reshape(64, 128)


def faces_added(part_ref, before_x_ref, after_x_ref, before_y_ref, after_y_ref):
    lane = lanes()
    row_y = lane // NP % NP
    rest = jnp.zeros((192, 128), F32)
    before = jnp.where(lane < 64, pltpu.roll(before_x_ref[...], 64, 1), 0.0)
    after = jnp.where(lane >= 64, pltpu.roll(after_x_ref[...], 64, 1), 0.0)
    none = jnp.zeros((ROWS, 128), F32)
    over_x = [jnp.concatenate([before, rest], 0), none, none, jnp.concatenate([rest, after], 0)]
    before_y, after_y = before_y_ref[...], after_y_ref[...]
    hole = jnp.zeros((EX, EY - 2, EZ, 128), F32)
    own, over_y = [], []
    for c in range(4):
        own.append(part_ref[:, 128 * c : 128 * c + 128])
        low = pltpu.roll(before_y, (128 - 8 * c) % 128, 1) if c else before_y
        low = jnp.where(row_y == 0, low, 0.0).reshape(EX, 1, EZ, 128)
        high = jnp.where(row_y == NP - 1, pltpu.roll(after_y, 56 - 8 * c, 1), 0.0)
        high = high.reshape(EX, 1, EZ, 128)
        over_y.append(jnp.concatenate([low, hole, high], 1).reshape(ROWS, 128))
    return own, over_x, over_y


EDGES = ((-1, -1, 0, 0, 0), (-1, 1, 48, 0, 56), (1, -1, 192, 3, 64), (1, 1, 240, 3, 120))


def over_lanes(x):
    for shift in (8, 16, 32, 64):
        x = x + pltpu.roll(x, shift, 1)
    return x


def diagonal_of(side_x, side_y):
    count_x, count_y = lax.axis_size("gx"), lax.axis_size(GY)
    at_y = lax.axis_index("gh") * lax.axis_size("gl") + lax.axis_index("gl")
    at_x = lax.rem(lax.axis_index("gx") + count_x + side_x, count_x)
    return at_x * count_y + lax.rem(at_y + count_y + side_y, count_y)


def edge_out(part_ref, row, block, first):
    lane = lanes()
    piece = part_ref[row : row + EZ, 128 * block : 128 * block + 128]
    piece = over_lanes(jnp.where((lane >= first) & (lane < first + NP), piece, 0.0))
    level = lax.broadcasted_iota(jnp.int32, (EZ, 1), 0)
    return jnp.sum(jnp.where(lane // NP == level, piece, 0.0), axis=0, keepdims=True)


def edge_in(line, first):
    lane = lanes()
    line = jnp.where(is_number(lane), pltpu.roll(line, 127, 1), line)
    level = lax.broadcasted_iota(jnp.int32, (EZ, 1), 0)
    spread = over_lanes(jnp.where(lane // NP == level, line, 0.0))
    return jnp.where((lane >= first) & (lane < first + NP), spread, 0.0)


def is_number(lane):
    return (lane % NP == NP - 1) & (lane < 4 * NP)


def factor_rows(ref, at, count):
    if at < count - 1:
        return ref[pl.ds(LEVELS * at, 24), :]
    return pltpu.roll(ref[pl.ds(LEVELS * count - 24, 24), :], LEVELS, 0)


def loads_of(unassembled, loads, leaf_ref, column_ref, top_ref, coeff_ref, leaf_out_ref, numbers):
    corner = product(unassembled, loads)
    lane = lanes()
    pad = jnp.zeros((8, 128), F32)
    lifted = []
    for at in range(EX * EY):
        piece = corner[16 * at : 16 * at + 16]
        same = jnp.concatenate([jnp.where(lane % 2 == 0, piece, 0.0), pad], 0)
        above = jnp.concatenate([jnp.where(lane % 2 == 1, piece, 0.0), pad], 0)
        lifted.append(same + pltpu.roll(above, 1, 0))
    top_sum = jnp.zeros((24, 256), F32)
    column_sum = jnp.zeros((24, 256), F32)
    leaf_sum = jnp.zeros((24, 256), F32)
    for vx in range(EX + 1):
        for vy in range(EY + 1):
            total = jnp.zeros((24, 128), F32)
            for sx in (0, 1):
                for sy in (0, 1):
                    if 0 <= vx - sx < EX and 0 <= vy - sy < EY:
                        piece = lifted[(vx - sx) * EY + vy - sy]
                        total = total + jnp.where(lane // 2 == sx * 2 + sy, piece, 0.0)
            vertex = jnp.sum(total, axis=1, keepdims=True)
            at = vx * (EY + 1) + vy
            top_sum = top_sum + factor_rows(top_ref, at, 25) * vertex
            if 0 < vx < EX:
                column_sum = column_sum + factor_rows(column_ref, at, 25) * vertex
                if 0 < vy < EY:
                    leaf_sum = leaf_sum + factor_rows(leaf_ref, (vx - 1) * 3 + vy - 1, 9) * vertex
    row = lax.broadcasted_iota(jnp.int32, (4, 1), 0)
    coeffs = jnp.where(row == 1, numbers, 0.0)
    coeffs = jnp.where(row == 0, jnp.sum(top_sum, axis=0, keepdims=True), coeffs)
    coeffs = jnp.where(row == 2, jnp.sum(column_sum, axis=0, keepdims=True), coeffs)
    coeff_ref[...] = jnp.broadcast_to(coeffs[None], coeff_ref.shape)
    leaf_out_ref[...] = jnp.sum(leaf_sum, axis=0, keepdims=True)


def coarse_of(coeffs, leaf_coeffs, spread, leaf_ref, column_ref, top_ref):
    lane = lanes()
    top, column = coeffs[0:1], coeffs[2:3]
    around = []
    for vx in range(EX + 1):
        for vy in range(EY + 1):
            at = vx * (EY + 1) + vy
            total = factor_rows(top_ref, at, 25) * top
            if 0 < vx < EX:
                total = total + factor_rows(column_ref, at, 25) * column
                if 0 < vy < EY:
                    total = total + factor_rows(leaf_ref, (vx - 1) * 3 + vy - 1, 9) * leaf_coeffs
            vertex = jnp.sum(total, axis=1, keepdims=True)
            same = jnp.broadcast_to(vertex, (24, 128))
            around.append(jnp.where(lane % 2 == 0, same, pltpu.roll(same, 23, 0))[:16])
    corners = []
    for ex in range(EX):
        for ey in range(EY):
            value = jnp.zeros((16, 128), F32)
            for sx in (0, 1):
                for sy in (0, 1):
                    piece = around[(ex + sx) * (EY + 1) + ey + sy]
                    value = jnp.where(lane // 2 == sx * 2 + sy, piece, value)
            corners.append(value)
    return product(jnp.concatenate(corners, 0), spread)


def total_of(x):
    return jnp.sum(jnp.sum(x, axis=0, keepdims=True), axis=1, keepdims=True)


def numbers_row(values, width=256, step=1):
    lane = lanes(width)
    row = jnp.zeros((1, width), F32)
    for at, value in enumerate(values):
        row = jnp.where(lane == step * (at + 1) - 1, value, row)
    return row


def start_kernel(
    order_ref, forcing_ref, diffusivity_ref, reaction_ref, leaf_ref, column_ref, top_ref, loads_ref,
    part_ref, below_ref, above_ref, coeff_ref, leaf_out_ref, pair_ref,
):
    slot = lax.broadcasted_iota(jnp.int32, (ROWS, ROWS), 0)
    chooser = (order_ref[...] == slot).astype(F32)
    diffusion = jnp.sum(chooser * diffusivity_ref[...], axis=1, keepdims=True)
    reacting = jnp.sum(chooser * reaction_ref[...], axis=1, keepdims=True)
    pair = jnp.where(lanes() == 0, diffusion, reacting)
    pair_ref[...] = pair
    below_ref[:, NODES:] = blocks(pair)[:, 0].reshape(64, 128)
    above_ref[:, NODES:] = blocks(pair)[:, EY - 1].reshape(64, 128)
    source = permuted(chooser.astype(BF16), forcing_ref[...])
    write_planes(assemble_inside(columns(source)), part_ref, below_ref, above_ref)
    loads_of(
        source, loads_ref[...], leaf_ref, column_ref, top_ref, coeff_ref, leaf_out_ref, numbers_row([])
    )


def own_plane(ref, c, plane):
    return blocks(ref[EY * EZ * plane : EY * EZ * (plane + 1), 128 * c : 128 * c + 128])


def got_plane(ref, c, plane):
    return blocks(ref[EZ * plane : EZ * (plane + 1), 128 * c : 128 * c + 128], 1)


def middle_kernel(part_ref, below_ref, above_ref, gathered_ref, *refs):
    with_pair = len(refs) == 4
    low_ref, high_ref, spread_ref = refs[-3:]
    row = lax.broadcasted_iota(jnp.int32, (4, 1), 0)
    halves_of, me = gathered_ref.shape[0] // lax.axis_size("gx"), lax.axis_index("gx")
    gathered = gathered_ref[...]
    source = lax.broadcasted_iota(jnp.int32, (gathered.shape[0], 1, 1), 0) // halves_of
    mine = jnp.sum(jnp.where(source == me, gathered, 0.0), axis=0)
    coeffs = jnp.where(row < 2, jnp.sum(gathered, axis=0), mine)
    spread_ref[...] = jnp.broadcast_to(coeffs[None], spread_ref.shape)
    for plane, out_ref in ((0, low_ref), (EX - 1, high_ref)):
        for c in range(4):
            sides = got_plane(below_ref, c, plane), got_plane(above_ref, c, plane)
            col = joined_y(own_plane(part_ref, c, plane), *sides)
            out_ref[:, 128 * c : 128 * c + 128] = col.reshape(-1, 128)
        if with_pair:
            sides = [got_plane(below_ref, 4, plane), own_plane(refs[0], 0, plane)]
            sides.append(got_plane(above_ref, 4, plane))
            out_ref[:, NODES:] = jnp.concatenate(sides, 1).reshape(-1, 128)


def wide_field(part_ref, below_ref, above_ref, left_ref, right_ref):
    middle, left, right = [], [], []
    for c in range(4):
        at = slice(128 * c, 128 * c + 128)
        middle.append(
            joined_y(blocks(part_ref[:, at]), blocks(below_ref[:, at], 1), blocks(above_ref[:, at], 1))
        )
        left.append(blocks(left_ref[:, at], EY + 2))
        right.append(blocks(right_ref[:, at], EY + 2))
    return joined_x(middle, left, right)


def inner_rows(cols):
    return jnp.concatenate([col[1:-1, 1:-1].reshape(ROWS, 128) for col in cols], 1)


def smoothed_of(cols, scale, shape):
    halves_of = fold([col.reshape(-1, 128) for col in cols])
    back = []
    for at, half in enumerate(halves_of):
        table = part_of(shape, at)
        modes = product(half, table) * scale[:, 256 * at : 256 * at + 256]
        back.append(product(modes, table, 1))
    return assemble_wide([blocks(col, EY + 2) for col in unfold(*back)])


def stiffness_of(field, pair, stiff, rows):
    halves_of = fold(columns(field))
    done = [product(half, part_of(stiff, at)) for at, half in enumerate(halves_of)]
    stiffened = jnp.concatenate(unfold(*done), 1)
    return stiffened * pair[:, 0:1] + field * (rows[1:2] * pair[:, 1:2])


def first_kernel(
    part_ref, below_ref, above_ref, left_ref, right_ref, pair_ref, gathered_ref, leaf_in_ref,
    rows_ref, shape, spread, leaf, column, top, stiff, loads,
    source_out, search_out, scale_out, out_ref, below_out_ref, above_out_ref, coeff_ref,
    leaf_out_ref,
):
    rows = rows_ref[...]
    weight = weight_of(rows[2:3])
    field = wide_field(part_ref, below_ref, above_ref, left_ref, right_ref)
    source = inner_rows(field)
    source_out[...] = source
    own = pair_ref[...]
    at = slice(NODES, NODES + 128)
    wide_pair = jnp.concatenate(
        [blocks(below_ref[:, at], 1), blocks(own), blocks(above_ref[:, at], 1)], 1
    ).reshape(-1, 128)
    wide_pair = jnp.concatenate([left_ref[:, at], wide_pair, right_ref[:, at]], 0)
    coeffs = jnp.sum(gathered_ref[...], axis=0)
    scale = 1.0 / (wide_pair[:, 0:1] * rows[0:1] + wide_pair[:, 1:2])
    scale_out[...] = scale
    smoothed = smoothed_of(field, scale, shape)
    search = jnp.concatenate(smoothed, 1) * weight + coarse_of(
        coeffs, leaf_in_ref[...], spread[...], leaf, column, top
    )
    search_out[...] = search
    image = stiffness_of(search, own, stiff, rows)
    write_planes(assemble_inside(columns(image)), out_ref, below_out_ref, above_out_ref)
    numbers = numbers_row(
        [total_of(source * source * weight), total_of(image * source), total_of(image * image)]
    )
    loads_of(image, loads[...], leaf, column, top, coeff_ref, leaf_out_ref, numbers)


def second_kernel(
    part_ref, below_ref, above_ref, left_ref, right_ref, pair_ref, gathered_ref, leaf_in_ref,
    rows_ref, smoother_scale, shape, spread, leaf, column, top, search, source, stiff,
    image_out, second_out, out_ref, face_left_ref, face_right_ref, face_low_ref, face_high_ref, sums_ref, total_ref,
):
    rows = rows_ref[...]
    weight = weight_of(rows[2:3])
    coeffs = jnp.sum(gathered_ref[...], axis=0)
    total_ref[...] = coeffs
    norm, along, size = coeffs[1:2, 0:1], coeffs[1:2, 1:2], coeffs[1:2, 2:3]
    overlap = along / norm
    scale = 1.0 / jnp.sqrt(size)
    field = wide_field(part_ref, below_ref, above_ref, left_ref, right_ref)
    first = inner_rows(field)
    image_out[...] = first
    smoothed = smoothed_of(field, smoother_scale[...], shape)
    whole = jnp.concatenate(smoothed, 1) * weight + coarse_of(
        coeffs, leaf_in_ref[...], spread[...], leaf, column, top
    )
    second = (whole - overlap * search[...]) * scale
    second_out[...] = second
    source = source[...]
    image = stiffness_of(second, pair_ref[...], stiff, rows)
    write_faces(assemble_inside(columns(image)), out_ref, face_left_ref, face_right_ref, face_low_ref, face_high_ref)
    basis = (first - overlap * source) * scale
    sums_ref[...] = numbers_row(
        [total_of(basis * basis * weight), total_of(image * source), total_of(image * basis)], 128, NP
    )


def chooser_back(order_ref):
    slot = lax.broadcasted_iota(jnp.int32, (ROWS, ROWS), 0)
    return (order_ref[...] == slot).astype(F32).T.astype(BF16)


def last_kernel(
    part_ref, before_x_ref, after_x_ref, before_y_ref, after_y_ref, sums_in_ref, rows,
    image_ref, sums_ref,
):
    lane = lanes()
    weight = columns(weight_of(rows[2:3]))
    row = lax.broadcasted_iota(jnp.int32, (ROWS, 1), 0)
    at_y = row // EZ % EY
    row_y = lane // NP % NP
    face_y = ((row_y == 0) & (at_y == 0)) | ((row_y == NP - 1) & (at_y == EY - 1))
    face_x = {0: (lane < 64) & (row < 64), 3: (lane >= 64) & (row >= 192)}
    square = jnp.zeros((ROWS, 128), F32)
    fields = faces_added(part_ref, before_x_ref, after_x_ref, before_y_ref, after_y_ref)
    for c, (own, over_x, over_y) in enumerate(zip(*fields)):
        image = own + over_x + over_y
        image_ref[:, 128 * c : 128 * c + 128] = image
        term = image * image
        if c in face_x:
            both = 4.0 * (own + over_x) * (own + over_y)
            term = jnp.where(face_x[c] & face_y, both, term)
        square = square + term * weight[c]
    sums = jnp.where(lane == 4 * NP - 1, total_of(square), sums_in_ref[...])
    device = lax.broadcasted_iota(jnp.int32, (sums_ref.shape[0], 1), 0)
    sent = jnp.zeros(sums_ref.shape, F32)
    for side_x, side_y, first_row, block, first in EDGES:
        edge = edge_out(part_ref, first_row, block, first)
        sent = jnp.where(device == diagonal_of(side_x, side_y), edge, sent)
    sums_ref[...] = jnp.where(is_number(lane), sums, sent)


def end_kernel(
    sums_ref, coeff_ref, image_two_ref, order, search_one, search_two, source, image_one,
    pressure_out, residual_out,
):
    got = sums_ref[...]
    sums = jnp.sum(got, axis=0, keepdims=True)
    squared, dot_source, dot_basis, dot_self = (
        sums[:, NP * at + NP - 1 : NP * at + NP] for at in range(4)
    )
    device = lax.broadcasted_iota(jnp.int32, (got.shape[0], 1), 0)
    image_two = columns(image_two_ref[...])
    for side_x, side_y, first_row, block, first in EDGES:
        line = jnp.where(device == diagonal_of(side_x, side_y), got, 0.0)
        edge = edge_in(jnp.sum(line, axis=0, keepdims=True), first)
        above, below = jnp.zeros((first_row, 128), F32), jnp.zeros((ROWS - EZ - first_row, 128), F32)
        parts = [part for part in (above, edge, below) if part.shape[0]]
        image_two[block] = image_two[block] + jnp.concatenate(parts, 0)
    image_two = jnp.concatenate(image_two, 1)
    coeffs = coeff_ref[...]
    norm, along, size = coeffs[1:2, 0:1], coeffs[1:2, 1:2], coeffs[1:2, 2:3]
    beta = jnp.sqrt(norm)
    basis_norm = jnp.sqrt(squared)
    first_diag = along / norm
    first_sub = basis_norm * jnp.sqrt(size) / beta
    second_top = dot_source / (beta * basis_norm)
    second_diag = dot_basis / squared
    second_sub_squared = jnp.maximum(
        dot_self / squared - second_top * second_top - second_diag * second_diag, 0.0
    )
    first_norm = jnp.sqrt(first_diag * first_diag + first_sub * first_sub)
    cosine = first_diag / first_norm
    sine_part = first_sub / first_norm
    rotated = cosine * second_top + sine_part * second_diag
    lowered = cosine * second_diag - sine_part * second_top
    second_norm = jnp.sqrt(lowered * lowered + second_sub_squared)
    factor_two = -(lowered / second_norm) * sine_part * beta / second_norm
    factor_one = (cosine * beta - rotated * factor_two) / first_norm
    step_one = factor_one / beta
    step_two = factor_two / basis_norm
    chooser = chooser_back(order)
    pressure_out.ref[...] = permuted(
        chooser, step_one * search_one[...] + step_two * search_two[...]
    )
    pressure_out.send()
    residual_out.ref[...] = permuted(
        chooser, source[...] - step_one * image_one[...] - step_two * image_two
    )
    residual_out.send()


class Far:
    def __init__(self, value):
        self.value = value


class Fetch:
    def __init__(self, source, target, sem):
        self.copy, self.target, self.waiting = pltpu.make_async_copy(source, target, sem), target, True
        self.copy.start()

    def __call__(self):
        if self.waiting:
            self.copy.wait()
            self.waiting = False
        return self.target


class Store:
    def __init__(self, ref, target, sem):
        self.ref, self.copy = ref, pltpu.make_async_copy(ref, target, sem)

    def send(self):
        self.copy.start()


def shaped(*shape):
    return jax.ShapeDtypeStruct(shape, F32)


def run(kernel, outs, *args):
    vmem, far = pl.BlockSpec(memory_space=pltpu.VMEM), pl.BlockSpec(memory_space=pltpu.HBM)
    far_in = [isinstance(arg, Far) for arg in args]
    far_out = [isinstance(out, Far) for out in outs]
    args = [arg.value if isinstance(arg, Far) else arg for arg in args]
    outs = [out.value if isinstance(out, Far) else out for out in outs]
    moved = [arg for arg, out_of in zip(args, far_in) if out_of]
    moved += [out for out, out_of in zip(outs, far_out) if out_of]
    count = len(moved)

    def body(*refs):
        ins, rest = refs[: len(args)], refs[len(args) :]
        results, scratch = rest[: len(outs)], rest[len(outs) :]
        at, given, stores = 0, [], []
        for ref, is_far in zip(ins, far_in):
            if is_far:
                ref = Fetch(ref, scratch[at], scratch[count].at[at])
                at += 1
            given.append(ref)
        for ref, is_far in zip(results, far_out):
            if is_far:
                ref = Store(scratch[at], ref, scratch[count].at[at])
                stores.append(ref)
                at += 1
            given.append(ref)
        kernel(*given)
        for store in stores:
            store.copy.wait()

    scratch = [pltpu.VMEM(item.shape, item.dtype) for item in moved]
    if count:
        scratch.append(pltpu.SemaphoreType.DMA((count,)))
    return pl.pallas_call(
        body,
        out_shape=tuple(outs),
        in_specs=[far if is_far else vmem for is_far in far_in],
        out_specs=tuple(far if is_far else vmem for is_far in far_out),
        scratch_shapes=scratch,
        compiler_params=pltpu.CompilerParams(vmem_limit_bytes=LIMIT),
    )(*args)


LIMIT = 28 * 2**20
GY = ("gh", "gl")
NEAR = ("gx", "gh")
FIELD = shaped(ROWS, NODES)
FACE = shaped(64, 128)
PAIRS = shaped(ROWS, 128)


def neighbours(low, high, axis):
    peers = lax.axis_size(axis)
    up = [(i, (i + 1) % peers) for i in range(peers)]
    down = [(j, i) for i, j in up]
    return lax.ppermute(high, axis, up), lax.ppermute(low, axis, down)


def surrounded(part, low, high, coeffs, pair=None):
    wide, across = low.shape[1], (EY + 2) * EZ
    below, above = neighbours(low, high, GY)
    gathered = lax.all_to_all(coeffs, NEAR, 0, 0)
    more = () if pair is None else (pair,)
    low, high, spread = run(
        middle_kernel,
        (shaped(across, wide), shaped(across, wide), shaped(lax.axis_size("gl"), 4, 256)),
        part, below, above, gathered, *more,
    )
    left, right = neighbours(low, high, "gx")
    return part, below, above, left, right, lax.all_to_all(spread, "gl", 0, 0)


def per_device(
    forcing, element_order, diffusivity, reaction, leaf_factor, column_factor, top_factor
):
    stiff, shape, loads, spread, rows = build_tables()
    factors = [factor[0, 0] for factor in (leaf_factor, column_factor, top_factor)]
    coarse = (shaped(lax.axis_size(NEAR), 4, 256), shaped(1, 256))
    order = element_order[0]
    part, low, high, coeffs, leaves, pair = run(
        start_kernel,
        (FIELD, shaped(64, NODES + 128), shaped(64, NODES + 128), *coarse, PAIRS),
        order, forcing[0, 0], diffusivity[0], reaction[0], *factors, loads,
    )
    *around, gathered = surrounded(part, low, high, coeffs, pair)
    source, search_one, scale, part, low, high, coeffs, leaves = run(
        first_kernel,
        (
            FIELD, FIELD, shaped((EX + 2) * (EY + 2) * EZ, NODES), FIELD, shaped(64, NODES), shaped(64, NODES), *coarse,
        ),
        *around, pair, gathered, leaves, rows, shape, spread, *factors, stiff, loads,
    )
    *around, gathered = surrounded(part, low, high, coeffs)
    image_one, search_two, part, face_left, face_right, face_low, face_high, sums, coeffs = run(
        second_kernel,
        (FIELD, FIELD, FIELD, FACE, FACE, FACE, FACE, shaped(1, 128), shaped(4, 256)),
        *around, pair, gathered, leaves, rows, scale, shape, spread, *factors,
        search_one, source, stiff,
    )
    before_x, after_x = neighbours(face_left, face_right, "gx")
    before_y, after_y = neighbours(face_low, face_high, GY)
    peers = lax.axis_size(("gx", *GY))
    image_two, sums = run(
        last_kernel, (FIELD, shaped(peers, 128)),
        part, before_x, after_x, before_y, after_y, sums, rows,
    )
    sums = lax.all_to_all(sums, ("gx", *GY), 0, 0, tiled=True)
    pressure, residual = run(
        end_kernel, (Far(FIELD), Far(FIELD)),
        sums, coeffs, image_two, order, search_one, search_two, source, image_one,
    )
    return (pressure[None, None], residual[None, None])


def solution(mesh):
    count_x, count_y = mesh.devices.shape
    mesh = Mesh(mesh.devices.reshape(count_x, 2, count_y // 2), ("gx", *GY))
    field = P("gx", GY, None, None)
    row = P("gx", GY, None)
    return jax.shard_map(
        per_device,
        mesh=mesh,
        in_specs=(field, row, row, row, field, field, field),
        out_specs=(field, field),
        check_vma=False,
    )
```

```python
import jax
import jax.numpy as jnp
import numpy as np
from jax import lax
from jax.experimental import pallas as pl
from jax.experimental.pallas import tpu as pltpu
from jax.sharding import Mesh, PartitionSpec as P

NP = 8
EX = 4
EY = 4
EZ = 16
ROWS = EX * EY * EZ
NODES = NP * NP * NP
LEVELS = EZ + 1
F32 = jnp.float32
BF16 = jnp.bfloat16


def legendre_columns(points, degree):
    columns_table = np.zeros((points.shape[0], degree + 1))
    columns_table[:, 0] = 1.0
    columns_table[:, 1] = points
    for level_at in range(2, degree + 1):
        columns_table[:, level_at] = (
            (2 * level_at - 1) * points * columns_table[:, level_at - 1]
            - (level_at - 1) * columns_table[:, level_at - 2]
        ) / level_at
    return columns_table


def jacobi_eigen(symmetric, npoints):
    matrix_work = symmetric.copy()
    vectors = np.eye(npoints)
    for sweep_at in range(15):
        for first_at in range(npoints):
            for second_at in range(first_at + 1, npoints):
                off_value = matrix_work[first_at, second_at]
                gap_value = matrix_work[second_at, second_at] - matrix_work[first_at, first_at]
                root_value = np.sqrt(gap_value * gap_value + 4.0 * off_value * off_value)
                sign_value = np.where(gap_value >= 0.0, 1.0, -1.0)
                denominator = np.abs(gap_value) + root_value
                safe_denominator = np.where(denominator > 0.0, denominator, 1.0)
                tangent = sign_value * 2.0 * off_value / safe_denominator
                cosine_value = 1.0 / np.sqrt(1.0 + tangent * tangent)
                sine_value = tangent * cosine_value
                rotation = np.eye(npoints)
                rotation[first_at, first_at] = cosine_value
                rotation[second_at, second_at] = cosine_value
                rotation[first_at, second_at] = sine_value
                rotation[second_at, first_at] = -sine_value
                matrix_work = rotation.T @ matrix_work @ rotation
                vectors = vectors @ rotation
    eigvals = np.array([matrix_work[place_at, place_at] for place_at in range(npoints)])
    return (eigvals, vectors)


def gll_tables(npoints):
    degree = npoints - 1
    estimate = -np.cos(np.pi * np.arange(npoints) / degree)
    for newton_at in range(100):
        columns_table = legendre_columns(estimate, degree)
        estimate = estimate - (
            estimate * columns_table[:, degree] - columns_table[:, degree - 1]
        ) / (npoints * columns_table[:, degree])
    values = legendre_columns(estimate, degree)[:, degree]
    weights = 2.0 / (degree * (degree + 1) * values**2)
    derivative = np.zeros((npoints, npoints))
    for row_at in range(npoints):
        for column_at in range(npoints):
            if row_at != column_at:
                derivative[row_at, column_at] = (
                    values[row_at] / values[column_at] / (estimate[row_at] - estimate[column_at])
                )
    derivative[0, 0] = -degree * (degree + 1) / 4.0
    derivative[degree, degree] = degree * (degree + 1) / 4.0
    stiffness = derivative.T @ (weights[:, None] * derivative)
    inv_root = 1.0 / np.sqrt(weights)
    symmetric = inv_root[:, None] * stiffness * inv_root[None, :]
    eigvals, eigvecs = jacobi_eigen(0.5 * (symmetric + symmetric.T), npoints)
    modes = inv_root[:, None] * eigvecs
    return (estimate, weights, stiffness, eigvals, modes)


def split_pair(table):
    high = table.astype(np.float32).astype(jnp.bfloat16)
    low = (table.astype(np.float32) - high.astype(np.float32)).astype(jnp.bfloat16)
    return np.stack([high, low])


def build_tables():
    points, weights, stiffness, eigvals, modes = gll_tables(8)
    massmat = weights[:, None] * np.eye(8)
    filler = np.ones(8)
    stiff_full = (
        np.kron(np.kron(stiffness, massmat), massmat)
        + np.kron(np.kron(massmat, stiffness), massmat)
        + np.kron(np.kron(massmat, massmat), stiffness)
    )
    mass_full = np.kron(np.kron(weights, weights), weights)
    eigen_full = (
        np.kron(np.kron(eigvals, filler), filler)
        + np.kron(np.kron(filler, eigvals), filler)
        + np.kron(np.kron(filler, filler), eigvals)
    )
    linear = np.stack([(1.0 - points) / 2.0, (1.0 + points) / 2.0], 1)
    trilinear = np.kron(np.kron(linear, linear), linear)
    even_first = np.argsort([np.sign(modes[0, m]) != np.sign(modes[7, m]) for m in range(8)], kind="stable")
    first = np.kron(np.kron(modes[:4, even_first], modes), modes)
    shape_full = np.stack([first[:, :256], first[:, 256:]])
    eigen_full = eigen_full.reshape(8, 64)[even_first].reshape(-1)
    tiles = stiff_full.reshape(8, 64, 8, 64)
    near, mirrored = tiles[:4, :, :4], tiles[:4, :, :3:-1]
    stiff_full = np.stack([near + mirrored, near - mirrored]).reshape(2, 256, 256) / 2.0
    ends = np.where((np.arange(8) == 0) | (np.arange(8) == 7), 0.5, 1.0)
    share = np.kron(np.kron(ends, ends), ends)
    rows = np.zeros((8, NODES), np.float32)
    rows[0], rows[1], rows[2] = eigen_full, mass_full, share
    loads = np.zeros((NODES, 128))
    loads[:, :8] = trilinear
    return (
        jnp.asarray(split_pair(stiff_full)),
        jnp.asarray(split_pair(shape_full)),
        jnp.asarray(split_pair(loads)),
        jnp.asarray(split_pair(loads.T)),
        jnp.asarray(rows),
    )


def lanes(width=128):
    return lax.broadcasted_iota(jnp.int32, (1, width), 1)


def halves(x):
    high = x.astype(BF16)
    return high, (x - high.astype(F32)).astype(BF16)


def product(x, table, contract=0):
    high, low = halves(x)
    dims = (((1,), (contract,)), ((), ()))

    def dot(p, q):
        return lax.dot_general(p, q, dims, preferred_element_type=F32)

    return dot(high, table[0]) + (dot(low, table[0]) + dot(high, table[1]))


def fold(cols):
    far, near = pltpu.roll(cols[3], 64, 1), pltpu.roll(cols[2], 64, 1)
    even = jnp.concatenate([cols[0] + far, cols[1] + near], 1)
    return even, jnp.concatenate([cols[0] - far, cols[1] - near], 1)


def unfold(even, odd):
    total, rest = even + odd, even - odd
    last, third = pltpu.roll(rest[:, :128], 64, 1), pltpu.roll(rest[:, 128:], 64, 1)
    return [total[:, :128], total[:, 128:], third, last]


def part_of(table, at):
    return table[0, at], table[1, at]


def permuted(chooser, x):
    high, rest = x.astype(BF16), x
    rest = rest - high.astype(F32)
    mid = rest.astype(BF16)
    low = (rest - mid.astype(F32)).astype(BF16)

    def dot(q):
        return jnp.dot(chooser, q, preferred_element_type=F32)

    return dot(high) + (dot(mid) + dot(low))


def columns(x):
    return [x[:, 128 * c : 128 * c + 128] for c in range(4)]


def weight_of(share):
    lane = lanes(NODES) % NP
    level = lax.broadcasted_iota(jnp.int32, (ROWS, 1), 0) % EZ
    end = ((lane == 0) & (level == 0)) | ((lane == NP - 1) & (level == EZ - 1))
    return jnp.where(end, 2.0 * share, share)


def first_plane(x):
    return jnp.where(lanes() < 64, roll_lanes(x, 64), 0.0)


def last_plane(x):
    return jnp.where(lanes() >= 64, roll_lanes(x, 64), 0.0)


def first_row(x):
    return jnp.where(lanes() // NP % NP == 0, roll_lanes(x, 72), 0.0)


def last_row(x):
    return jnp.where(lanes() // NP % NP == NP - 1, roll_lanes(x, 56), 0.0)


def roll_lanes(x, shift):
    return pltpu.roll(x.reshape(-1, 128), shift, 1).reshape(x.shape)


def sum_levels(col):
    rows = col.shape[0]
    row_z = lanes() % NP
    level = lax.broadcasted_iota(jnp.int32, (rows, 1), 0) % EZ
    up = pltpu.roll(pltpu.roll(col, 121, 1), 1, 0)
    down = pltpu.roll(pltpu.roll(col, 7, 1), rows - 1, 0)
    return (
        col
        + jnp.where((row_z == 0) & (level > 0), up, 0.0)
        + jnp.where((row_z == NP - 1) & (level < EZ - 1), down, 0.0)
    )


def blocks(col, length=EY):
    return col.reshape(-1, length, EZ, 128)


def assemble_inside(cols):
    cols = [blocks(col) for col in cols]
    edge = jnp.zeros((1, EY, EZ, 128), F32)
    cols = [
        cols[0] + jnp.concatenate([edge, first_plane(cols[3][: EX - 1])], 0),
        cols[1],
        cols[2],
        cols[3] + jnp.concatenate([last_plane(cols[0][1:]), edge], 0),
    ]
    edge = jnp.zeros((EX, 1, EZ, 128), F32)
    result = []
    for col in cols:
        col = (
            col
            + jnp.concatenate([edge, first_row(col[:, : EY - 1])], 1)
            + jnp.concatenate([last_row(col[:, 1:]), edge], 1)
        )
        result.append(sum_levels(col.reshape(ROWS, 128)))
    return result


def joined_x(middle, left, right):
    middle, left, right = list(middle), list(left), list(right)
    low, high = middle[0], middle[3]
    hole = jnp.zeros_like(low[1:])
    middle[0] = low + jnp.concatenate([first_plane(left[3]), hole], 0)
    middle[3] = high + jnp.concatenate([hole, last_plane(right[0])], 0)
    left[3] = left[3] + last_plane(low[:1])
    right[0] = right[0] + first_plane(high[EX - 1 :])
    return [jnp.concatenate(parts, 0) for parts in zip(left, middle, right)]


def joined_y(middle, below, above):
    first, last = middle[:, :1], middle[:, EY - 1 :]
    hole = jnp.zeros_like(middle[:, 1 : EY - 1])
    middle = middle + jnp.concatenate([first_row(below), hole, last_row(above)], 1)
    return jnp.concatenate([below + last_row(first), middle, above + first_row(last)], 1)


def assemble_wide(cols):
    cols = [
        cols[0][1:-1] + first_plane(cols[3][:-2]),
        cols[1][1:-1],
        cols[2][1:-1],
        cols[3][1:-1] + last_plane(cols[0][2:]),
    ]
    return [
        sum_levels((col[:, 1:-1] + first_row(col[:, :-2]) + last_row(col[:, 2:])).reshape(ROWS, 128))
        for col in cols
    ]


def is_even(axis):
    return lax.rem(lax.axis_index("gx" if axis == "gx" else "gl"), 2) == 0


def write_sides(axis, first_ref, second_ref, at, low, high):
    even = is_even(axis)
    first_ref[at] = jnp.where(even, high, low)
    second_ref[at] = jnp.where(even, low, high)


class Side:
    def __init__(self, axis, even_ref, odd_ref):
        self.even, self.refs = is_even(axis), (even_ref, odd_ref)
        self.shape = even_ref.shape

    def __getitem__(self, at):
        return jnp.where(self.even, self.refs[0][at], self.refs[1][at])


def sides_of(axis, first_ref, second_ref):
    return Side(axis, second_ref, first_ref), Side(axis, first_ref, second_ref)


def write_faces(cols, part_ref, face_left_ref, face_right_ref, face_low_ref, face_high_ref):
    row_y = lanes() // NP % NP
    for c in range(4):
        part_ref[:, 128 * c : 128 * c + 128] = cols[c]
    write_sides("gx", face_left_ref, face_right_ref, ..., cols[0][:64], cols[3][192:])
    low = jnp.zeros((64, 128), F32)
    high = jnp.zeros((64, 128), F32)
    for c in range(4):
        split = cols[c].reshape(EX, EY, EZ, 128)
        first = jnp.where(row_y == 0, split[:, 0].reshape(64, 128), 0.0)
        last = jnp.where(row_y == NP - 1, split[:, EY - 1].reshape(64, 128), 0.0)
        low = low + (pltpu.roll(first, 8 * c, 1) if c else first)
        high = high + pltpu.roll(last, (72 + 8 * c) % 128, 1)
    write_sides("gy", face_low_ref, face_high_ref, ..., low, high)


def write_planes(cols, part_ref, below_ref, above_ref):
    for c in range(4):
        at = slice(128 * c, 128 * c + 128)
        part_ref[:, at] = cols[c]
        write_plane_pair(cols[c], below_ref, above_ref, at)


def write_plane_pair(col, first_ref, second_ref, at):
    low, high = blocks(col)[:, 0].reshape(64, 128), blocks(col)[:, EY - 1].reshape(64, 128)
    write_sides("gy", first_ref, second_ref, (slice(None), at), low, high)


def faces_added(part_ref, before_x_ref, after_x_ref, before_y_ref, after_y_ref):
    lane = lanes()
    row_y = lane // NP % NP
    rest = jnp.zeros((192, 128), F32)
    before = jnp.where(lane < 64, pltpu.roll(before_x_ref[...], 64, 1), 0.0)
    after = jnp.where(lane >= 64, pltpu.roll(after_x_ref[...], 64, 1), 0.0)
    none = jnp.zeros((ROWS, 128), F32)
    over_x = [jnp.concatenate([before, rest], 0), none, none, jnp.concatenate([rest, after], 0)]
    before_y, after_y = before_y_ref[...], after_y_ref[...]
    hole = jnp.zeros((EX, EY - 2, EZ, 128), F32)
    own, over_y = [], []
    for c in range(4):
        own.append(part_ref[:, 128 * c : 128 * c + 128])
        low = pltpu.roll(before_y, (128 - 8 * c) % 128, 1) if c else before_y
        low = jnp.where(row_y == 0, low, 0.0).reshape(EX, 1, EZ, 128)
        high = jnp.where(row_y == NP - 1, pltpu.roll(after_y, 56 - 8 * c, 1), 0.0)
        high = high.reshape(EX, 1, EZ, 128)
        over_y.append(jnp.concatenate([low, hole, high], 1).reshape(ROWS, 128))
    return own, over_x, over_y


EDGES = ((-1, -1, 0, 0, 0), (-1, 1, 48, 0, 56), (1, -1, 192, 3, 64), (1, 1, 240, 3, 120))


def over_lanes(x):
    for shift in (8, 16, 32, 64):
        x = x + pltpu.roll(x, shift, 1)
    return x


def diagonal_of(side_x, side_y):
    count_x, count_y = lax.axis_size("gx"), lax.axis_size(GY)
    at_y = lax.axis_index("gh") * lax.axis_size("gl") + lax.axis_index("gl")
    at_x = lax.rem(lax.axis_index("gx") + count_x + side_x, count_x)
    return at_x * count_y + lax.rem(at_y + count_y + side_y, count_y)


def edge_out(part_ref, row, block, first):
    lane = lanes()
    piece = part_ref[row : row + EZ, 128 * block : 128 * block + 128]
    piece = over_lanes(jnp.where((lane >= first) & (lane < first + NP), piece, 0.0))
    level = lax.broadcasted_iota(jnp.int32, (EZ, 1), 0)
    return jnp.sum(jnp.where(lane // NP == level, piece, 0.0), axis=0, keepdims=True)


def edge_in(line, first):
    lane = lanes()
    line = jnp.where(is_number(lane), pltpu.roll(line, 127, 1), line)
    level = lax.broadcasted_iota(jnp.int32, (EZ, 1), 0)
    spread = over_lanes(jnp.where(lane // NP == level, line, 0.0))
    return jnp.where((lane >= first) & (lane < first + NP), spread, 0.0)


def is_number(lane):
    return (lane % NP == NP - 1) & (lane < 4 * NP)


def factor_rows(ref, at, count):
    if at < count - 1:
        return ref[pl.ds(LEVELS * at, 24), :]
    return pltpu.roll(ref[pl.ds(LEVELS * count - 24, 24), :], LEVELS, 0)


def loads_of(unassembled, loads, leaf_ref, column_ref, top_ref, coeff_ref, leaf_out_ref, numbers):
    corner = product(unassembled, loads)
    lane = lanes()
    pad = jnp.zeros((8, 128), F32)
    lifted = []
    for at in range(EX * EY):
        piece = corner[16 * at : 16 * at + 16]
        same = jnp.concatenate([jnp.where(lane % 2 == 0, piece, 0.0), pad], 0)
        above = jnp.concatenate([jnp.where(lane % 2 == 1, piece, 0.0), pad], 0)
        lifted.append(same + pltpu.roll(above, 1, 0))
    top_sum = jnp.zeros((24, 256), F32)
    column_sum = jnp.zeros((24, 256), F32)
    leaf_sum = jnp.zeros((24, 256), F32)
    for vx in range(EX + 1):
        for vy in range(EY + 1):
            total = jnp.zeros((24, 128), F32)
            for sx in (0, 1):
                for sy in (0, 1):
                    if 0 <= vx - sx < EX and 0 <= vy - sy < EY:
                        piece = lifted[(vx - sx) * EY + vy - sy]
                        total = total + jnp.where(lane // 2 == sx * 2 + sy, piece, 0.0)
            vertex = jnp.sum(total, axis=1, keepdims=True)
            at = vx * (EY + 1) + vy
            top_sum = top_sum + factor_rows(top_ref, at, 25) * vertex
            if 0 < vx < EX:
                column_sum = column_sum + factor_rows(column_ref, at, 25) * vertex
                if 0 < vy < EY:
                    leaf_sum = leaf_sum + factor_rows(leaf_ref, (vx - 1) * 3 + vy - 1, 9) * vertex
    row = lax.broadcasted_iota(jnp.int32, (4, 1), 0)
    coeffs = jnp.where(row == 1, numbers, 0.0)
    coeffs = jnp.where(row == 0, jnp.sum(top_sum, axis=0, keepdims=True), coeffs)
    coeffs = jnp.where(row == 2, jnp.sum(column_sum, axis=0, keepdims=True), coeffs)
    coeff_ref[...] = jnp.broadcast_to(coeffs[None], coeff_ref.shape)
    leaf_out_ref[...] = jnp.sum(leaf_sum, axis=0, keepdims=True)


def coarse_of(coeffs, leaf_coeffs, spread, leaf_ref, column_ref, top_ref):
    lane = lanes()
    top, column = coeffs[0:1], coeffs[2:3]
    around = []
    for vx in range(EX + 1):
        for vy in range(EY + 1):
            at = vx * (EY + 1) + vy
            total = factor_rows(top_ref, at, 25) * top
            if 0 < vx < EX:
                total = total + factor_rows(column_ref, at, 25) * column
                if 0 < vy < EY:
                    total = total + factor_rows(leaf_ref, (vx - 1) * 3 + vy - 1, 9) * leaf_coeffs
            vertex = jnp.sum(total, axis=1, keepdims=True)
            same = jnp.broadcast_to(vertex, (24, 128))
            around.append(jnp.where(lane % 2 == 0, same, pltpu.roll(same, 23, 0))[:16])
    corners = []
    for ex in range(EX):
        for ey in range(EY):
            value = jnp.zeros((16, 128), F32)
            for sx in (0, 1):
                for sy in (0, 1):
                    piece = around[(ex + sx) * (EY + 1) + ey + sy]
                    value = jnp.where(lane // 2 == sx * 2 + sy, piece, value)
            corners.append(value)
    return product(jnp.concatenate(corners, 0), spread)


def total_of(x):
    return jnp.sum(jnp.sum(x, axis=0, keepdims=True), axis=1, keepdims=True)


def numbers_row(values, width=256, step=1):
    lane = lanes(width)
    row = jnp.zeros((1, width), F32)
    for at, value in enumerate(values):
        row = jnp.where(lane == step * (at + 1) - 1, value, row)
    return row


def start_kernel(
    order_ref, forcing_ref, diffusivity_ref, reaction_ref, leaf_ref, column_ref, top_ref, loads_ref,
    part_ref, below_ref, above_ref, coeff_ref, leaf_out_ref, pair_ref,
):
    slot = lax.broadcasted_iota(jnp.int32, (ROWS, ROWS), 0)
    chooser = (order_ref[...] == slot).astype(F32)
    diffusion = jnp.sum(chooser * diffusivity_ref[...], axis=1, keepdims=True)
    reacting = jnp.sum(chooser * reaction_ref[...], axis=1, keepdims=True)
    pair = jnp.where(lanes() == 0, diffusion, reacting)
    pair_ref[...] = pair
    write_plane_pair(pair, below_ref, above_ref, slice(NODES, NODES + 128))
    source = permuted(chooser.astype(BF16), forcing_ref[...])
    write_planes(assemble_inside(columns(source)), part_ref, below_ref, above_ref)
    loads_of(
        source, loads_ref[...], leaf_ref, column_ref, top_ref, coeff_ref, leaf_out_ref, numbers_row([])
    )


def own_plane(ref, c, plane):
    return blocks(ref[EY * EZ * plane : EY * EZ * (plane + 1), 128 * c : 128 * c + 128])


def got_plane(ref, c, plane):
    return blocks(ref[EZ * plane : EZ * (plane + 1), 128 * c : 128 * c + 128], 1)


def middle_kernel(part_ref, below_ref, above_ref, gathered_ref, *refs):
    below_ref, above_ref = sides_of("gy", below_ref, above_ref)
    with_pair = len(refs) == 4
    low_ref, high_ref, spread_ref = refs[-3:]
    row = lax.broadcasted_iota(jnp.int32, (4, 1), 0)
    halves_of, me = gathered_ref.shape[0] // lax.axis_size("gx"), lax.axis_index("gx")
    gathered = gathered_ref[...]
    source = lax.broadcasted_iota(jnp.int32, (gathered.shape[0], 1, 1), 0) // halves_of
    mine = jnp.sum(jnp.where(source == me, gathered, 0.0), axis=0)
    coeffs = jnp.where(row < 2, jnp.sum(gathered, axis=0), mine)
    spread_ref[...] = jnp.broadcast_to(coeffs[None], spread_ref.shape)
    for c in range(4 + with_pair):
        found = []
        for plane in (0, EX - 1):
            sides = got_plane(below_ref, c, plane), got_plane(above_ref, c, plane)
            if c < 4:
                col = joined_y(own_plane(part_ref, c, plane), *sides)
            else:
                col = jnp.concatenate([sides[0], own_plane(refs[0], 0, plane), sides[1]], 1)
            found.append(col.reshape(-1, 128))
        write_sides("gx", low_ref, high_ref, (slice(None), slice(128 * c, 128 * c + 128)), *found)


def wide_field(part_ref, below_ref, above_ref, left_ref, right_ref):
    middle, left, right = [], [], []
    for c in range(4):
        at = slice(128 * c, 128 * c + 128)
        middle.append(
            joined_y(blocks(part_ref[:, at]), blocks(below_ref[:, at], 1), blocks(above_ref[:, at], 1))
        )
        left.append(blocks(left_ref[:, at], EY + 2))
        right.append(blocks(right_ref[:, at], EY + 2))
    return joined_x(middle, left, right)


def inner_rows(cols):
    return jnp.concatenate([col[1:-1, 1:-1].reshape(ROWS, 128) for col in cols], 1)


def smoothed_of(cols, scale, shape):
    halves_of = fold([col.reshape(-1, 128) for col in cols])
    back = []
    for at, half in enumerate(halves_of):
        table = part_of(shape, at)
        modes = product(half, table) * scale[:, 256 * at : 256 * at + 256]
        back.append(product(modes, table, 1))
    return assemble_wide([blocks(col, EY + 2) for col in unfold(*back)])


def stiffness_of(field, pair, stiff, rows):
    halves_of = fold(columns(field))
    done = [product(half, part_of(stiff, at)) for at, half in enumerate(halves_of)]
    stiffened = jnp.concatenate(unfold(*done), 1)
    return stiffened * pair[:, 0:1] + field * (rows[1:2] * pair[:, 1:2])


def first_kernel(
    part_ref, below_ref, above_ref, left_ref, right_ref, pair_ref, gathered_ref, leaf_in_ref,
    rows_ref, shape, spread, leaf, column, top, stiff, loads,
    source_out, search_out, scale_out, out_ref, below_out_ref, above_out_ref, coeff_ref,
    leaf_out_ref,
):
    rows = rows_ref[...]
    weight = weight_of(rows[2:3])
    below_ref, above_ref = sides_of("gy", below_ref, above_ref)
    left_ref, right_ref = sides_of("gx", left_ref, right_ref)
    field = wide_field(part_ref, below_ref, above_ref, left_ref, right_ref)
    source = inner_rows(field)
    source_out[...] = source
    own = pair_ref[...]
    at = slice(NODES, NODES + 128)
    wide_pair = jnp.concatenate(
        [blocks(below_ref[:, at], 1), blocks(own), blocks(above_ref[:, at], 1)], 1
    ).reshape(-1, 128)
    wide_pair = jnp.concatenate([left_ref[:, at], wide_pair, right_ref[:, at]], 0)
    coeffs = jnp.sum(gathered_ref[...], axis=0)
    scale = 1.0 / (wide_pair[:, 0:1] * rows[0:1] + wide_pair[:, 1:2])
    scale_out[...] = scale
    smoothed = smoothed_of(field, scale, shape)
    search = jnp.concatenate(smoothed, 1) * weight + coarse_of(
        coeffs, leaf_in_ref[...], spread[...], leaf, column, top
    )
    search_out[...] = search
    image = stiffness_of(search, own, stiff, rows)
    write_planes(assemble_inside(columns(image)), out_ref, below_out_ref, above_out_ref)
    numbers = numbers_row(
        [total_of(source * source * weight), total_of(image * source), total_of(image * image)]
    )
    loads_of(image, loads[...], leaf, column, top, coeff_ref, leaf_out_ref, numbers)


def second_kernel(
    part_ref, below_ref, above_ref, left_ref, right_ref, pair_ref, gathered_ref, leaf_in_ref,
    rows_ref, smoother_scale, shape, spread, leaf, column, top, search, source, stiff,
    image_out, second_out, out_ref, face_left_ref, face_right_ref, face_low_ref, face_high_ref, sums_ref, total_ref,
):
    rows = rows_ref[...]
    weight = weight_of(rows[2:3])
    coeffs = jnp.sum(gathered_ref[...], axis=0)
    total_ref[...] = coeffs
    norm, along, size = coeffs[1:2, 0:1], coeffs[1:2, 1:2], coeffs[1:2, 2:3]
    overlap = along / norm
    scale = 1.0 / jnp.sqrt(size)
    below_ref, above_ref = sides_of("gy", below_ref, above_ref)
    left_ref, right_ref = sides_of("gx", left_ref, right_ref)
    field = wide_field(part_ref, below_ref, above_ref, left_ref, right_ref)
    first = inner_rows(field)
    image_out[...] = first
    smoothed = smoothed_of(field, smoother_scale[...], shape)
    whole = jnp.concatenate(smoothed, 1) * weight + coarse_of(
        coeffs, leaf_in_ref[...], spread[...], leaf, column, top
    )
    second = (whole - overlap * search[...]) * scale
    second_out[...] = second
    source = source[...]
    image = stiffness_of(second, pair_ref[...], stiff, rows)
    write_faces(assemble_inside(columns(image)), out_ref, face_left_ref, face_right_ref, face_low_ref, face_high_ref)
    basis = (first - overlap * source) * scale
    sums_ref[...] = numbers_row(
        [total_of(basis * basis * weight), total_of(image * source), total_of(image * basis)], 128, NP
    )


def chooser_back(order_ref):
    slot = lax.broadcasted_iota(jnp.int32, (ROWS, ROWS), 0)
    return (order_ref[...] == slot).astype(F32).T.astype(BF16)


def last_kernel(
    part_ref, after_y_ref, before_y_ref, after_x_ref, before_x_ref, sums_in_ref, rows,
    image_ref, sums_ref,
):
    lane = lanes()
    weight = columns(weight_of(rows[2:3]))
    row = lax.broadcasted_iota(jnp.int32, (ROWS, 1), 0)
    at_y = row // EZ % EY
    row_y = lane // NP % NP
    face_y = ((row_y == 0) & (at_y == 0)) | ((row_y == NP - 1) & (at_y == EY - 1))
    face_x = {0: (lane < 64) & (row < 64), 3: (lane >= 64) & (row >= 192)}
    square = jnp.zeros((ROWS, 128), F32)
    before_x_ref, after_x_ref = sides_of("gx", before_x_ref, after_x_ref)
    before_y_ref, after_y_ref = sides_of("gy", before_y_ref, after_y_ref)
    fields = faces_added(part_ref, before_x_ref, after_x_ref, before_y_ref, after_y_ref)
    for c, (own, over_x, over_y) in enumerate(zip(*fields)):
        image = own + over_x + over_y
        image_ref[:, 128 * c : 128 * c + 128] = image
        term = image * image
        if c in face_x:
            both = 4.0 * (own + over_x) * (own + over_y)
            term = jnp.where(face_x[c] & face_y, both, term)
        square = square + term * weight[c]
    sums = jnp.where(lane == 4 * NP - 1, total_of(square), sums_in_ref[...])
    device = lax.broadcasted_iota(jnp.int32, (sums_ref.shape[0], 1), 0)
    sent = jnp.zeros(sums_ref.shape, F32)
    for side_x, side_y, first_row, block, first in EDGES:
        edge = edge_out(part_ref, first_row, block, first)
        sent = jnp.where(device == diagonal_of(side_x, side_y), edge, sent)
    sums_ref[...] = jnp.where(is_number(lane), sums, sent)


def end_kernel(
    sums_ref, coeff_ref, image_two_ref, order, search_one, search_two, source, image_one,
    pressure_out, residual_out,
):
    got = sums_ref[...]
    sums = jnp.sum(got, axis=0, keepdims=True)
    squared, dot_source, dot_basis, dot_self = (
        sums[:, NP * at + NP - 1 : NP * at + NP] for at in range(4)
    )
    device = lax.broadcasted_iota(jnp.int32, (got.shape[0], 1), 0)
    image_two = columns(image_two_ref[...])
    for side_x, side_y, first_row, block, first in EDGES:
        line = jnp.where(device == diagonal_of(side_x, side_y), got, 0.0)
        edge = edge_in(jnp.sum(line, axis=0, keepdims=True), first)
        above, below = jnp.zeros((first_row, 128), F32), jnp.zeros((ROWS - EZ - first_row, 128), F32)
        parts = [part for part in (above, edge, below) if part.shape[0]]
        image_two[block] = image_two[block] + jnp.concatenate(parts, 0)
    image_two = jnp.concatenate(image_two, 1)
    coeffs = coeff_ref[...]
    norm, along, size = coeffs[1:2, 0:1], coeffs[1:2, 1:2], coeffs[1:2, 2:3]
    beta = jnp.sqrt(norm)
    basis_norm = jnp.sqrt(squared)
    first_diag = along / norm
    first_sub = basis_norm * jnp.sqrt(size) / beta
    second_top = dot_source / (beta * basis_norm)
    second_diag = dot_basis / squared
    second_sub_squared = jnp.maximum(
        dot_self / squared - second_top * second_top - second_diag * second_diag, 0.0
    )
    first_norm = jnp.sqrt(first_diag * first_diag + first_sub * first_sub)
    cosine = first_diag / first_norm
    sine_part = first_sub / first_norm
    rotated = cosine * second_top + sine_part * second_diag
    lowered = cosine * second_diag - sine_part * second_top
    second_norm = jnp.sqrt(lowered * lowered + second_sub_squared)
    factor_two = -(lowered / second_norm) * sine_part * beta / second_norm
    factor_one = (cosine * beta - rotated * factor_two) / first_norm
    step_one = factor_one / beta
    step_two = factor_two / basis_norm
    chooser = chooser_back(order)
    pressure_out.ref[...] = permuted(
        chooser, step_one * search_one[...] + step_two * search_two[...]
    )
    pressure_out.send()
    residual_out.ref[...] = permuted(
        chooser, source[...] - step_one * image_one[...] - step_two * image_two
    )
    residual_out.send()


class Far:
    def __init__(self, value):
        self.value = value


class Fetch:
    def __init__(self, source, target, sem):
        self.copy, self.target, self.waiting = pltpu.make_async_copy(source, target, sem), target, True
        self.copy.start()

    def __call__(self):
        if self.waiting:
            self.copy.wait()
            self.waiting = False
        return self.target


class Store:
    def __init__(self, ref, target, sem):
        self.ref, self.copy = ref, pltpu.make_async_copy(ref, target, sem)

    def send(self):
        self.copy.start()


def shaped(*shape):
    return jax.ShapeDtypeStruct(shape, F32)


def run(kernel, outs, *args):
    vmem, far = pl.BlockSpec(memory_space=pltpu.VMEM), pl.BlockSpec(memory_space=pltpu.HBM)
    far_in = [isinstance(arg, Far) for arg in args]
    far_out = [isinstance(out, Far) for out in outs]
    args = [arg.value if isinstance(arg, Far) else arg for arg in args]
    outs = [out.value if isinstance(out, Far) else out for out in outs]
    moved = [arg for arg, out_of in zip(args, far_in) if out_of]
    moved += [out for out, out_of in zip(outs, far_out) if out_of]
    count = len(moved)

    def body(*refs):
        ins, rest = refs[: len(args)], refs[len(args) :]
        results, scratch = rest[: len(outs)], rest[len(outs) :]
        at, given, stores = 0, [], []
        for ref, is_far in zip(ins, far_in):
            if is_far:
                ref = Fetch(ref, scratch[at], scratch[count].at[at])
                at += 1
            given.append(ref)
        for ref, is_far in zip(results, far_out):
            if is_far:
                ref = Store(scratch[at], ref, scratch[count].at[at])
                stores.append(ref)
                at += 1
            given.append(ref)
        kernel(*given)
        for store in stores:
            store.copy.wait()

    scratch = [pltpu.VMEM(item.shape, item.dtype) for item in moved]
    if count:
        scratch.append(pltpu.SemaphoreType.DMA((count,)))
    return pl.pallas_call(
        body,
        out_shape=tuple(outs),
        in_specs=[far if is_far else vmem for is_far in far_in],
        out_specs=tuple(far if is_far else vmem for is_far in far_out),
        scratch_shapes=scratch,
        compiler_params=pltpu.CompilerParams(vmem_limit_bytes=LIMIT),
    )(*args)


LIMIT = 28 * 2**20
GY = ("gh", "gl")
NEAR = ("gx", "gh")
FIELD = shaped(ROWS, NODES)
FACE = shaped(64, 128)
PAIRS = shaped(ROWS, 128)


def neighbours(first, second, axis):
    peers = lax.axis_size(axis)
    pairs = [(i, i ^ 1) for i in range(peers)]
    others = [(i, (i + 2 * (i % 2) - 1) % peers) for i in range(peers)]
    return lax.ppermute(first, axis, pairs), lax.ppermute(second, axis, others)


def surrounded(part, low, high, coeffs, pair=None):
    wide, across = low.shape[1], (EY + 2) * EZ
    below, above = neighbours(low, high, GY)
    gathered = lax.all_to_all(coeffs, NEAR, 0, 0)
    more = () if pair is None else (pair,)
    low, high, spread = run(
        middle_kernel,
        (shaped(across, wide), shaped(across, wide), shaped(lax.axis_size("gl"), 4, 256)),
        part, below, above, gathered, *more,
    )
    left, right = neighbours(low, high, "gx")
    return part, below, above, left, right, lax.all_to_all(spread, "gl", 0, 0)


def per_device(
    forcing, element_order, diffusivity, reaction, leaf_factor, column_factor, top_factor
):
    stiff, shape, loads, spread, rows = build_tables()
    factors = [factor[0, 0] for factor in (leaf_factor, column_factor, top_factor)]
    coarse = (shaped(lax.axis_size(NEAR), 4, 256), shaped(1, 256))
    order = element_order[0]
    part, low, high, coeffs, leaves, pair = run(
        start_kernel,
        (FIELD, shaped(64, NODES + 128), shaped(64, NODES + 128), *coarse, PAIRS),
        order, forcing[0, 0], diffusivity[0], reaction[0], *factors, loads,
    )
    *around, gathered = surrounded(part, low, high, coeffs, pair)
    source, search_one, scale, part, low, high, coeffs, leaves = run(
        first_kernel,
        (
            FIELD, FIELD, shaped((EX + 2) * (EY + 2) * EZ, NODES), FIELD, shaped(64, NODES), shaped(64, NODES), *coarse,
        ),
        *around, pair, gathered, leaves, rows, shape, spread, *factors, stiff, loads,
    )
    *around, gathered = surrounded(part, low, high, coeffs)
    image_one, search_two, part, face_left, face_right, face_low, face_high, sums, coeffs = run(
        second_kernel,
        (FIELD, FIELD, FIELD, FACE, FACE, FACE, FACE, shaped(1, 128), shaped(4, 256)),
        *around, pair, gathered, leaves, rows, scale, shape, spread, *factors,
        search_one, source, stiff,
    )
    before_x, after_x = neighbours(face_left, face_right, "gx")
    before_y, after_y = neighbours(face_low, face_high, GY)
    peers = lax.axis_size(("gx", *GY))
    image_two, sums = run(
        last_kernel, (FIELD, shaped(peers, 128)),
        part, after_y, before_y, after_x, before_x, sums, rows,
    )
    sums = lax.all_to_all(sums, ("gx", *GY), 0, 0, tiled=True)
    pressure, residual = run(
        end_kernel, (Far(FIELD), Far(FIELD)),
        sums, coeffs, image_two, order, search_one, search_two, source, image_one,
    )
    return (pressure[None, None], residual[None, None])


def solution(mesh):
    count_x, count_y = mesh.devices.shape
    mesh = Mesh(mesh.devices.reshape(count_x, 2, count_y // 2), ("gx", *GY))
    field = P("gx", GY, None, None)
    row = P("gx", GY, None)
    return jax.shard_map(
        per_device,
        mesh=mesh,
        in_specs=(field, row, row, row, field, field, field),
        out_specs=(field, field),
        check_vma=False,
    )
```

```python
import jax
import jax.numpy as jnp
import numpy as np
from jax import lax
from jax.experimental import pallas as pl
from jax.experimental.pallas import tpu as pltpu
from jax.sharding import Mesh, PartitionSpec as P

NP = 8
EX = 4
EY = 4
EZ = 16
ROWS = EX * EY * EZ
NODES = NP * NP * NP
LEVELS = EZ + 1
F32 = jnp.float32
BF16 = jnp.bfloat16


def legendre_columns(points, degree):
    columns_table = np.zeros((points.shape[0], degree + 1))
    columns_table[:, 0] = 1.0
    columns_table[:, 1] = points
    for level_at in range(2, degree + 1):
        columns_table[:, level_at] = (
            (2 * level_at - 1) * points * columns_table[:, level_at - 1]
            - (level_at - 1) * columns_table[:, level_at - 2]
        ) / level_at
    return columns_table


def jacobi_eigen(symmetric, npoints):
    matrix_work = symmetric.copy()
    vectors = np.eye(npoints)
    for sweep_at in range(15):
        for first_at in range(npoints):
            for second_at in range(first_at + 1, npoints):
                off_value = matrix_work[first_at, second_at]
                gap_value = matrix_work[second_at, second_at] - matrix_work[first_at, first_at]
                root_value = np.sqrt(gap_value * gap_value + 4.0 * off_value * off_value)
                sign_value = np.where(gap_value >= 0.0, 1.0, -1.0)
                denominator = np.abs(gap_value) + root_value
                safe_denominator = np.where(denominator > 0.0, denominator, 1.0)
                tangent = sign_value * 2.0 * off_value / safe_denominator
                cosine_value = 1.0 / np.sqrt(1.0 + tangent * tangent)
                sine_value = tangent * cosine_value
                rotation = np.eye(npoints)
                rotation[first_at, first_at] = cosine_value
                rotation[second_at, second_at] = cosine_value
                rotation[first_at, second_at] = sine_value
                rotation[second_at, first_at] = -sine_value
                matrix_work = rotation.T @ matrix_work @ rotation
                vectors = vectors @ rotation
    eigvals = np.array([matrix_work[place_at, place_at] for place_at in range(npoints)])
    return (eigvals, vectors)


def gll_tables(npoints):
    degree = npoints - 1
    estimate = -np.cos(np.pi * np.arange(npoints) / degree)
    for newton_at in range(100):
        columns_table = legendre_columns(estimate, degree)
        estimate = estimate - (
            estimate * columns_table[:, degree] - columns_table[:, degree - 1]
        ) / (npoints * columns_table[:, degree])
    values = legendre_columns(estimate, degree)[:, degree]
    weights = 2.0 / (degree * (degree + 1) * values**2)
    derivative = np.zeros((npoints, npoints))
    for row_at in range(npoints):
        for column_at in range(npoints):
            if row_at != column_at:
                derivative[row_at, column_at] = (
                    values[row_at] / values[column_at] / (estimate[row_at] - estimate[column_at])
                )
    derivative[0, 0] = -degree * (degree + 1) / 4.0
    derivative[degree, degree] = degree * (degree + 1) / 4.0
    stiffness = derivative.T @ (weights[:, None] * derivative)
    inv_root = 1.0 / np.sqrt(weights)
    symmetric = inv_root[:, None] * stiffness * inv_root[None, :]
    eigvals, eigvecs = jacobi_eigen(0.5 * (symmetric + symmetric.T), npoints)
    modes = inv_root[:, None] * eigvecs
    return (estimate, weights, stiffness, eigvals, modes)


def split_pair(table):
    high = table.astype(np.float32).astype(jnp.bfloat16)
    low = (table.astype(np.float32) - high.astype(np.float32)).astype(jnp.bfloat16)
    return np.stack([high, low])


def build_tables():
    points, weights, stiffness, eigvals, modes = gll_tables(8)
    massmat = weights[:, None] * np.eye(8)
    filler = np.ones(8)
    stiff_full = (
        np.kron(np.kron(stiffness, massmat), massmat)
        + np.kron(np.kron(massmat, stiffness), massmat)
        + np.kron(np.kron(massmat, massmat), stiffness)
    )
    mass_full = np.kron(np.kron(weights, weights), weights)
    eigen_full = (
        np.kron(np.kron(eigvals, filler), filler)
        + np.kron(np.kron(filler, eigvals), filler)
        + np.kron(np.kron(filler, filler), eigvals)
    )
    linear = np.stack([(1.0 - points) / 2.0, (1.0 + points) / 2.0], 1)
    trilinear = np.kron(np.kron(linear, linear), linear)
    even_first = np.argsort([np.sign(modes[0, m]) != np.sign(modes[7, m]) for m in range(8)], kind="stable")
    first = np.kron(np.kron(modes[:4, even_first], modes), modes)
    shape_full = np.stack([first[:, :256], first[:, 256:]])
    eigen_full = eigen_full.reshape(8, 64)[even_first].reshape(-1)
    tiles = stiff_full.reshape(8, 64, 8, 64)
    near, mirrored = tiles[:4, :, :4], tiles[:4, :, :3:-1]
    stiff_full = np.stack([near + mirrored, near - mirrored]).reshape(2, 256, 256) / 2.0
    ends = np.where((np.arange(8) == 0) | (np.arange(8) == 7), 0.5, 1.0)
    share = np.kron(np.kron(ends, ends), ends)
    rows = np.zeros((8, NODES), np.float32)
    rows[0], rows[1], rows[2] = eigen_full, mass_full, share
    loads = np.zeros((NODES, 128))
    loads[:, :8] = trilinear
    return (
        jnp.asarray(split_pair(stiff_full)),
        jnp.asarray(split_pair(shape_full)),
        jnp.asarray(split_pair(loads)),
        jnp.asarray(split_pair(loads.T)),
        jnp.asarray(rows),
    )


def lanes(width=128):
    return lax.broadcasted_iota(jnp.int32, (1, width), 1)


def halves(x):
    high = x.astype(BF16)
    return high, (x - high.astype(F32)).astype(BF16)


def product(x, table, contract=0):
    high, low = halves(x)
    dims = (((1,), (contract,)), ((), ()))

    def dot(p, q):
        return lax.dot_general(p, q, dims, preferred_element_type=F32)

    return dot(high, table[0]) + (dot(low, table[0]) + dot(high, table[1]))


def fold(cols):
    far, near = pltpu.roll(cols[3], 64, 1), pltpu.roll(cols[2], 64, 1)
    even = jnp.concatenate([cols[0] + far, cols[1] + near], 1)
    return even, jnp.concatenate([cols[0] - far, cols[1] - near], 1)


def unfold(even, odd):
    total, rest = even + odd, even - odd
    last, third = pltpu.roll(rest[:, :128], 64, 1), pltpu.roll(rest[:, 128:], 64, 1)
    return [total[:, :128], total[:, 128:], third, last]


def part_of(table, at):
    return table[0, at], table[1, at]


def permuted(chooser, x):
    high, rest = x.astype(BF16), x
    rest = rest - high.astype(F32)
    mid = rest.astype(BF16)
    low = (rest - mid.astype(F32)).astype(BF16)

    def dot(q):
        return jnp.dot(chooser, q, preferred_element_type=F32)

    return dot(high) + (dot(mid) + dot(low))


def columns(x):
    return [x[:, 128 * c : 128 * c + 128] for c in range(4)]


def weight_of(share):
    lane = lanes(NODES) % NP
    level = lax.broadcasted_iota(jnp.int32, (ROWS, 1), 0) % EZ
    end = ((lane == 0) & (level == 0)) | ((lane == NP - 1) & (level == EZ - 1))
    return jnp.where(end, 2.0 * share, share)


def first_plane(x):
    return jnp.where(lanes() < 64, roll_lanes(x, 64), 0.0)


def last_plane(x):
    return jnp.where(lanes() >= 64, roll_lanes(x, 64), 0.0)


def first_row(x):
    return jnp.where(lanes() // NP % NP == 0, roll_lanes(x, 72), 0.0)


def last_row(x):
    return jnp.where(lanes() // NP % NP == NP - 1, roll_lanes(x, 56), 0.0)


def swap_lanes(x, step):
    flat = x.reshape(-1, 128)
    lane = lax.broadcasted_iota(jnp.int32, flat.shape, 1)
    place = lane // step % NP
    move = jnp.where(place == 0, 7 * step, jnp.where(place == NP - 1, -7 * step, 0))
    return jnp.take_along_axis(flat, lane + move, axis=1, mode="promise_in_bounds").reshape(x.shape)


def from_rows(before, after):
    row_y = lanes() // NP % NP
    return swap_lanes(
        jnp.where(row_y == NP - 1, before, jnp.where(row_y == 0, after, 0.0)), NP
    )


def roll_lanes(x, shift):
    return pltpu.roll(x.reshape(-1, 128), shift, 1).reshape(x.shape)


def sum_levels(col):
    rows = col.shape[0]
    row_z = lanes() % NP
    level = lax.broadcasted_iota(jnp.int32, (rows, 1), 0) % EZ
    swapped = swap_lanes(col, 1)
    up = pltpu.roll(swapped, 1, 0)
    down = pltpu.roll(swapped, rows - 1, 0)
    kept = jnp.where(
        (row_z == 0) & (level > 0), up, jnp.where((row_z == NP - 1) & (level < EZ - 1), down, 0.0)
    )
    return col + kept


def blocks(col, length=EY):
    return col.reshape(-1, length, EZ, 128)


def assemble_inside(cols):
    cols = [blocks(col) for col in cols]
    edge = jnp.zeros((1, EY, EZ, 128), F32)
    cols = [
        cols[0] + jnp.concatenate([edge, first_plane(cols[3][: EX - 1])], 0),
        cols[1],
        cols[2],
        cols[3] + jnp.concatenate([last_plane(cols[0][1:]), edge], 0),
    ]
    edge = jnp.zeros((EX, 1, EZ, 128), F32)
    result = []
    for col in cols:
        before = jnp.concatenate([edge, col[:, : EY - 1]], 1)
        after = jnp.concatenate([col[:, 1:], edge], 1)
        result.append(sum_levels((col + from_rows(before, after)).reshape(ROWS, 128)))
    return result


def joined_x(middle, left, right):
    middle, left, right = list(middle), list(left), list(right)
    low, high = middle[0], middle[3]
    hole = jnp.zeros_like(low[1:])
    middle[0] = low + jnp.concatenate([first_plane(left[3]), hole], 0)
    middle[3] = high + jnp.concatenate([hole, last_plane(right[0])], 0)
    left[3] = left[3] + last_plane(low[:1])
    right[0] = right[0] + first_plane(high[EX - 1 :])
    return [jnp.concatenate(parts, 0) for parts in zip(left, middle, right)]


def joined_y(middle, below, above):
    first, last = middle[:, :1], middle[:, EY - 1 :]
    hole = jnp.zeros_like(middle[:, 1 : EY - 1])
    middle = middle + jnp.concatenate([first_row(below), hole, last_row(above)], 1)
    return jnp.concatenate([below + last_row(first), middle, above + first_row(last)], 1)


def assemble_wide(cols):
    cols = [
        cols[0][1:-1] + first_plane(cols[3][:-2]),
        cols[1][1:-1],
        cols[2][1:-1],
        cols[3][1:-1] + last_plane(cols[0][2:]),
    ]
    return [
        sum_levels((col[:, 1:-1] + from_rows(col[:, :-2], col[:, 2:])).reshape(ROWS, 128))
        for col in cols
    ]


def is_even(axis):
    return lax.rem(lax.axis_index("gx" if axis == "gx" else "gl"), 2) == 0


def write_sides(axis, first_ref, second_ref, at, low, high):
    even = is_even(axis)
    first_ref[at] = jnp.where(even, high, low)
    second_ref[at] = jnp.where(even, low, high)


class Side:
    def __init__(self, axis, even_ref, odd_ref):
        self.even, self.refs = is_even(axis), (even_ref, odd_ref)
        self.shape = even_ref.shape

    def __getitem__(self, at):
        return jnp.where(self.even, self.refs[0][at], self.refs[1][at])


def sides_of(axis, first_ref, second_ref):
    return Side(axis, second_ref, first_ref), Side(axis, first_ref, second_ref)


def write_faces(cols, part_ref, face_left_ref, face_right_ref, face_low_ref, face_high_ref):
    row_y = lanes() // NP % NP
    for c in range(4):
        part_ref[:, 128 * c : 128 * c + 128] = cols[c]
    write_sides("gx", face_left_ref, face_right_ref, ..., cols[0][:64], cols[3][192:])
    low = jnp.zeros((64, 128), F32)
    high = jnp.zeros((64, 128), F32)
    for c in range(4):
        split = cols[c].reshape(EX, EY, EZ, 128)
        first = jnp.where(row_y == 0, split[:, 0].reshape(64, 128), 0.0)
        last = jnp.where(row_y == NP - 1, split[:, EY - 1].reshape(64, 128), 0.0)
        low = low + (pltpu.roll(first, 8 * c, 1) if c else first)
        high = high + pltpu.roll(last, (72 + 8 * c) % 128, 1)
    write_sides("gy", face_low_ref, face_high_ref, ..., low, high)


def write_planes(cols, part_ref, below_ref, above_ref):
    for c in range(4):
        at = slice(128 * c, 128 * c + 128)
        part_ref[:, at] = cols[c]
        write_plane_pair(cols[c], below_ref, above_ref, at)


def write_plane_pair(col, first_ref, second_ref, at):
    low, high = blocks(col)[:, 0].reshape(64, 128), blocks(col)[:, EY - 1].reshape(64, 128)
    write_sides("gy", first_ref, second_ref, (slice(None), at), low, high)


def faces_added(part_ref, before_x_ref, after_x_ref, before_y_ref, after_y_ref):
    lane = lanes()
    row_y = lane // NP % NP
    rest = jnp.zeros((192, 128), F32)
    before = jnp.where(lane < 64, pltpu.roll(before_x_ref[...], 64, 1), 0.0)
    after = jnp.where(lane >= 64, pltpu.roll(after_x_ref[...], 64, 1), 0.0)
    none = jnp.zeros((ROWS, 128), F32)
    over_x = [jnp.concatenate([before, rest], 0), none, none, jnp.concatenate([rest, after], 0)]
    before_y, after_y = before_y_ref[...], after_y_ref[...]
    hole = jnp.zeros((EX, EY - 2, EZ, 128), F32)
    own, over_y = [], []
    for c in range(4):
        own.append(part_ref[:, 128 * c : 128 * c + 128])
        low = pltpu.roll(before_y, (128 - 8 * c) % 128, 1) if c else before_y
        low = jnp.where(row_y == 0, low, 0.0).reshape(EX, 1, EZ, 128)
        high = jnp.where(row_y == NP - 1, pltpu.roll(after_y, 56 - 8 * c, 1), 0.0)
        high = high.reshape(EX, 1, EZ, 128)
        over_y.append(jnp.concatenate([low, hole, high], 1).reshape(ROWS, 128))
    return own, over_x, over_y


EDGES = ((-1, -1, 0, 0, 0), (-1, 1, 48, 0, 56), (1, -1, 192, 3, 64), (1, 1, 240, 3, 120))


def over_lanes(x):
    for shift in (8, 16, 32, 64):
        x = x + pltpu.roll(x, shift, 1)
    return x


def diagonal_of(side_x, side_y):
    count_x, count_y = lax.axis_size("gx"), lax.axis_size(GY)
    at_y = lax.axis_index("gh") * lax.axis_size("gl") + lax.axis_index("gl")
    at_x = lax.rem(lax.axis_index("gx") + count_x + side_x, count_x)
    return at_x * count_y + lax.rem(at_y + count_y + side_y, count_y)


def edge_out(part_ref, row, block, first):
    lane = lanes()
    piece = part_ref[row : row + EZ, 128 * block : 128 * block + 128]
    piece = over_lanes(jnp.where((lane >= first) & (lane < first + NP), piece, 0.0))
    level = lax.broadcasted_iota(jnp.int32, (EZ, 1), 0)
    return jnp.sum(jnp.where(lane // NP == level, piece, 0.0), axis=0, keepdims=True)


def edge_in(line, first):
    lane = lanes()
    line = jnp.where(is_number(lane), pltpu.roll(line, 127, 1), line)
    level = lax.broadcasted_iota(jnp.int32, (EZ, 1), 0)
    spread = over_lanes(jnp.where(lane // NP == level, line, 0.0))
    return jnp.where((lane >= first) & (lane < first + NP), spread, 0.0)


def is_number(lane):
    return (lane % NP == NP - 1) & (lane < 4 * NP)


def factor_rows(ref, at, count):
    if at < count - 1:
        return ref[pl.ds(LEVELS * at, 24), :]
    return pltpu.roll(ref[pl.ds(LEVELS * count - 24, 24), :], LEVELS, 0)


def loads_of(unassembled, loads, leaf_ref, column_ref, top_ref, coeff_ref, leaf_out_ref, numbers):
    corner = product(unassembled, loads)
    lane = lanes()
    pad = jnp.zeros((8, 128), F32)
    lifted = []
    for at in range(EX * EY):
        piece = corner[16 * at : 16 * at + 16]
        same = jnp.concatenate([jnp.where(lane % 2 == 0, piece, 0.0), pad], 0)
        above = jnp.concatenate([jnp.where(lane % 2 == 1, piece, 0.0), pad], 0)
        lifted.append(same + pltpu.roll(above, 1, 0))
    top_sum = jnp.zeros((24, 256), F32)
    column_sum = jnp.zeros((24, 256), F32)
    leaf_sum = jnp.zeros((24, 256), F32)
    for vx in range(EX + 1):
        for vy in range(EY + 1):
            total = jnp.zeros((24, 128), F32)
            for sx in (0, 1):
                for sy in (0, 1):
                    if 0 <= vx - sx < EX and 0 <= vy - sy < EY:
                        piece = lifted[(vx - sx) * EY + vy - sy]
                        total = total + jnp.where(lane // 2 == sx * 2 + sy, piece, 0.0)
            vertex = jnp.sum(total, axis=1, keepdims=True)
            at = vx * (EY + 1) + vy
            top_sum = top_sum + factor_rows(top_ref, at, 25) * vertex
            if 0 < vx < EX:
                column_sum = column_sum + factor_rows(column_ref, at, 25) * vertex
                if 0 < vy < EY:
                    leaf_sum = leaf_sum + factor_rows(leaf_ref, (vx - 1) * 3 + vy - 1, 9) * vertex
    row = lax.broadcasted_iota(jnp.int32, (4, 1), 0)
    coeffs = jnp.where(row == 1, numbers, 0.0)
    coeffs = jnp.where(row == 0, jnp.sum(top_sum, axis=0, keepdims=True), coeffs)
    coeffs = jnp.where(row == 2, jnp.sum(column_sum, axis=0, keepdims=True), coeffs)
    coeff_ref[...] = jnp.broadcast_to(coeffs[None], coeff_ref.shape)
    leaf_out_ref[...] = jnp.sum(leaf_sum, axis=0, keepdims=True)


def coarse_of(coeffs, leaf_coeffs, spread, leaf_ref, column_ref, top_ref):
    lane = lanes()
    top, column = coeffs[0:1], coeffs[2:3]
    around = []
    for vx in range(EX + 1):
        for vy in range(EY + 1):
            at = vx * (EY + 1) + vy
            total = factor_rows(top_ref, at, 25) * top
            if 0 < vx < EX:
                total = total + factor_rows(column_ref, at, 25) * column
                if 0 < vy < EY:
                    total = total + factor_rows(leaf_ref, (vx - 1) * 3 + vy - 1, 9) * leaf_coeffs
            vertex = jnp.sum(total, axis=1, keepdims=True)
            same = jnp.broadcast_to(vertex, (24, 128))
            around.append(jnp.where(lane % 2 == 0, same, pltpu.roll(same, 23, 0))[:16])
    corners = []
    for ex in range(EX):
        for ey in range(EY):
            value = jnp.zeros((16, 128), F32)
            for sx in (0, 1):
                for sy in (0, 1):
                    piece = around[(ex + sx) * (EY + 1) + ey + sy]
                    value = jnp.where(lane // 2 == sx * 2 + sy, piece, value)
            corners.append(value)
    return product(jnp.concatenate(corners, 0), spread)


def total_of(x):
    return jnp.sum(jnp.sum(x, axis=0, keepdims=True), axis=1, keepdims=True)


def numbers_row(values, width=256, step=1):
    lane = lanes(width)
    row = jnp.zeros((1, width), F32)
    for at, value in enumerate(values):
        row = jnp.where(lane == step * (at + 1) - 1, value, row)
    return row


def start_kernel(
    order_ref, forcing_ref, diffusivity_ref, reaction_ref, leaf_ref, column_ref, top_ref, loads_ref,
    part_ref, below_ref, above_ref, coeff_ref, leaf_out_ref, pair_ref,
):
    slot = lax.broadcasted_iota(jnp.int32, (ROWS, ROWS), 0)
    chooser = (order_ref[...] == slot).astype(F32)
    diffusion = jnp.sum(chooser * diffusivity_ref[...], axis=1, keepdims=True)
    reacting = jnp.sum(chooser * reaction_ref[...], axis=1, keepdims=True)
    pair = jnp.where(lanes() == 0, diffusion, reacting)
    pair_ref[...] = pair
    write_plane_pair(pair, below_ref, above_ref, slice(NODES, NODES + 128))
    source = permuted(chooser.astype(BF16), forcing_ref[...])
    write_planes(assemble_inside(columns(source)), part_ref, below_ref, above_ref)
    loads_of(
        source, loads_ref[...], leaf_ref, column_ref, top_ref, coeff_ref, leaf_out_ref, numbers_row([])
    )


def own_plane(ref, c, plane):
    return blocks(ref[EY * EZ * plane : EY * EZ * (plane + 1), 128 * c : 128 * c + 128])


def got_plane(ref, c, plane):
    return blocks(ref[EZ * plane : EZ * (plane + 1), 128 * c : 128 * c + 128], 1)


def middle_kernel(part_ref, below_ref, above_ref, gathered_ref, *refs):
    below_ref, above_ref = sides_of("gy", below_ref, above_ref)
    with_pair = len(refs) == 4
    low_ref, high_ref, spread_ref = refs[-3:]
    row = lax.broadcasted_iota(jnp.int32, (4, 1), 0)
    halves_of, me = gathered_ref.shape[0] // lax.axis_size("gx"), lax.axis_index("gx")
    gathered = gathered_ref[...]
    source = lax.broadcasted_iota(jnp.int32, (gathered.shape[0], 1, 1), 0) // halves_of
    mine = jnp.sum(jnp.where(source == me, gathered, 0.0), axis=0)
    coeffs = jnp.where(row < 2, jnp.sum(gathered, axis=0), mine)
    spread_ref[...] = jnp.broadcast_to(coeffs[None], spread_ref.shape)
    for c in range(4 + with_pair):
        found = []
        for plane in (0, EX - 1):
            sides = got_plane(below_ref, c, plane), got_plane(above_ref, c, plane)
            if c < 4:
                col = joined_y(own_plane(part_ref, c, plane), *sides)
            else:
                col = jnp.concatenate([sides[0], own_plane(refs[0], 0, plane), sides[1]], 1)
            found.append(col.reshape(-1, 128))
        write_sides("gx", low_ref, high_ref, (slice(None), slice(128 * c, 128 * c + 128)), *found)


def wide_field(part_ref, below_ref, above_ref, left_ref, right_ref):
    middle, left, right = [], [], []
    for c in range(4):
        at = slice(128 * c, 128 * c + 128)
        middle.append(
            joined_y(blocks(part_ref[:, at]), blocks(below_ref[:, at], 1), blocks(above_ref[:, at], 1))
        )
        left.append(blocks(left_ref[:, at], EY + 2))
        right.append(blocks(right_ref[:, at], EY + 2))
    return joined_x(middle, left, right)


def inner_rows(cols):
    return jnp.concatenate([col[1:-1, 1:-1].reshape(ROWS, 128) for col in cols], 1)


def smoothed_of(cols, scale, shape):
    halves_of = fold([col.reshape(-1, 128) for col in cols])
    back = []
    for at, half in enumerate(halves_of):
        table = part_of(shape, at)
        modes = product(half, table) * scale[:, 256 * at : 256 * at + 256]
        back.append(product(modes, table, 1))
    return assemble_wide([blocks(col, EY + 2) for col in unfold(*back)])


def stiffness_of(field, pair, stiff, rows):
    halves_of = fold(columns(field))
    done = [product(half, part_of(stiff, at)) for at, half in enumerate(halves_of)]
    stiffened = jnp.concatenate(unfold(*done), 1)
    return stiffened * pair[:, 0:1] + field * (rows[1:2] * pair[:, 1:2])


def first_kernel(
    part_ref, below_ref, above_ref, left_ref, right_ref, pair_ref, gathered_ref, leaf_in_ref,
    rows_ref, shape, spread, leaf, column, top, stiff, loads,
    source_out, search_out, scale_out, out_ref, below_out_ref, above_out_ref, coeff_ref,
    leaf_out_ref,
):
    rows = rows_ref[...]
    weight = weight_of(rows[2:3])
    below_ref, above_ref = sides_of("gy", below_ref, above_ref)
    left_ref, right_ref = sides_of("gx", left_ref, right_ref)
    field = wide_field(part_ref, below_ref, above_ref, left_ref, right_ref)
    source = inner_rows(field)
    source_out[...] = source
    own = pair_ref[...]
    at = slice(NODES, NODES + 128)
    wide_pair = jnp.concatenate(
        [blocks(below_ref[:, at], 1), blocks(own), blocks(above_ref[:, at], 1)], 1
    ).reshape(-1, 128)
    wide_pair = jnp.concatenate([left_ref[:, at], wide_pair, right_ref[:, at]], 0)
    coeffs = jnp.sum(gathered_ref[...], axis=0)
    scale = 1.0 / (wide_pair[:, 0:1] * rows[0:1] + wide_pair[:, 1:2])
    scale_out[...] = scale
    smoothed = smoothed_of(field, scale, shape)
    search = jnp.concatenate(smoothed, 1) * weight + coarse_of(
        coeffs, leaf_in_ref[...], spread[...], leaf, column, top
    )
    search_out[...] = search
    image = stiffness_of(search, own, stiff, rows)
    write_planes(assemble_inside(columns(image)), out_ref, below_out_ref, above_out_ref)
    numbers = numbers_row(
        [total_of(source * source * weight), total_of(image * source), total_of(image * image)]
    )
    loads_of(image, loads[...], leaf, column, top, coeff_ref, leaf_out_ref, numbers)


def second_kernel(
    part_ref, below_ref, above_ref, left_ref, right_ref, pair_ref, gathered_ref, leaf_in_ref,
    rows_ref, smoother_scale, shape, spread, leaf, column, top, search, source, stiff,
    image_out, second_out, out_ref, face_left_ref, face_right_ref, face_low_ref, face_high_ref, sums_ref, total_ref,
):
    rows = rows_ref[...]
    weight = weight_of(rows[2:3])
    coeffs = jnp.sum(gathered_ref[...], axis=0)
    total_ref[...] = coeffs
    norm, along, size = coeffs[1:2, 0:1], coeffs[1:2, 1:2], coeffs[1:2, 2:3]
    overlap = along / norm
    scale = 1.0 / jnp.sqrt(size)
    below_ref, above_ref = sides_of("gy", below_ref, above_ref)
    left_ref, right_ref = sides_of("gx", left_ref, right_ref)
    field = wide_field(part_ref, below_ref, above_ref, left_ref, right_ref)
    first = inner_rows(field)
    image_out[...] = first
    smoothed = smoothed_of(field, smoother_scale[...], shape)
    whole = jnp.concatenate(smoothed, 1) * weight + coarse_of(
        coeffs, leaf_in_ref[...], spread[...], leaf, column, top
    )
    second = (whole - overlap * search[...]) * scale
    second_out[...] = second
    source = source[...]
    image = stiffness_of(second, pair_ref[...], stiff, rows)
    write_faces(assemble_inside(columns(image)), out_ref, face_left_ref, face_right_ref, face_low_ref, face_high_ref)
    basis = (first - overlap * source) * scale
    sums_ref[...] = numbers_row(
        [total_of(basis * basis * weight), total_of(image * source), total_of(image * basis)], 128, NP
    )


def chooser_back(order_ref):
    slot = lax.broadcasted_iota(jnp.int32, (ROWS, ROWS), 0)
    return (order_ref[...] == slot).astype(F32).T.astype(BF16)


def last_kernel(
    part_ref, after_y_ref, before_y_ref, after_x_ref, before_x_ref, sums_in_ref, rows,
    image_ref, sums_ref,
):
    lane = lanes()
    weight = columns(weight_of(rows[2:3]))
    row = lax.broadcasted_iota(jnp.int32, (ROWS, 1), 0)
    at_y = row // EZ % EY
    row_y = lane // NP % NP
    face_y = ((row_y == 0) & (at_y == 0)) | ((row_y == NP - 1) & (at_y == EY - 1))
    face_x = {0: (lane < 64) & (row < 64), 3: (lane >= 64) & (row >= 192)}
    square = jnp.zeros((ROWS, 128), F32)
    before_x_ref, after_x_ref = sides_of("gx", before_x_ref, after_x_ref)
    before_y_ref, after_y_ref = sides_of("gy", before_y_ref, after_y_ref)
    fields = faces_added(part_ref, before_x_ref, after_x_ref, before_y_ref, after_y_ref)
    for c, (own, over_x, over_y) in enumerate(zip(*fields)):
        image = own + over_x + over_y
        image_ref[:, 128 * c : 128 * c + 128] = image
        term = image * image
        if c in face_x:
            both = 4.0 * (own + over_x) * (own + over_y)
            term = jnp.where(face_x[c] & face_y, both, term)
        square = square + term * weight[c]
    sums = jnp.where(lane == 4 * NP - 1, total_of(square), sums_in_ref[...])
    device = lax.broadcasted_iota(jnp.int32, (sums_ref.shape[0], 1), 0)
    sent = jnp.zeros(sums_ref.shape, F32)
    for side_x, side_y, first_row, block, first in EDGES:
        edge = edge_out(part_ref, first_row, block, first)
        sent = jnp.where(device == diagonal_of(side_x, side_y), edge, sent)
    sums_ref[...] = jnp.where(is_number(lane), sums, sent)


def end_kernel(
    sums_ref, coeff_ref, image_two_ref, order, search_one, search_two, source, image_one,
    pressure_out, residual_out,
):
    got = sums_ref[...]
    sums = jnp.sum(got, axis=0, keepdims=True)
    squared, dot_source, dot_basis, dot_self = (
        sums[:, NP * at + NP - 1 : NP * at + NP] for at in range(4)
    )
    device = lax.broadcasted_iota(jnp.int32, (got.shape[0], 1), 0)
    image_two = columns(image_two_ref[...])
    for side_x, side_y, first_row, block, first in EDGES:
        line = jnp.where(device == diagonal_of(side_x, side_y), got, 0.0)
        edge = edge_in(jnp.sum(line, axis=0, keepdims=True), first)
        above, below = jnp.zeros((first_row, 128), F32), jnp.zeros((ROWS - EZ - first_row, 128), F32)
        parts = [part for part in (above, edge, below) if part.shape[0]]
        image_two[block] = image_two[block] + jnp.concatenate(parts, 0)
    image_two = jnp.concatenate(image_two, 1)
    coeffs = coeff_ref[...]
    norm, along, size = coeffs[1:2, 0:1], coeffs[1:2, 1:2], coeffs[1:2, 2:3]
    beta = jnp.sqrt(norm)
    basis_norm = jnp.sqrt(squared)
    first_diag = along / norm
    first_sub = basis_norm * jnp.sqrt(size) / beta
    second_top = dot_source / (beta * basis_norm)
    second_diag = dot_basis / squared
    second_sub_squared = jnp.maximum(
        dot_self / squared - second_top * second_top - second_diag * second_diag, 0.0
    )
    first_norm = jnp.sqrt(first_diag * first_diag + first_sub * first_sub)
    cosine = first_diag / first_norm
    sine_part = first_sub / first_norm
    rotated = cosine * second_top + sine_part * second_diag
    lowered = cosine * second_diag - sine_part * second_top
    second_norm = jnp.sqrt(lowered * lowered + second_sub_squared)
    factor_two = -(lowered / second_norm) * sine_part * beta / second_norm
    factor_one = (cosine * beta - rotated * factor_two) / first_norm
    step_one = factor_one / beta
    step_two = factor_two / basis_norm
    chooser = chooser_back(order)
    pressure_out.ref[...] = permuted(
        chooser, step_one * search_one[...] + step_two * search_two[...]
    )
    pressure_out.send()
    residual_out.ref[...] = permuted(
        chooser, source[...] - step_one * image_one[...] - step_two * image_two
    )
    residual_out.send()


class Far:
    def __init__(self, value):
        self.value = value


class Fetch:
    def __init__(self, source, target, sem):
        self.copy, self.target, self.waiting = pltpu.make_async_copy(source, target, sem), target, True
        self.copy.start()

    def __call__(self):
        if self.waiting:
            self.copy.wait()
            self.waiting = False
        return self.target


class Store:
    def __init__(self, ref, target, sem):
        self.ref, self.copy = ref, pltpu.make_async_copy(ref, target, sem)

    def send(self):
        self.copy.start()


def shaped(*shape):
    return jax.ShapeDtypeStruct(shape, F32)


def run(kernel, outs, *args):
    vmem, far = pl.BlockSpec(memory_space=pltpu.VMEM), pl.BlockSpec(memory_space=pltpu.HBM)
    far_in = [isinstance(arg, Far) for arg in args]
    far_out = [isinstance(out, Far) for out in outs]
    args = [arg.value if isinstance(arg, Far) else arg for arg in args]
    outs = [out.value if isinstance(out, Far) else out for out in outs]
    moved = [arg for arg, out_of in zip(args, far_in) if out_of]
    moved += [out for out, out_of in zip(outs, far_out) if out_of]
    count = len(moved)

    def body(*refs):
        ins, rest = refs[: len(args)], refs[len(args) :]
        results, scratch = rest[: len(outs)], rest[len(outs) :]
        at, given, stores = 0, [], []
        for ref, is_far in zip(ins, far_in):
            if is_far:
                ref = Fetch(ref, scratch[at], scratch[count].at[at])
                at += 1
            given.append(ref)
        for ref, is_far in zip(results, far_out):
            if is_far:
                ref = Store(scratch[at], ref, scratch[count].at[at])
                stores.append(ref)
                at += 1
            given.append(ref)
        kernel(*given)
        for store in stores:
            store.copy.wait()

    scratch = [pltpu.VMEM(item.shape, item.dtype) for item in moved]
    if count:
        scratch.append(pltpu.SemaphoreType.DMA((count,)))
    return pl.pallas_call(
        body,
        out_shape=tuple(outs),
        in_specs=[far if is_far else vmem for is_far in far_in],
        out_specs=tuple(far if is_far else vmem for is_far in far_out),
        scratch_shapes=scratch,
        compiler_params=pltpu.CompilerParams(vmem_limit_bytes=LIMIT),
    )(*args)


LIMIT = 28 * 2**20
GY = ("gh", "gl")
NEAR = ("gx", "gh")
FIELD = shaped(ROWS, NODES)
FACE = shaped(64, 128)
PAIRS = shaped(ROWS, 128)


def neighbours(first, second, axis):
    peers = lax.axis_size(axis)
    pairs = [(i, i ^ 1) for i in range(peers)]
    others = [(i, (i + 2 * (i % 2) - 1) % peers) for i in range(peers)]
    return lax.ppermute(first, axis, pairs), lax.ppermute(second, axis, others)


def surrounded(part, low, high, coeffs, pair=None):
    wide, across = low.shape[1], (EY + 2) * EZ
    below, above = neighbours(low, high, GY)
    gathered = lax.all_to_all(coeffs, NEAR, 0, 0)
    more = () if pair is None else (pair,)
    low, high, spread = run(
        middle_kernel,
        (shaped(across, wide), shaped(across, wide), shaped(lax.axis_size("gl"), 4, 256)),
        part, below, above, gathered, *more,
    )
    left, right = neighbours(low, high, "gx")
    return part, below, above, left, right, lax.all_to_all(spread, "gl", 0, 0)


def per_device(
    forcing, element_order, diffusivity, reaction, leaf_factor, column_factor, top_factor
):
    stiff, shape, loads, spread, rows = build_tables()
    factors = [factor[0, 0] for factor in (leaf_factor, column_factor, top_factor)]
    coarse = (shaped(lax.axis_size(NEAR), 4, 256), shaped(1, 256))
    order = element_order[0]
    part, low, high, coeffs, leaves, pair = run(
        start_kernel,
        (FIELD, shaped(64, NODES + 128), shaped(64, NODES + 128), *coarse, PAIRS),
        order, forcing[0, 0], diffusivity[0], reaction[0], *factors, loads,
    )
    *around, gathered = surrounded(part, low, high, coeffs, pair)
    source, search_one, scale, part, low, high, coeffs, leaves = run(
        first_kernel,
        (
            FIELD, FIELD, shaped((EX + 2) * (EY + 2) * EZ, NODES), FIELD, shaped(64, NODES), shaped(64, NODES), *coarse,
        ),
        *around, pair, gathered, leaves, rows, shape, spread, *factors, stiff, loads,
    )
    *around, gathered = surrounded(part, low, high, coeffs)
    image_one, search_two, part, face_left, face_right, face_low, face_high, sums, coeffs = run(
        second_kernel,
        (FIELD, FIELD, FIELD, FACE, FACE, FACE, FACE, shaped(1, 128), shaped(4, 256)),
        *around, pair, gathered, leaves, rows, scale, shape, spread, *factors,
        search_one, source, stiff,
    )
    before_x, after_x = neighbours(face_left, face_right, "gx")
    before_y, after_y = neighbours(face_low, face_high, GY)
    peers = lax.axis_size(("gx", *GY))
    image_two, sums = run(
        last_kernel, (FIELD, shaped(peers, 128)),
        part, after_y, before_y, after_x, before_x, sums, rows,
    )
    sums = lax.all_to_all(sums, ("gx", *GY), 0, 0, tiled=True)
    pressure, residual = run(
        end_kernel, (Far(FIELD), Far(FIELD)),
        sums, coeffs, image_two, order, search_one, search_two, source, image_one,
    )
    return (pressure[None, None], residual[None, None])


def solution(mesh):
    count_x, count_y = mesh.devices.shape
    mesh = Mesh(mesh.devices.reshape(count_x, 2, count_y // 2), ("gx", *GY))
    field = P("gx", GY, None, None)
    row = P("gx", GY, None)
    return jax.shard_map(
        per_device,
        mesh=mesh,
        in_specs=(field, row, row, row, field, field, field),
        out_specs=(field, field),
        check_vma=False,
    )
```

```python
import jax
import jax.numpy as jnp
import numpy as np
from jax import lax
from jax.experimental import pallas as pl
from jax.experimental.pallas import tpu as pltpu
from jax.sharding import Mesh, PartitionSpec as P

NP = 8
EX = 4
EY = 4
EZ = 16
ROWS = EX * EY * EZ
NODES = NP * NP * NP
LEVELS = EZ + 1
F32 = jnp.float32
BF16 = jnp.bfloat16


def legendre_columns(points, degree):
    columns_table = np.zeros((points.shape[0], degree + 1))
    columns_table[:, 0] = 1.0
    columns_table[:, 1] = points
    for level_at in range(2, degree + 1):
        columns_table[:, level_at] = (
            (2 * level_at - 1) * points * columns_table[:, level_at - 1]
            - (level_at - 1) * columns_table[:, level_at - 2]
        ) / level_at
    return columns_table


def jacobi_eigen(symmetric, npoints):
    matrix_work = symmetric.copy()
    vectors = np.eye(npoints)
    for sweep_at in range(15):
        for first_at in range(npoints):
            for second_at in range(first_at + 1, npoints):
                off_value = matrix_work[first_at, second_at]
                gap_value = matrix_work[second_at, second_at] - matrix_work[first_at, first_at]
                root_value = np.sqrt(gap_value * gap_value + 4.0 * off_value * off_value)
                sign_value = np.where(gap_value >= 0.0, 1.0, -1.0)
                denominator = np.abs(gap_value) + root_value
                safe_denominator = np.where(denominator > 0.0, denominator, 1.0)
                tangent = sign_value * 2.0 * off_value / safe_denominator
                cosine_value = 1.0 / np.sqrt(1.0 + tangent * tangent)
                sine_value = tangent * cosine_value
                rotation = np.eye(npoints)
                rotation[first_at, first_at] = cosine_value
                rotation[second_at, second_at] = cosine_value
                rotation[first_at, second_at] = sine_value
                rotation[second_at, first_at] = -sine_value
                matrix_work = rotation.T @ matrix_work @ rotation
                vectors = vectors @ rotation
    eigvals = np.array([matrix_work[place_at, place_at] for place_at in range(npoints)])
    return (eigvals, vectors)


def gll_tables(npoints):
    degree = npoints - 1
    estimate = -np.cos(np.pi * np.arange(npoints) / degree)
    for newton_at in range(100):
        columns_table = legendre_columns(estimate, degree)
        estimate = estimate - (
            estimate * columns_table[:, degree] - columns_table[:, degree - 1]
        ) / (npoints * columns_table[:, degree])
    values = legendre_columns(estimate, degree)[:, degree]
    weights = 2.0 / (degree * (degree + 1) * values**2)
    derivative = np.zeros((npoints, npoints))
    for row_at in range(npoints):
        for column_at in range(npoints):
            if row_at != column_at:
                derivative[row_at, column_at] = (
                    values[row_at] / values[column_at] / (estimate[row_at] - estimate[column_at])
                )
    derivative[0, 0] = -degree * (degree + 1) / 4.0
    derivative[degree, degree] = degree * (degree + 1) / 4.0
    stiffness = derivative.T @ (weights[:, None] * derivative)
    inv_root = 1.0 / np.sqrt(weights)
    symmetric = inv_root[:, None] * stiffness * inv_root[None, :]
    eigvals, eigvecs = jacobi_eigen(0.5 * (symmetric + symmetric.T), npoints)
    modes = inv_root[:, None] * eigvecs
    return (estimate, weights, stiffness, eigvals, modes)


def split_pair(table):
    high = table.astype(np.float32).astype(jnp.bfloat16)
    low = (table.astype(np.float32) - high.astype(np.float32)).astype(jnp.bfloat16)
    return np.stack([high, low])


def build_tables():
    points, weights, stiffness, eigvals, modes = gll_tables(8)
    massmat = weights[:, None] * np.eye(8)
    filler = np.ones(8)
    stiff_full = (
        np.kron(np.kron(stiffness, massmat), massmat)
        + np.kron(np.kron(massmat, stiffness), massmat)
        + np.kron(np.kron(massmat, massmat), stiffness)
    )
    mass_full = np.kron(np.kron(weights, weights), weights)
    eigen_full = (
        np.kron(np.kron(eigvals, filler), filler)
        + np.kron(np.kron(filler, eigvals), filler)
        + np.kron(np.kron(filler, filler), eigvals)
    )
    linear = np.stack([(1.0 - points) / 2.0, (1.0 + points) / 2.0], 1)
    trilinear = np.kron(np.kron(linear, linear), linear)
    even_first = np.argsort([np.sign(modes[0, m]) != np.sign(modes[7, m]) for m in range(8)], kind="stable")
    first = np.kron(np.kron(modes[:4, even_first], modes), modes)
    shape_full = np.stack([first[:, :256], first[:, 256:]])
    eigen_full = eigen_full.reshape(8, 64)[even_first].reshape(-1)
    tiles = stiff_full.reshape(8, 64, 8, 64)
    near, mirrored = tiles[:4, :, :4], tiles[:4, :, :3:-1]
    stiff_full = np.stack([near + mirrored, near - mirrored]).reshape(2, 256, 256) / 2.0
    ends = np.where((np.arange(8) == 0) | (np.arange(8) == 7), 0.5, 1.0)
    share = np.kron(np.kron(ends, ends), ends)
    rows = np.zeros((8, NODES), np.float32)
    rows[0], rows[1], rows[2] = eigen_full, mass_full, share
    loads = np.zeros((NODES, 128))
    loads[:, :8] = trilinear
    return (
        jnp.asarray(split_pair(stiff_full)),
        jnp.asarray(split_pair(shape_full)),
        jnp.asarray(split_pair(loads)),
        jnp.asarray(split_pair(loads.T)),
        jnp.asarray(rows),
    )


def lanes(width=128):
    return lax.broadcasted_iota(jnp.int32, (1, width), 1)


def halves(x):
    high = x.astype(BF16)
    return high, (x - high.astype(F32)).astype(BF16)


def product(x, table, contract=0):
    high, low = halves(x)
    dims = (((1,), (contract,)), ((), ()))

    def dot(p, q):
        return lax.dot_general(p, q, dims, preferred_element_type=F32)

    return dot(high, table[0]) + (dot(low, table[0]) + dot(high, table[1]))


def fold(cols):
    far, near = pltpu.roll(cols[3], 64, 1), pltpu.roll(cols[2], 64, 1)
    even = jnp.concatenate([cols[0] + far, cols[1] + near], 1)
    return even, jnp.concatenate([cols[0] - far, cols[1] - near], 1)


def unfold(even, odd):
    total, rest = even + odd, even - odd
    last, third = pltpu.roll(rest[:, :128], 64, 1), pltpu.roll(rest[:, 128:], 64, 1)
    return [total[:, :128], total[:, 128:], third, last]


def part_of(table, at):
    return table[0, at], table[1, at]


def permuted(chooser, x):
    high, rest = x.astype(BF16), x
    rest = rest - high.astype(F32)
    mid = rest.astype(BF16)
    low = (rest - mid.astype(F32)).astype(BF16)

    def dot(q):
        return jnp.dot(chooser, q, preferred_element_type=F32)

    return dot(high) + (dot(mid) + dot(low))


def columns(x):
    return [x[:, 128 * c : 128 * c + 128] for c in range(4)]


def weight_of(share):
    lane = lanes(NODES) % NP
    level = lax.broadcasted_iota(jnp.int32, (ROWS, 1), 0) % EZ
    end = ((lane == 0) & (level == 0)) | ((lane == NP - 1) & (level == EZ - 1))
    return jnp.where(end, 2.0 * share, share)


def first_plane(x):
    return jnp.where(lanes() < 64, roll_lanes(x, 64), 0.0)


def last_plane(x):
    return jnp.where(lanes() >= 64, roll_lanes(x, 64), 0.0)


def first_row(x):
    return jnp.where(lanes() // NP % NP == 0, roll_lanes(x, 72), 0.0)


def last_row(x):
    return jnp.where(lanes() // NP % NP == NP - 1, roll_lanes(x, 56), 0.0)


def swap_lanes(x, step):
    flat = x.reshape(-1, 128)
    lane = lax.broadcasted_iota(jnp.int32, flat.shape, 1)
    place = lane // step % NP
    move = jnp.where(place == 0, 7 * step, jnp.where(place == NP - 1, -7 * step, 0))
    return jnp.take_along_axis(flat, lane + move, axis=1, mode="promise_in_bounds").reshape(x.shape)


def from_rows(before, after):
    row_y = lanes() // NP % NP
    return swap_lanes(
        jnp.where(row_y == NP - 1, before, jnp.where(row_y == 0, after, 0.0)), NP
    )


def roll_lanes(x, shift):
    return pltpu.roll(x.reshape(-1, 128), shift, 1).reshape(x.shape)


def sum_levels(col):
    rows = col.shape[0]
    row_z = lanes() % NP
    level = lax.broadcasted_iota(jnp.int32, (rows, 1), 0) % EZ
    swapped = swap_lanes(col, 1)
    up = pltpu.roll(swapped, 1, 0)
    down = pltpu.roll(swapped, rows - 1, 0)
    kept = jnp.where(
        (row_z == 0) & (level > 0), up, jnp.where((row_z == NP - 1) & (level < EZ - 1), down, 0.0)
    )
    return col + kept


def blocks(col, length=EY):
    return col.reshape(-1, length, EZ, 128)


def assemble_inside(cols):
    cols = [blocks(col) for col in cols]
    edge = jnp.zeros((1, EY, EZ, 128), F32)
    cols = [
        cols[0] + jnp.concatenate([edge, first_plane(cols[3][: EX - 1])], 0),
        cols[1],
        cols[2],
        cols[3] + jnp.concatenate([last_plane(cols[0][1:]), edge], 0),
    ]
    edge = jnp.zeros((EX, 1, EZ, 128), F32)
    result = []
    for col in cols:
        before = jnp.concatenate([edge, col[:, : EY - 1]], 1)
        after = jnp.concatenate([col[:, 1:], edge], 1)
        result.append(sum_levels((col + from_rows(before, after)).reshape(ROWS, 128)))
    return result


def joined_x(middle, left, right):
    middle, left, right = list(middle), list(left), list(right)
    low, high = middle[0], middle[3]
    hole = jnp.zeros_like(low[1:])
    middle[0] = low + jnp.concatenate([first_plane(left[3]), hole], 0)
    middle[3] = high + jnp.concatenate([hole, last_plane(right[0])], 0)
    left[3] = left[3] + last_plane(low[:1])
    right[0] = right[0] + first_plane(high[EX - 1 :])
    return [jnp.concatenate(parts, 0) for parts in zip(left, middle, right)]


def joined_y(middle, below, above):
    first, last = middle[:, :1], middle[:, EY - 1 :]
    hole = jnp.zeros_like(middle[:, 1 : EY - 1])
    middle = middle + jnp.concatenate([first_row(below), hole, last_row(above)], 1)
    return jnp.concatenate([below + last_row(first), middle, above + first_row(last)], 1)


def assemble_wide(cols):
    cols = [
        cols[0][1:-1] + first_plane(cols[3][:-2]),
        cols[1][1:-1],
        cols[2][1:-1],
        cols[3][1:-1] + last_plane(cols[0][2:]),
    ]
    return [
        sum_levels((col[:, 1:-1] + from_rows(col[:, :-2], col[:, 2:])).reshape(ROWS, 128))
        for col in cols
    ]


def is_even(axis):
    return lax.rem(lax.axis_index("gx" if axis == "gx" else "gl"), 2) == 0


def write_sides(axis, first_ref, second_ref, at, low, high):
    even = is_even(axis)
    first_ref[at] = jnp.where(even, high, low)
    second_ref[at] = jnp.where(even, low, high)


class Side:
    def __init__(self, axis, even_ref, odd_ref):
        self.even, self.refs = is_even(axis), (even_ref, odd_ref)
        self.shape = even_ref.shape

    def __getitem__(self, at):
        return jnp.where(self.even, self.refs[0][at], self.refs[1][at])


def sides_of(axis, first_ref, second_ref):
    return Side(axis, second_ref, first_ref), Side(axis, first_ref, second_ref)


def write_faces(cols, part_ref, face_left_ref, face_right_ref, face_low_ref, face_high_ref):
    row_y = lanes() // NP % NP
    for c in range(4):
        part_ref[:, 128 * c : 128 * c + 128] = cols[c]
    write_sides("gx", face_left_ref, face_right_ref, ..., cols[0][:64], cols[3][192:])
    low = jnp.zeros((64, 128), F32)
    high = jnp.zeros((64, 128), F32)
    for c in range(4):
        split = cols[c].reshape(EX, EY, EZ, 128)
        first = jnp.where(row_y == 0, split[:, 0].reshape(64, 128), 0.0)
        last = jnp.where(row_y == NP - 1, split[:, EY - 1].reshape(64, 128), 0.0)
        low = low + (pltpu.roll(first, 8 * c, 1) if c else first)
        high = high + pltpu.roll(last, (72 + 8 * c) % 128, 1)
    write_sides("gy", face_low_ref, face_high_ref, ..., low, high)


def write_planes(cols, part_ref, below_ref, above_ref):
    for c in range(4):
        at = slice(128 * c, 128 * c + 128)
        part_ref[:, at] = cols[c]
        write_plane_pair(cols[c], below_ref, above_ref, at)


def write_plane_pair(col, first_ref, second_ref, at):
    low, high = blocks(col)[:, 0].reshape(64, 128), blocks(col)[:, EY - 1].reshape(64, 128)
    write_sides("gy", first_ref, second_ref, (slice(None), at), low, high)


def faces_added(part_ref, before_x_ref, after_x_ref, before_y_ref, after_y_ref):
    lane = lanes()
    row_y = lane // NP % NP
    rest = jnp.zeros((192, 128), F32)
    before = jnp.where(lane < 64, pltpu.roll(before_x_ref[...], 64, 1), 0.0)
    after = jnp.where(lane >= 64, pltpu.roll(after_x_ref[...], 64, 1), 0.0)
    none = jnp.zeros((ROWS, 128), F32)
    over_x = [jnp.concatenate([before, rest], 0), none, none, jnp.concatenate([rest, after], 0)]
    before_y, after_y = before_y_ref[...], after_y_ref[...]
    hole = jnp.zeros((EX, EY - 2, EZ, 128), F32)
    own, over_y = [], []
    for c in range(4):
        own.append(part_ref[:, 128 * c : 128 * c + 128])
        low = pltpu.roll(before_y, (128 - 8 * c) % 128, 1) if c else before_y
        low = jnp.where(row_y == 0, low, 0.0).reshape(EX, 1, EZ, 128)
        high = jnp.where(row_y == NP - 1, pltpu.roll(after_y, 56 - 8 * c, 1), 0.0)
        high = high.reshape(EX, 1, EZ, 128)
        over_y.append(jnp.concatenate([low, hole, high], 1).reshape(ROWS, 128))
    return own, over_x, over_y


EDGES = ((-1, -1, 0, 0, 0), (-1, 1, 48, 0, 56), (1, -1, 192, 3, 64), (1, 1, 240, 3, 120))


def over_lanes(x):
    for shift in (8, 16, 32, 64):
        x = x + pltpu.roll(x, shift, 1)
    return x


def diagonal_of(side_x, side_y):
    count_x, count_y = lax.axis_size("gx"), lax.axis_size(GY)
    at_y = lax.axis_index("gh") * lax.axis_size("gl") + lax.axis_index("gl")
    at_x = lax.rem(lax.axis_index("gx") + count_x + side_x, count_x)
    return at_x * count_y + lax.rem(at_y + count_y + side_y, count_y)


def edge_out(part_ref, row, block, first):
    lane = lanes()
    piece = part_ref[row : row + EZ, 128 * block : 128 * block + 128]
    piece = over_lanes(jnp.where((lane >= first) & (lane < first + NP), piece, 0.0))
    level = lax.broadcasted_iota(jnp.int32, (EZ, 1), 0)
    return jnp.sum(jnp.where(lane // NP == level, piece, 0.0), axis=0, keepdims=True)


def edge_in(line, first):
    lane = lanes()
    line = jnp.where(is_number(lane), pltpu.roll(line, 127, 1), line)
    level = lax.broadcasted_iota(jnp.int32, (EZ, 1), 0)
    spread = over_lanes(jnp.where(lane // NP == level, line, 0.0))
    return jnp.where((lane >= first) & (lane < first + NP), spread, 0.0)


def is_number(lane):
    return (lane % NP == NP - 1) & (lane < 4 * NP)


def factor_rows(ref, at):
    return ref[24 * at : 24 * at + 24, :]


def align_rows(ref, out_ref):
    count = out_ref.shape[0] // 24
    for at in range(count):
        if at < count - 1:
            block = ref[pl.ds(LEVELS * at, 24), :]
        else:
            block = pltpu.roll(ref[pl.ds(LEVELS * count - 24, 24), :], LEVELS, 0)
        out_ref[24 * at : 24 * at + 24, :] = block


def loads_of(unassembled, loads, leaf_ref, column_ref, top_ref, coeff_ref, leaf_out_ref, numbers):
    corner = product(unassembled, loads)
    lane = lanes()
    pad = jnp.zeros((8, 128), F32)
    lifted = []
    for at in range(EX * EY):
        piece = corner[16 * at : 16 * at + 16]
        same = jnp.concatenate([jnp.where(lane % 2 == 0, piece, 0.0), pad], 0)
        above = jnp.concatenate([jnp.where(lane % 2 == 1, piece, 0.0), pad], 0)
        lifted.append(same + pltpu.roll(above, 1, 0))
    top_sum = jnp.zeros((24, 256), F32)
    column_sum = jnp.zeros((24, 256), F32)
    leaf_sum = jnp.zeros((24, 256), F32)
    for vx in range(EX + 1):
        for vy in range(EY + 1):
            total = jnp.zeros((24, 128), F32)
            for sx in (0, 1):
                for sy in (0, 1):
                    if 0 <= vx - sx < EX and 0 <= vy - sy < EY:
                        piece = lifted[(vx - sx) * EY + vy - sy]
                        total = total + jnp.where(lane // 2 == sx * 2 + sy, piece, 0.0)
            vertex = jnp.sum(total, axis=1, keepdims=True)
            at = vx * (EY + 1) + vy
            top_sum = top_sum + factor_rows(top_ref, at) * vertex
            if 0 < vx < EX:
                column_sum = column_sum + factor_rows(column_ref, at) * vertex
                if 0 < vy < EY:
                    leaf_sum = leaf_sum + factor_rows(leaf_ref, (vx - 1) * 3 + vy - 1) * vertex
    row = lax.broadcasted_iota(jnp.int32, (4, 1), 0)
    coeffs = jnp.where(row == 1, numbers, 0.0)
    coeffs = jnp.where(row == 0, jnp.sum(top_sum, axis=0, keepdims=True), coeffs)
    coeffs = jnp.where(row == 2, jnp.sum(column_sum, axis=0, keepdims=True), coeffs)
    coeff_ref[...] = jnp.broadcast_to(coeffs[None], coeff_ref.shape)
    leaf_out_ref[...] = jnp.sum(leaf_sum, axis=0, keepdims=True)


def coarse_of(coeffs, leaf_coeffs, spread, leaf_ref, column_ref, top_ref):
    lane = lanes()
    top, column = coeffs[0:1], coeffs[2:3]
    around = []
    for vx in range(EX + 1):
        for vy in range(EY + 1):
            at = vx * (EY + 1) + vy
            total = factor_rows(top_ref, at) * top
            if 0 < vx < EX:
                total = total + factor_rows(column_ref, at) * column
                if 0 < vy < EY:
                    total = total + factor_rows(leaf_ref, (vx - 1) * 3 + vy - 1) * leaf_coeffs
            vertex = jnp.sum(total, axis=1, keepdims=True)
            same = jnp.broadcast_to(vertex, (24, 128))
            around.append(jnp.where(lane % 2 == 0, same, pltpu.roll(same, 23, 0))[:16])
    corners = []
    for ex in range(EX):
        for ey in range(EY):
            value = jnp.zeros((16, 128), F32)
            for sx in (0, 1):
                for sy in (0, 1):
                    piece = around[(ex + sx) * (EY + 1) + ey + sy]
                    value = jnp.where(lane // 2 == sx * 2 + sy, piece, value)
            corners.append(value)
    return product(jnp.concatenate(corners, 0), spread)


def total_of(x):
    return jnp.sum(jnp.sum(x, axis=0, keepdims=True), axis=1, keepdims=True)


def numbers_row(values, width=256, step=1):
    lane = lanes(width)
    row = jnp.zeros((1, width), F32)
    for at, value in enumerate(values):
        row = jnp.where(lane == step * (at + 1) - 1, value, row)
    return row


def start_kernel(
    order_ref, forcing_ref, diffusivity_ref, reaction_ref, leaf_in_ref, column_in_ref, top_in_ref,
    loads_ref,
    part_ref, below_ref, above_ref, coeff_ref, leaf_out_ref, pair_ref, leaf_ref, column_ref, top_ref,
):
    align_rows(leaf_in_ref, leaf_ref)
    align_rows(column_in_ref, column_ref)
    align_rows(top_in_ref, top_ref)
    slot = lax.broadcasted_iota(jnp.int32, (ROWS, ROWS), 0)
    chooser = (order_ref[...] == slot).astype(F32)
    diffusion = jnp.sum(chooser * diffusivity_ref[...], axis=1, keepdims=True)
    reacting = jnp.sum(chooser * reaction_ref[...], axis=1, keepdims=True)
    pair = jnp.where(lanes() == 0, diffusion, reacting)
    pair_ref[...] = pair
    write_plane_pair(pair, below_ref, above_ref, slice(NODES, NODES + 128))
    source = permuted(chooser.astype(BF16), forcing_ref[...])
    write_planes(assemble_inside(columns(source)), part_ref, below_ref, above_ref)
    loads_of(
        source, loads_ref[...], leaf_ref, column_ref, top_ref, coeff_ref, leaf_out_ref, numbers_row([])
    )


def own_plane(ref, c, plane):
    return blocks(ref[EY * EZ * plane : EY * EZ * (plane + 1), 128 * c : 128 * c + 128])


def got_plane(ref, c, plane):
    return blocks(ref[EZ * plane : EZ * (plane + 1), 128 * c : 128 * c + 128], 1)


def middle_kernel(part_ref, below_ref, above_ref, gathered_ref, *refs):
    below_ref, above_ref = sides_of("gy", below_ref, above_ref)
    with_pair = len(refs) == 4
    low_ref, high_ref, spread_ref = refs[-3:]
    row = lax.broadcasted_iota(jnp.int32, (4, 1), 0)
    halves_of, me = gathered_ref.shape[0] // lax.axis_size("gx"), lax.axis_index("gx")
    gathered = gathered_ref[...]
    source = lax.broadcasted_iota(jnp.int32, (gathered.shape[0], 1, 1), 0) // halves_of
    mine = jnp.sum(jnp.where(source == me, gathered, 0.0), axis=0)
    coeffs = jnp.where(row < 2, jnp.sum(gathered, axis=0), mine)
    spread_ref[...] = jnp.broadcast_to(coeffs[None], spread_ref.shape)
    for c in range(4 + with_pair):
        found = []
        for plane in (0, EX - 1):
            sides = got_plane(below_ref, c, plane), got_plane(above_ref, c, plane)
            if c < 4:
                col = joined_y(own_plane(part_ref, c, plane), *sides)
            else:
                col = jnp.concatenate([sides[0], own_plane(refs[0], 0, plane), sides[1]], 1)
            found.append(col.reshape(-1, 128))
        write_sides("gx", low_ref, high_ref, (slice(None), slice(128 * c, 128 * c + 128)), *found)


def wide_field(part_ref, below_ref, above_ref, left_ref, right_ref):
    middle, left, right = [], [], []
    for c in range(4):
        at = slice(128 * c, 128 * c + 128)
        middle.append(
            joined_y(blocks(part_ref[:, at]), blocks(below_ref[:, at], 1), blocks(above_ref[:, at], 1))
        )
        left.append(blocks(left_ref[:, at], EY + 2))
        right.append(blocks(right_ref[:, at], EY + 2))
    return joined_x(middle, left, right)


def inner_rows(cols):
    return jnp.concatenate([col[1:-1, 1:-1].reshape(ROWS, 128) for col in cols], 1)


def smoothed_of(cols, scale, shape):
    halves_of = fold([col.reshape(-1, 128) for col in cols])
    back = []
    for at, half in enumerate(halves_of):
        table = part_of(shape, at)
        modes = product(half, table) * scale[:, 256 * at : 256 * at + 256]
        back.append(product(modes, table, 1))
    return assemble_wide([blocks(col, EY + 2) for col in unfold(*back)])


def stiffness_of(field, pair, stiff, rows):
    halves_of = fold(columns(field))
    done = [product(half, part_of(stiff, at)) for at, half in enumerate(halves_of)]
    stiffened = jnp.concatenate(unfold(*done), 1)
    return stiffened * pair[:, 0:1] + field * (rows[1:2] * pair[:, 1:2])


def first_kernel(
    part_ref, below_ref, above_ref, left_ref, right_ref, pair_ref, gathered_ref, leaf_in_ref,
    rows_ref, shape, spread, leaf, column, top, stiff, loads,
    source_out, search_out, scale_out, out_ref, below_out_ref, above_out_ref, coeff_ref,
    leaf_out_ref,
):
    rows = rows_ref[...]
    weight = weight_of(rows[2:3])
    below_ref, above_ref = sides_of("gy", below_ref, above_ref)
    left_ref, right_ref = sides_of("gx", left_ref, right_ref)
    field = wide_field(part_ref, below_ref, above_ref, left_ref, right_ref)
    source = inner_rows(field)
    source_out[...] = source
    own = pair_ref[...]
    at = slice(NODES, NODES + 128)
    wide_pair = jnp.concatenate(
        [blocks(below_ref[:, at], 1), blocks(own), blocks(above_ref[:, at], 1)], 1
    ).reshape(-1, 128)
    wide_pair = jnp.concatenate([left_ref[:, at], wide_pair, right_ref[:, at]], 0)
    coeffs = jnp.sum(gathered_ref[...], axis=0)
    scale = 1.0 / (wide_pair[:, 0:1] * rows[0:1] + wide_pair[:, 1:2])
    scale_out[...] = scale
    smoothed = smoothed_of(field, scale, shape)
    search = jnp.concatenate(smoothed, 1) * weight + coarse_of(
        coeffs, leaf_in_ref[...], spread[...], leaf, column, top
    )
    search_out[...] = search
    image = stiffness_of(search, own, stiff, rows)
    write_planes(assemble_inside(columns(image)), out_ref, below_out_ref, above_out_ref)
    numbers = numbers_row(
        [total_of(source * source * weight), total_of(image * source), total_of(image * image)]
    )
    loads_of(image, loads[...], leaf, column, top, coeff_ref, leaf_out_ref, numbers)


def second_kernel(
    part_ref, below_ref, above_ref, left_ref, right_ref, pair_ref, gathered_ref, leaf_in_ref,
    rows_ref, smoother_scale, shape, spread, leaf, column, top, search, source, stiff,
    image_out, second_out, out_ref, face_left_ref, face_right_ref, face_low_ref, face_high_ref, sums_ref, total_ref,
):
    rows = rows_ref[...]
    weight = weight_of(rows[2:3])
    coeffs = jnp.sum(gathered_ref[...], axis=0)
    total_ref[...] = coeffs
    norm, along, size = coeffs[1:2, 0:1], coeffs[1:2, 1:2], coeffs[1:2, 2:3]
    overlap = along / norm
    scale = 1.0 / jnp.sqrt(size)
    below_ref, above_ref = sides_of("gy", below_ref, above_ref)
    left_ref, right_ref = sides_of("gx", left_ref, right_ref)
    field = wide_field(part_ref, below_ref, above_ref, left_ref, right_ref)
    first = inner_rows(field)
    image_out[...] = first
    smoothed = smoothed_of(field, smoother_scale[...], shape)
    whole = jnp.concatenate(smoothed, 1) * weight + coarse_of(
        coeffs, leaf_in_ref[...], spread[...], leaf, column, top
    )
    second = (whole - overlap * search[...]) * scale
    second_out[...] = second
    source = source[...]
    image = stiffness_of(second, pair_ref[...], stiff, rows)
    write_faces(assemble_inside(columns(image)), out_ref, face_left_ref, face_right_ref, face_low_ref, face_high_ref)
    basis = (first - overlap * source) * scale
    sums_ref[...] = numbers_row(
        [total_of(basis * basis * weight), total_of(image * source), total_of(image * basis)], 128, NP
    )


def chooser_back(order_ref):
    slot = lax.broadcasted_iota(jnp.int32, (ROWS, ROWS), 0)
    return (order_ref[...] == slot).astype(F32).T.astype(BF16)


def last_kernel(
    part_ref, after_y_ref, before_y_ref, after_x_ref, before_x_ref, sums_in_ref, rows,
    image_ref, sums_ref,
):
    lane = lanes()
    weight = columns(weight_of(rows[2:3]))
    row = lax.broadcasted_iota(jnp.int32, (ROWS, 1), 0)
    at_y = row // EZ % EY
    row_y = lane // NP % NP
    face_y = ((row_y == 0) & (at_y == 0)) | ((row_y == NP - 1) & (at_y == EY - 1))
    face_x = {0: (lane < 64) & (row < 64), 3: (lane >= 64) & (row >= 192)}
    square = jnp.zeros((ROWS, 128), F32)
    before_x_ref, after_x_ref = sides_of("gx", before_x_ref, after_x_ref)
    before_y_ref, after_y_ref = sides_of("gy", before_y_ref, after_y_ref)
    fields = faces_added(part_ref, before_x_ref, after_x_ref, before_y_ref, after_y_ref)
    for c, (own, over_x, over_y) in enumerate(zip(*fields)):
        image = own + over_x + over_y
        image_ref[:, 128 * c : 128 * c + 128] = image
        term = image * image
        if c in face_x:
            both = 4.0 * (own + over_x) * (own + over_y)
            term = jnp.where(face_x[c] & face_y, both, term)
        square = square + term * weight[c]
    sums = jnp.where(lane == 4 * NP - 1, total_of(square), sums_in_ref[...])
    device = lax.broadcasted_iota(jnp.int32, (sums_ref.shape[0], 1), 0)
    sent = jnp.zeros(sums_ref.shape, F32)
    for side_x, side_y, first_row, block, first in EDGES:
        edge = edge_out(part_ref, first_row, block, first)
        sent = jnp.where(device == diagonal_of(side_x, side_y), edge, sent)
    sums_ref[...] = jnp.where(is_number(lane), sums, sent)


def end_kernel(
    sums_ref, coeff_ref, image_two_ref, order, search_one, search_two, source, image_one,
    pressure_out, residual_out,
):
    got = sums_ref[...]
    sums = jnp.sum(got, axis=0, keepdims=True)
    squared, dot_source, dot_basis, dot_self = (
        sums[:, NP * at + NP - 1 : NP * at + NP] for at in range(4)
    )
    device = lax.broadcasted_iota(jnp.int32, (got.shape[0], 1), 0)
    image_two = columns(image_two_ref[...])
    for side_x, side_y, first_row, block, first in EDGES:
        line = jnp.where(device == diagonal_of(side_x, side_y), got, 0.0)
        edge = edge_in(jnp.sum(line, axis=0, keepdims=True), first)
        above, below = jnp.zeros((first_row, 128), F32), jnp.zeros((ROWS - EZ - first_row, 128), F32)
        parts = [part for part in (above, edge, below) if part.shape[0]]
        image_two[block] = image_two[block] + jnp.concatenate(parts, 0)
    image_two = jnp.concatenate(image_two, 1)
    coeffs = coeff_ref[...]
    norm, along, size = coeffs[1:2, 0:1], coeffs[1:2, 1:2], coeffs[1:2, 2:3]
    beta = jnp.sqrt(norm)
    basis_norm = jnp.sqrt(squared)
    first_diag = along / norm
    first_sub = basis_norm * jnp.sqrt(size) / beta
    second_top = dot_source / (beta * basis_norm)
    second_diag = dot_basis / squared
    second_sub_squared = jnp.maximum(
        dot_self / squared - second_top * second_top - second_diag * second_diag, 0.0
    )
    first_norm = jnp.sqrt(first_diag * first_diag + first_sub * first_sub)
    cosine = first_diag / first_norm
    sine_part = first_sub / first_norm
    rotated = cosine * second_top + sine_part * second_diag
    lowered = cosine * second_diag - sine_part * second_top
    second_norm = jnp.sqrt(lowered * lowered + second_sub_squared)
    factor_two = -(lowered / second_norm) * sine_part * beta / second_norm
    factor_one = (cosine * beta - rotated * factor_two) / first_norm
    step_one = factor_one / beta
    step_two = factor_two / basis_norm
    chooser = chooser_back(order)
    pressure_out.ref[...] = permuted(
        chooser, step_one * search_one[...] + step_two * search_two[...]
    )
    pressure_out.send()
    residual_out.ref[...] = permuted(
        chooser, source[...] - step_one * image_one[...] - step_two * image_two
    )
    residual_out.send()


class Far:
    def __init__(self, value):
        self.value = value


class Fetch:
    def __init__(self, source, target, sem):
        self.copy, self.target, self.waiting = pltpu.make_async_copy(source, target, sem), target, True
        self.copy.start()

    def __call__(self):
        if self.waiting:
            self.copy.wait()
            self.waiting = False
        return self.target


class Store:
    def __init__(self, ref, target, sem):
        self.ref, self.copy = ref, pltpu.make_async_copy(ref, target, sem)

    def send(self):
        self.copy.start()


def shaped(*shape):
    return jax.ShapeDtypeStruct(shape, F32)


def run(kernel, outs, *args):
    vmem, far = pl.BlockSpec(memory_space=pltpu.VMEM), pl.BlockSpec(memory_space=pltpu.HBM)
    far_in = [isinstance(arg, Far) for arg in args]
    far_out = [isinstance(out, Far) for out in outs]
    args = [arg.value if isinstance(arg, Far) else arg for arg in args]
    outs = [out.value if isinstance(out, Far) else out for out in outs]
    moved = [arg for arg, out_of in zip(args, far_in) if out_of]
    moved += [out for out, out_of in zip(outs, far_out) if out_of]
    count = len(moved)

    def body(*refs):
        ins, rest = refs[: len(args)], refs[len(args) :]
        results, scratch = rest[: len(outs)], rest[len(outs) :]
        at, given, stores = 0, [], []
        for ref, is_far in zip(ins, far_in):
            if is_far:
                ref = Fetch(ref, scratch[at], scratch[count].at[at])
                at += 1
            given.append(ref)
        for ref, is_far in zip(results, far_out):
            if is_far:
                ref = Store(scratch[at], ref, scratch[count].at[at])
                stores.append(ref)
                at += 1
            given.append(ref)
        kernel(*given)
        for store in stores:
            store.copy.wait()

    scratch = [pltpu.VMEM(item.shape, item.dtype) for item in moved]
    if count:
        scratch.append(pltpu.SemaphoreType.DMA((count,)))
    return pl.pallas_call(
        body,
        out_shape=tuple(outs),
        in_specs=[far if is_far else vmem for is_far in far_in],
        out_specs=tuple(far if is_far else vmem for is_far in far_out),
        scratch_shapes=scratch,
        compiler_params=pltpu.CompilerParams(vmem_limit_bytes=LIMIT),
    )(*args)


LIMIT = 28 * 2**20
GY = ("gh", "gl")
NEAR = ("gx", "gh")
FIELD = shaped(ROWS, NODES)
FACE = shaped(64, 128)
PAIRS = shaped(ROWS, 128)


def neighbours(first, second, axis):
    peers = lax.axis_size(axis)
    pairs = [(i, i ^ 1) for i in range(peers)]
    others = [(i, (i + 2 * (i % 2) - 1) % peers) for i in range(peers)]
    return lax.ppermute(first, axis, pairs), lax.ppermute(second, axis, others)


def surrounded(part, low, high, coeffs, pair=None):
    wide, across = low.shape[1], (EY + 2) * EZ
    below, above = neighbours(low, high, GY)
    gathered = lax.all_to_all(coeffs, NEAR, 0, 0)
    more = () if pair is None else (pair,)
    low, high, spread = run(
        middle_kernel,
        (shaped(across, wide), shaped(across, wide), shaped(lax.axis_size("gl"), 4, 256)),
        part, below, above, gathered, *more,
    )
    left, right = neighbours(low, high, "gx")
    return part, below, above, left, right, lax.all_to_all(spread, "gl", 0, 0)


def per_device(
    forcing, element_order, diffusivity, reaction, leaf_factor, column_factor, top_factor
):
    stiff, shape, loads, spread, rows = build_tables()
    factors = [factor[0, 0] for factor in (leaf_factor, column_factor, top_factor)]
    coarse = (shaped(lax.axis_size(NEAR), 4, 256), shaped(1, 256))
    order = element_order[0]
    part, low, high, coeffs, leaves, pair, *factors = run(
        start_kernel,
        (
            FIELD, shaped(64, NODES + 128), shaped(64, NODES + 128), *coarse, PAIRS,
            *(shaped(item.shape[0] // LEVELS * 24, 256) for item in factors),
        ),
        order, forcing[0, 0], diffusivity[0], reaction[0], *factors, loads,
    )
    *around, gathered = surrounded(part, low, high, coeffs, pair)
    source, search_one, scale, part, low, high, coeffs, leaves = run(
        first_kernel,
        (
            FIELD, FIELD, shaped((EX + 2) * (EY + 2) * EZ, NODES), FIELD, shaped(64, NODES), shaped(64, NODES), *coarse,
        ),
        *around, pair, gathered, leaves, rows, shape, spread, *factors, stiff, loads,
    )
    *around, gathered = surrounded(part, low, high, coeffs)
    image_one, search_two, part, face_left, face_right, face_low, face_high, sums, coeffs = run(
        second_kernel,
        (FIELD, FIELD, FIELD, FACE, FACE, FACE, FACE, shaped(1, 128), shaped(4, 256)),
        *around, pair, gathered, leaves, rows, scale, shape, spread, *factors,
        search_one, source, stiff,
    )
    before_x, after_x = neighbours(face_left, face_right, "gx")
    before_y, after_y = neighbours(face_low, face_high, GY)
    peers = lax.axis_size(("gx", *GY))
    image_two, sums = run(
        last_kernel, (FIELD, shaped(peers, 128)),
        part, after_y, before_y, after_x, before_x, sums, rows,
    )
    sums = lax.all_to_all(sums, ("gx", *GY), 0, 0, tiled=True)
    pressure, residual = run(
        end_kernel, (Far(FIELD), Far(FIELD)),
        sums, coeffs, image_two, order, search_one, search_two, source, image_one,
    )
    return (pressure[None, None], residual[None, None])


def solution(mesh):
    count_x, count_y = mesh.devices.shape
    mesh = Mesh(mesh.devices.reshape(count_x, 2, count_y // 2), ("gx", *GY))
    field = P("gx", GY, None, None)
    row = P("gx", GY, None)
    return jax.shard_map(
        per_device,
        mesh=mesh,
        in_specs=(field, row, row, row, field, field, field),
        out_specs=(field, field),
        check_vma=False,
    )
```

```python
import jax
import jax.numpy as jnp
import numpy as np
from jax import lax
from jax.experimental import pallas as pl
from jax.experimental.pallas import tpu as pltpu
from jax.sharding import Mesh, PartitionSpec as P

NP = 8
EX = 4
EY = 4
EZ = 16
ROWS = EX * EY * EZ
NODES = NP * NP * NP
LEVELS = EZ + 1
F32 = jnp.float32
BF16 = jnp.bfloat16


def legendre_columns(points, degree):
    columns_table = np.zeros((points.shape[0], degree + 1))
    columns_table[:, 0] = 1.0
    columns_table[:, 1] = points
    for level_at in range(2, degree + 1):
        columns_table[:, level_at] = (
            (2 * level_at - 1) * points * columns_table[:, level_at - 1]
            - (level_at - 1) * columns_table[:, level_at - 2]
        ) / level_at
    return columns_table


def jacobi_eigen(symmetric, npoints):
    matrix_work = symmetric.copy()
    vectors = np.eye(npoints)
    for sweep_at in range(15):
        for first_at in range(npoints):
            for second_at in range(first_at + 1, npoints):
                off_value = matrix_work[first_at, second_at]
                gap_value = matrix_work[second_at, second_at] - matrix_work[first_at, first_at]
                root_value = np.sqrt(gap_value * gap_value + 4.0 * off_value * off_value)
                sign_value = np.where(gap_value >= 0.0, 1.0, -1.0)
                denominator = np.abs(gap_value) + root_value
                safe_denominator = np.where(denominator > 0.0, denominator, 1.0)
                tangent = sign_value * 2.0 * off_value / safe_denominator
                cosine_value = 1.0 / np.sqrt(1.0 + tangent * tangent)
                sine_value = tangent * cosine_value
                rotation = np.eye(npoints)
                rotation[first_at, first_at] = cosine_value
                rotation[second_at, second_at] = cosine_value
                rotation[first_at, second_at] = sine_value
                rotation[second_at, first_at] = -sine_value
                matrix_work = rotation.T @ matrix_work @ rotation
                vectors = vectors @ rotation
    eigvals = np.array([matrix_work[place_at, place_at] for place_at in range(npoints)])
    return (eigvals, vectors)


def gll_tables(npoints):
    degree = npoints - 1
    estimate = -np.cos(np.pi * np.arange(npoints) / degree)
    for newton_at in range(100):
        columns_table = legendre_columns(estimate, degree)
        estimate = estimate - (
            estimate * columns_table[:, degree] - columns_table[:, degree - 1]
        ) / (npoints * columns_table[:, degree])
    values = legendre_columns(estimate, degree)[:, degree]
    weights = 2.0 / (degree * (degree + 1) * values**2)
    derivative = np.zeros((npoints, npoints))
    for row_at in range(npoints):
        for column_at in range(npoints):
            if row_at != column_at:
                derivative[row_at, column_at] = (
                    values[row_at] / values[column_at] / (estimate[row_at] - estimate[column_at])
                )
    derivative[0, 0] = -degree * (degree + 1) / 4.0
    derivative[degree, degree] = degree * (degree + 1) / 4.0
    stiffness = derivative.T @ (weights[:, None] * derivative)
    inv_root = 1.0 / np.sqrt(weights)
    symmetric = inv_root[:, None] * stiffness * inv_root[None, :]
    eigvals, eigvecs = jacobi_eigen(0.5 * (symmetric + symmetric.T), npoints)
    modes = inv_root[:, None] * eigvecs
    return (estimate, weights, stiffness, eigvals, modes)


def split_pair(table):
    high = table.astype(np.float32).astype(jnp.bfloat16)
    low = (table.astype(np.float32) - high.astype(np.float32)).astype(jnp.bfloat16)
    return np.stack([high, low])


def build_tables():
    points, weights, stiffness, eigvals, modes = gll_tables(8)
    massmat = weights[:, None] * np.eye(8)
    filler = np.ones(8)
    stiff_full = (
        np.kron(np.kron(stiffness, massmat), massmat)
        + np.kron(np.kron(massmat, stiffness), massmat)
        + np.kron(np.kron(massmat, massmat), stiffness)
    )
    mass_full = np.kron(np.kron(weights, weights), weights)
    eigen_full = (
        np.kron(np.kron(eigvals, filler), filler)
        + np.kron(np.kron(filler, eigvals), filler)
        + np.kron(np.kron(filler, filler), eigvals)
    )
    linear = np.stack([(1.0 - points) / 2.0, (1.0 + points) / 2.0], 1)
    trilinear = np.kron(np.kron(linear, linear), linear)
    even_first = np.argsort([np.sign(modes[0, m]) != np.sign(modes[7, m]) for m in range(8)], kind="stable")
    first = np.kron(np.kron(modes[:4, even_first], modes), modes)
    shape_full = np.stack([first[:, :256], first[:, 256:]])
    eigen_full = eigen_full.reshape(8, 64)[even_first].reshape(-1)
    tiles = stiff_full.reshape(8, 64, 8, 64)
    near, mirrored = tiles[:4, :, :4], tiles[:4, :, :3:-1]
    stiff_full = np.stack([near + mirrored, near - mirrored]).reshape(2, 256, 256) / 2.0
    ends = np.where((np.arange(8) == 0) | (np.arange(8) == 7), 0.5, 1.0)
    share = np.kron(np.kron(ends, ends), ends)
    rows = np.zeros((8, NODES), np.float32)
    rows[0], rows[1], rows[2] = eigen_full, mass_full, share
    loads = np.zeros((NODES, 128))
    loads[:, :8] = trilinear
    return (
        jnp.asarray(split_pair(stiff_full)),
        jnp.asarray(split_pair(shape_full)),
        jnp.asarray(split_pair(loads)),
        jnp.asarray(split_pair(loads.T)),
        jnp.asarray(rows),
    )


def lanes(width=128):
    return lax.broadcasted_iota(jnp.int32, (1, width), 1)


def halves(x):
    high = x.astype(BF16)
    return high, (x - high.astype(F32)).astype(BF16)


def product(x, table, contract=0):
    high, low = halves(x)
    dims = (((1,), (contract,)), ((), ()))

    def dot(p, q):
        return lax.dot_general(p, q, dims, preferred_element_type=F32)

    return dot(high, table[0]) + (dot(low, table[0]) + dot(high, table[1]))


def fold(cols):
    far, near = pltpu.roll(cols[3], 64, 1), pltpu.roll(cols[2], 64, 1)
    even = jnp.concatenate([cols[0] + far, cols[1] + near], 1)
    return even, jnp.concatenate([cols[0] - far, cols[1] - near], 1)


def unfold(even, odd):
    total, rest = even + odd, even - odd
    last, third = pltpu.roll(rest[:, :128], 64, 1), pltpu.roll(rest[:, 128:], 64, 1)
    return [total[:, :128], total[:, 128:], third, last]


def part_of(table, at):
    return table[0, at], table[1, at]


def permuted(chooser, x):
    high, rest = x.astype(BF16), x
    rest = rest - high.astype(F32)
    mid = rest.astype(BF16)
    low = (rest - mid.astype(F32)).astype(BF16)

    def dot(q):
        return jnp.dot(chooser, q, preferred_element_type=F32)

    return dot(high) + (dot(mid) + dot(low))


def columns(x):
    return [x[:, 128 * c : 128 * c + 128] for c in range(4)]


def weight_of(share):
    lane = lanes(NODES) % NP
    level = lax.broadcasted_iota(jnp.int32, (ROWS, 1), 0) % EZ
    end = ((lane == 0) & (level == 0)) | ((lane == NP - 1) & (level == EZ - 1))
    return jnp.where(end, 2.0 * share, share)


def first_plane(x):
    return jnp.where(lanes() < 64, roll_lanes(x, 64), 0.0)


def last_plane(x):
    return jnp.where(lanes() >= 64, roll_lanes(x, 64), 0.0)


def first_row(x):
    return jnp.where(lanes() // NP % NP == 0, roll_lanes(x, 72), 0.0)


def last_row(x):
    return jnp.where(lanes() // NP % NP == NP - 1, roll_lanes(x, 56), 0.0)


def swap_lanes(x, step):
    flat = x.reshape(-1, 128)
    lane = lax.broadcasted_iota(jnp.int32, flat.shape, 1)
    place = lane // step % NP
    move = jnp.where(place == 0, 7 * step, jnp.where(place == NP - 1, -7 * step, 0))
    return jnp.take_along_axis(flat, lane + move, axis=1, mode="promise_in_bounds").reshape(x.shape)


def from_rows(before, after):
    row_y = lanes() // NP % NP
    return swap_lanes(
        jnp.where(row_y == NP - 1, before, jnp.where(row_y == 0, after, 0.0)), NP
    )


def roll_lanes(x, shift):
    return pltpu.roll(x.reshape(-1, 128), shift, 1).reshape(x.shape)


def sum_levels(col):
    rows = col.shape[0]
    row_z = lanes() % NP
    level = lax.broadcasted_iota(jnp.int32, (rows, 1), 0) % EZ
    swapped = swap_lanes(col, 1)
    up = pltpu.roll(swapped, 1, 0)
    down = pltpu.roll(swapped, rows - 1, 0)
    kept = jnp.where(
        (row_z == 0) & (level > 0), up, jnp.where((row_z == NP - 1) & (level < EZ - 1), down, 0.0)
    )
    return col + kept


def blocks(col, length=EY):
    return col.reshape(-1, length, EZ, 128)


def assemble_inside(cols):
    cols = [blocks(col) for col in cols]
    edge = jnp.zeros((1, EY, EZ, 128), F32)
    cols = [
        cols[0] + jnp.concatenate([edge, first_plane(cols[3][: EX - 1])], 0),
        cols[1],
        cols[2],
        cols[3] + jnp.concatenate([last_plane(cols[0][1:]), edge], 0),
    ]
    edge = jnp.zeros((EX, 1, EZ, 128), F32)
    result = []
    for col in cols:
        before = jnp.concatenate([edge, col[:, : EY - 1]], 1)
        after = jnp.concatenate([col[:, 1:], edge], 1)
        result.append(sum_levels((col + from_rows(before, after)).reshape(ROWS, 128)))
    return result


def joined_x(middle, left, right):
    middle, left, right = list(middle), list(left), list(right)
    low, high = middle[0], middle[3]
    hole = jnp.zeros_like(low[1:])
    middle[0] = low + jnp.concatenate([first_plane(left[3]), hole], 0)
    middle[3] = high + jnp.concatenate([hole, last_plane(right[0])], 0)
    left[3] = left[3] + last_plane(low[:1])
    right[0] = right[0] + first_plane(high[EX - 1 :])
    return [jnp.concatenate(parts, 0) for parts in zip(left, middle, right)]


def joined_y(middle, below, above):
    first, last = middle[:, :1], middle[:, EY - 1 :]
    hole = jnp.zeros_like(middle[:, 1 : EY - 1])
    middle = middle + jnp.concatenate([first_row(below), hole, last_row(above)], 1)
    return jnp.concatenate([below + last_row(first), middle, above + first_row(last)], 1)


def assemble_wide(cols):
    cols = [
        cols[0][1:-1] + first_plane(cols[3][:-2]),
        cols[1][1:-1],
        cols[2][1:-1],
        cols[3][1:-1] + last_plane(cols[0][2:]),
    ]
    return [
        sum_levels((col[:, 1:-1] + from_rows(col[:, :-2], col[:, 2:])).reshape(ROWS, 128))
        for col in cols
    ]


def is_even(axis):
    return lax.rem(lax.axis_index("gx" if axis == "gx" else "gl"), 2) == 0


def write_sides(axis, first_ref, second_ref, at, low, high):
    even = is_even(axis)
    first_ref[at] = jnp.where(even, high, low)
    second_ref[at] = jnp.where(even, low, high)


class Side:
    def __init__(self, axis, even_ref, odd_ref):
        self.even, self.refs = is_even(axis), (even_ref, odd_ref)
        self.shape = even_ref.shape

    def __getitem__(self, at):
        return jnp.where(self.even, self.refs[0][at], self.refs[1][at])


def sides_of(axis, first_ref, second_ref):
    return Side(axis, second_ref, first_ref), Side(axis, first_ref, second_ref)


def write_faces(cols, part_ref, face_left_ref, face_right_ref, face_low_ref, face_high_ref):
    row_y = lanes() // NP % NP
    for c in range(4):
        part_ref[:, 128 * c : 128 * c + 128] = cols[c]
    write_sides("gx", face_left_ref, face_right_ref, ..., cols[0][:64], cols[3][192:])
    low = jnp.zeros((64, 128), F32)
    high = jnp.zeros((64, 128), F32)
    for c in range(4):
        split = cols[c].reshape(EX, EY, EZ, 128)
        first = jnp.where(row_y == 0, split[:, 0].reshape(64, 128), 0.0)
        last = jnp.where(row_y == NP - 1, split[:, EY - 1].reshape(64, 128), 0.0)
        low = low + (pltpu.roll(first, 8 * c, 1) if c else first)
        high = high + pltpu.roll(last, (72 + 8 * c) % 128, 1)
    write_sides("gy", face_low_ref, face_high_ref, ..., low, high)


def write_planes(cols, part_ref, below_ref, above_ref):
    for c in range(4):
        at = slice(128 * c, 128 * c + 128)
        part_ref[:, at] = cols[c]
        write_plane_pair(cols[c], below_ref, above_ref, at)


def write_plane_pair(col, first_ref, second_ref, at):
    low, high = blocks(col)[:, 0].reshape(64, 128), blocks(col)[:, EY - 1].reshape(64, 128)
    write_sides("gy", first_ref, second_ref, (slice(None), at), low, high)


def faces_added(part_ref, before_x_ref, after_x_ref, before_y_ref, after_y_ref):
    lane = lanes()
    row_y = lane // NP % NP
    rest = jnp.zeros((192, 128), F32)
    before = jnp.where(lane < 64, pltpu.roll(before_x_ref[...], 64, 1), 0.0)
    after = jnp.where(lane >= 64, pltpu.roll(after_x_ref[...], 64, 1), 0.0)
    none = jnp.zeros((ROWS, 128), F32)
    over_x = [jnp.concatenate([before, rest], 0), none, none, jnp.concatenate([rest, after], 0)]
    before_y, after_y = before_y_ref[...], after_y_ref[...]
    hole = jnp.zeros((EX, EY - 2, EZ, 128), F32)
    own, over_y = [], []
    for c in range(4):
        own.append(part_ref[:, 128 * c : 128 * c + 128])
        low = pltpu.roll(before_y, (128 - 8 * c) % 128, 1) if c else before_y
        low = jnp.where(row_y == 0, low, 0.0).reshape(EX, 1, EZ, 128)
        high = jnp.where(row_y == NP - 1, pltpu.roll(after_y, 56 - 8 * c, 1), 0.0)
        high = high.reshape(EX, 1, EZ, 128)
        over_y.append(jnp.concatenate([low, hole, high], 1).reshape(ROWS, 128))
    return own, over_x, over_y


EDGES = ((-1, -1, 0, 0, 0), (-1, 1, 48, 0, 56), (1, -1, 192, 3, 64), (1, 1, 240, 3, 120))


def over_lanes(x):
    for shift in (8, 16, 32, 64):
        x = x + pltpu.roll(x, shift, 1)
    return x


def diagonal_of(side_x, side_y):
    count_x, count_y = lax.axis_size("gx"), lax.axis_size(GY)
    at_y = lax.axis_index("gh") * lax.axis_size("gl") + lax.axis_index("gl")
    at_x = lax.rem(lax.axis_index("gx") + count_x + side_x, count_x)
    return at_x * count_y + lax.rem(at_y + count_y + side_y, count_y)


def edge_out(part_ref, row, block, first):
    lane = lanes()
    piece = part_ref[row : row + EZ, 128 * block : 128 * block + 128]
    piece = over_lanes(jnp.where((lane >= first) & (lane < first + NP), piece, 0.0))
    level = lax.broadcasted_iota(jnp.int32, (EZ, 1), 0)
    return jnp.sum(jnp.where(lane // NP == level, piece, 0.0), axis=0, keepdims=True)


def edge_in(line, first):
    lane = lanes()
    line = jnp.where(is_number(lane), pltpu.roll(line, 127, 1), line)
    level = lax.broadcasted_iota(jnp.int32, (EZ, 1), 0)
    spread = over_lanes(jnp.where(lane // NP == level, line, 0.0))
    return jnp.where((lane >= first) & (lane < first + NP), spread, 0.0)


def is_number(lane):
    return (lane % NP == NP - 1) & (lane < 4 * NP)


def factor_rows(ref, at):
    return ref[24 * at : 24 * at + 24, :]


def align_rows(ref, out_ref):
    count = out_ref.shape[0] // 24
    for at in range(count):
        if at < count - 1:
            block = ref[pl.ds(LEVELS * at, 24), :]
        else:
            block = pltpu.roll(ref[pl.ds(LEVELS * count - 24, 24), :], LEVELS, 0)
        out_ref[24 * at : 24 * at + 24, :] = block


def loads_of(unassembled, loads, leaf_ref, column_ref, top_ref, coeff_ref, leaf_out_ref, numbers):
    corner = product(unassembled, loads)
    lane = lanes()
    pad = jnp.zeros((8, 128), F32)
    lifted = []
    for at in range(EX * EY):
        piece = corner[16 * at : 16 * at + 16]
        same = jnp.concatenate([jnp.where(lane % 2 == 0, piece, 0.0), pad], 0)
        above = jnp.concatenate([jnp.where(lane % 2 == 1, piece, 0.0), pad], 0)
        lifted.append(same + pltpu.roll(above, 1, 0))
    top_sum = jnp.zeros((24, 256), F32)
    column_sum = jnp.zeros((24, 256), F32)
    leaf_sum = jnp.zeros((24, 256), F32)
    for vx in range(EX + 1):
        for vy in range(EY + 1):
            total = jnp.zeros((24, 128), F32)
            for sx in (0, 1):
                for sy in (0, 1):
                    if 0 <= vx - sx < EX and 0 <= vy - sy < EY:
                        piece = lifted[(vx - sx) * EY + vy - sy]
                        total = total + jnp.where(lane // 2 == sx * 2 + sy, piece, 0.0)
            vertex = jnp.sum(total, axis=1, keepdims=True)
            at = vx * (EY + 1) + vy
            top_sum = top_sum + factor_rows(top_ref, at) * vertex
            if 0 < vx < EX:
                column_sum = column_sum + factor_rows(column_ref, at) * vertex
                if 0 < vy < EY:
                    leaf_sum = leaf_sum + factor_rows(leaf_ref, (vx - 1) * 3 + vy - 1) * vertex
    row = lax.broadcasted_iota(jnp.int32, (4, 1), 0)
    coeffs = jnp.where(row == 1, numbers, 0.0)
    coeffs = jnp.where(row == 0, jnp.sum(top_sum, axis=0, keepdims=True), coeffs)
    coeffs = jnp.where(row == 2, jnp.sum(column_sum, axis=0, keepdims=True), coeffs)
    coeff_ref[...] = jnp.broadcast_to(coeffs[None], coeff_ref.shape)
    leaf_out_ref[...] = jnp.sum(leaf_sum, axis=0, keepdims=True)


def coarse_of(coeffs, leaf_coeffs, spread, leaf_ref, column_ref, top_ref):
    lane = lanes()
    top, column = coeffs[0:1], coeffs[2:3]
    around = []
    for vx in range(EX + 1):
        for vy in range(EY + 1):
            at = vx * (EY + 1) + vy
            total = factor_rows(top_ref, at) * top
            if 0 < vx < EX:
                total = total + factor_rows(column_ref, at) * column
                if 0 < vy < EY:
                    total = total + factor_rows(leaf_ref, (vx - 1) * 3 + vy - 1) * leaf_coeffs
            vertex = jnp.sum(total, axis=1, keepdims=True)
            same = jnp.broadcast_to(vertex, (24, 128))
            around.append(jnp.where(lane % 2 == 0, same, pltpu.roll(same, 23, 0))[:16])
    corners = []
    for ex in range(EX):
        for ey in range(EY):
            value = jnp.zeros((16, 128), F32)
            for sx in (0, 1):
                for sy in (0, 1):
                    piece = around[(ex + sx) * (EY + 1) + ey + sy]
                    value = jnp.where(lane // 2 == sx * 2 + sy, piece, value)
            corners.append(value)
    return product(jnp.concatenate(corners, 0), spread)


def total_of(x):
    return jnp.sum(jnp.sum(x, axis=0, keepdims=True), axis=1, keepdims=True)


def numbers_row(values, width=256, step=1):
    lane = lanes(width)
    row = jnp.zeros((1, width), F32)
    for at, value in enumerate(values):
        row = jnp.where(lane == step * (at + 1) - 1, value, row)
    return row


def start_kernel(
    order_ref, forcing_ref, diffusivity_ref, reaction_ref, leaf_in_ref, column_in_ref, top_in_ref,
    loads_ref,
    part_ref, below_ref, above_ref, coeff_ref, leaf_out_ref, pair_ref, leaf_ref, column_ref, top_ref,
):
    align_rows(leaf_in_ref, leaf_ref)
    align_rows(column_in_ref, column_ref)
    align_rows(top_in_ref, top_ref)
    slot = lax.broadcasted_iota(jnp.int32, (ROWS, ROWS), 0)
    chooser = (order_ref[...] == slot).astype(F32)
    diffusion = jnp.sum(chooser * diffusivity_ref[...], axis=1, keepdims=True)
    reacting = jnp.sum(chooser * reaction_ref[...], axis=1, keepdims=True)
    pair = jnp.where(lanes() == 0, diffusion, reacting)
    pair_ref[...] = pair
    write_plane_pair(pair, below_ref, above_ref, slice(NODES, NODES + 128))
    source = permuted(chooser.astype(BF16), forcing_ref[...])
    write_planes(assemble_inside(columns(source)), part_ref, below_ref, above_ref)
    loads_of(
        source, loads_ref[...], leaf_ref, column_ref, top_ref, coeff_ref, leaf_out_ref, numbers_row([])
    )


def own_plane(ref, c, plane):
    return blocks(ref[EY * EZ * plane : EY * EZ * (plane + 1), 128 * c : 128 * c + 128])


def got_plane(ref, c, plane):
    return blocks(ref[EZ * plane : EZ * (plane + 1), 128 * c : 128 * c + 128], 1)


def middle_kernel(part_ref, below_ref, above_ref, gathered_ref, *refs):
    below_ref, above_ref = sides_of("gy", below_ref, above_ref)
    with_pair = len(refs) == 4
    low_ref, high_ref, spread_ref = refs[-3:]
    row = lax.broadcasted_iota(jnp.int32, (4, 1), 0)
    halves_of, me = gathered_ref.shape[0] // lax.axis_size("gx"), lax.axis_index("gx")
    gathered = gathered_ref[...]
    source = lax.broadcasted_iota(jnp.int32, (gathered.shape[0], 1, 1), 0) // halves_of
    mine = jnp.sum(jnp.where(source == me, gathered, 0.0), axis=0)
    coeffs = jnp.where(row < 2, jnp.sum(gathered, axis=0), mine)
    spread_ref[...] = jnp.broadcast_to(coeffs[None], spread_ref.shape)
    for c in range(4 + with_pair):
        found = []
        for plane in (0, EX - 1):
            sides = got_plane(below_ref, c, plane), got_plane(above_ref, c, plane)
            if c < 4:
                col = joined_y(own_plane(part_ref, c, plane), *sides)
            else:
                col = jnp.concatenate([sides[0], own_plane(refs[0], 0, plane), sides[1]], 1)
            found.append(col.reshape(-1, 128))
        write_sides("gx", low_ref, high_ref, (slice(None), slice(128 * c, 128 * c + 128)), *found)


def wide_field(part_ref, below_ref, above_ref, left_ref, right_ref):
    middle, left, right = [], [], []
    for c in range(4):
        at = slice(128 * c, 128 * c + 128)
        middle.append(
            joined_y(blocks(part_ref[:, at]), blocks(below_ref[:, at], 1), blocks(above_ref[:, at], 1))
        )
        left.append(blocks(left_ref[:, at], EY + 2))
        right.append(blocks(right_ref[:, at], EY + 2))
    return joined_x(middle, left, right)


def inner_rows(cols):
    return jnp.concatenate([col[1:-1, 1:-1].reshape(ROWS, 128) for col in cols], 1)


def smoothed_of(cols, scale, shape):
    halves_of = fold([col.reshape(-1, 128) for col in cols])
    back = []
    for at, half in enumerate(halves_of):
        table = part_of(shape, at)
        modes = product(half, table) * scale[:, 256 * at : 256 * at + 256]
        back.append(product(modes, table, 1))
    return assemble_wide([blocks(col, EY + 2) for col in unfold(*back)])


def stiffness_of(field, pair, stiff, rows):
    halves_of = fold(columns(field))
    done = [product(half, part_of(stiff, at)) for at, half in enumerate(halves_of)]
    stiffened = jnp.concatenate(unfold(*done), 1)
    return stiffened * pair[:, 0:1] + field * (rows[1:2] * pair[:, 1:2])


def first_kernel(
    part_ref, below_ref, above_ref, left_ref, right_ref, pair_ref, gathered_ref, leaf_in_ref,
    rows_ref, shape, spread, leaf, column, top, stiff, loads,
    source_out, search_out, scale_out, out_ref, below_out_ref, above_out_ref, coeff_ref,
    leaf_out_ref,
):
    rows = rows_ref[...]
    weight = weight_of(rows[2:3])
    below_ref, above_ref = sides_of("gy", below_ref, above_ref)
    left_ref, right_ref = sides_of("gx", left_ref, right_ref)
    field = wide_field(part_ref, below_ref, above_ref, left_ref, right_ref)
    source = inner_rows(field)
    source_out[...] = source
    own = pair_ref[...]
    at = slice(NODES, NODES + 128)
    wide_pair = jnp.concatenate(
        [blocks(below_ref[:, at], 1), blocks(own), blocks(above_ref[:, at], 1)], 1
    ).reshape(-1, 128)
    wide_pair = jnp.concatenate([left_ref[:, at], wide_pair, right_ref[:, at]], 0)
    coeffs = jnp.sum(gathered_ref[...], axis=0)
    scale = 1.0 / (wide_pair[:, 0:1] * rows[0:1] + wide_pair[:, 1:2])
    scale_out[...] = scale
    smoothed = smoothed_of(field, scale, shape)
    search = jnp.concatenate(smoothed, 1) * weight + coarse_of(
        coeffs, leaf_in_ref[...], spread[...], leaf, column, top
    )
    search_out[...] = search
    image = stiffness_of(search, own, stiff, rows)
    write_planes(assemble_inside(columns(image)), out_ref, below_out_ref, above_out_ref)
    numbers = numbers_row(
        [total_of(source * source * weight), total_of(image * source), total_of(image * image)]
    )
    loads_of(image, loads[...], leaf, column, top, coeff_ref, leaf_out_ref, numbers)


def second_kernel(
    part_ref, below_ref, above_ref, left_ref, right_ref, pair_ref, gathered_ref, leaf_in_ref,
    rows_ref, smoother_scale, shape, spread, leaf, column, top, search, source, stiff,
    image_out, second_out, out_ref, face_left_ref, face_right_ref, face_low_ref, face_high_ref, sums_ref, total_ref,
):
    rows = rows_ref[...]
    weight = weight_of(rows[2:3])
    coeffs = jnp.sum(gathered_ref[...], axis=0)
    total_ref[...] = coeffs
    norm, along, size = coeffs[1:2, 0:1], coeffs[1:2, 1:2], coeffs[1:2, 2:3]
    overlap = along / norm
    scale = 1.0 / jnp.sqrt(size)
    below_ref, above_ref = sides_of("gy", below_ref, above_ref)
    left_ref, right_ref = sides_of("gx", left_ref, right_ref)
    field = wide_field(part_ref, below_ref, above_ref, left_ref, right_ref)
    first = inner_rows(field)
    image_out[...] = first
    smoothed = smoothed_of(field, smoother_scale[...], shape)
    whole = jnp.concatenate(smoothed, 1) * weight + coarse_of(
        coeffs, leaf_in_ref[...], spread[...], leaf, column, top
    )
    second = (whole - overlap * search[...]) * scale
    second_out[...] = second
    source = source[...]
    image = stiffness_of(second, pair_ref[...], stiff, rows)
    write_faces(assemble_inside(columns(image)), out_ref, face_left_ref, face_right_ref, face_low_ref, face_high_ref)
    basis = (first - overlap * source) * scale
    sums_ref[...] = numbers_row(
        [total_of(basis * basis * weight), total_of(image * source), total_of(image * basis)], 128, NP
    )


def chooser_back(order_ref):
    slot = lax.broadcasted_iota(jnp.int32, (ROWS, ROWS), 0)
    return (order_ref[...] == slot).astype(F32).T.astype(BF16)


def last_kernel(
    part_ref, after_y_ref, before_y_ref, after_x_ref, before_x_ref, sums_in_ref, rows,
    image_ref, sums_ref,
):
    lane = lanes()
    weight = columns(weight_of(rows[2:3]))
    row = lax.broadcasted_iota(jnp.int32, (ROWS, 1), 0)
    at_y = row // EZ % EY
    row_y = lane // NP % NP
    face_y = ((row_y == 0) & (at_y == 0)) | ((row_y == NP - 1) & (at_y == EY - 1))
    face_x = {0: (lane < 64) & (row < 64), 3: (lane >= 64) & (row >= 192)}
    square = jnp.zeros((ROWS, 128), F32)
    before_x_ref, after_x_ref = sides_of("gx", before_x_ref, after_x_ref)
    before_y_ref, after_y_ref = sides_of("gy", before_y_ref, after_y_ref)
    fields = faces_added(part_ref, before_x_ref, after_x_ref, before_y_ref, after_y_ref)
    for c, (own, over_x, over_y) in enumerate(zip(*fields)):
        image = own + over_x + over_y
        image_ref[:, 128 * c : 128 * c + 128] = image
        term = image * image
        if c in face_x:
            both = 4.0 * (own + over_x) * (own + over_y)
            term = jnp.where(face_x[c] & face_y, both, term)
        square = square + term * weight[c]
    sums = jnp.where(lane == 4 * NP - 1, total_of(square), sums_in_ref[...])
    device = lax.broadcasted_iota(jnp.int32, (sums_ref.shape[0], 1), 0)
    sent = jnp.zeros(sums_ref.shape, F32)
    for side_x, side_y, first_row, block, first in EDGES:
        edge = edge_out(part_ref, first_row, block, first)
        sent = jnp.where(device == diagonal_of(side_x, side_y), edge, sent)
    sums_ref[...] = jnp.where(is_number(lane), sums, sent)


def end_kernel(
    sums_ref, coeff_ref, image_two_ref, order, search_one, search_two, source, image_one,
    pressure_out, residual_out,
):
    got = sums_ref[...]
    sums = jnp.sum(got, axis=0, keepdims=True)
    squared, dot_source, dot_basis, dot_self = (
        sums[:, NP * at + NP - 1 : NP * at + NP] for at in range(4)
    )
    device = lax.broadcasted_iota(jnp.int32, (got.shape[0], 1), 0)
    image_two = columns(image_two_ref[...])
    for side_x, side_y, first_row, block, first in EDGES:
        line = jnp.where(device == diagonal_of(side_x, side_y), got, 0.0)
        edge = edge_in(jnp.sum(line, axis=0, keepdims=True), first)
        above, below = jnp.zeros((first_row, 128), F32), jnp.zeros((ROWS - EZ - first_row, 128), F32)
        parts = [part for part in (above, edge, below) if part.shape[0]]
        image_two[block] = image_two[block] + jnp.concatenate(parts, 0)
    image_two = jnp.concatenate(image_two, 1)
    coeffs = coeff_ref[...]
    norm, along, size = coeffs[1:2, 0:1], coeffs[1:2, 1:2], coeffs[1:2, 2:3]
    beta = jnp.sqrt(norm)
    basis_norm = jnp.sqrt(squared)
    first_diag = along / norm
    first_sub = basis_norm * jnp.sqrt(size) / beta
    second_top = dot_source / (beta * basis_norm)
    second_diag = dot_basis / squared
    second_sub_squared = jnp.maximum(
        dot_self / squared - second_top * second_top - second_diag * second_diag, 0.0
    )
    first_norm = jnp.sqrt(first_diag * first_diag + first_sub * first_sub)
    cosine = first_diag / first_norm
    sine_part = first_sub / first_norm
    rotated = cosine * second_top + sine_part * second_diag
    lowered = cosine * second_diag - sine_part * second_top
    second_norm = jnp.sqrt(lowered * lowered + second_sub_squared)
    factor_two = -(lowered / second_norm) * sine_part * beta / second_norm
    factor_one = (cosine * beta - rotated * factor_two) / first_norm
    step_one = factor_one / beta
    step_two = factor_two / basis_norm
    chooser = chooser_back(order)
    pressure = step_one * search_one[...] + step_two * search_two[...]
    residual = source[...] - step_one * image_one[...] - step_two * image_two
    for field, out in ((pressure, pressure_out), (residual, residual_out)):
        for at in range(QUARTERS):
            rows = ROWS // QUARTERS
            out.send(at, permuted(chooser[rows * at : rows * (at + 1)], field))


class Far:
    def __init__(self, value):
        self.value = value


class Fetch:
    def __init__(self, source, target, sem):
        self.copy, self.target, self.waiting = pltpu.make_async_copy(source, target, sem), target, True
        self.copy.start()

    def __call__(self):
        if self.waiting:
            self.copy.wait()
            self.waiting = False
        return self.target


class Store:
    def __init__(self, ref, target, sems):
        self.ref, self.rows = ref, ref.shape[0] // QUARTERS
        spans = [pl.ds(self.rows * at, self.rows) for at in range(QUARTERS)]
        self.copies = [
            pltpu.make_async_copy(ref.at[span], target.at[span], sems[at]) for at, span in enumerate(spans)
        ]

    def send(self, at, value):
        self.ref[self.rows * at : self.rows * (at + 1)] = value
        self.copies[at].start()


def shaped(*shape):
    return jax.ShapeDtypeStruct(shape, F32)


def run(kernel, outs, *args):
    vmem, far = pl.BlockSpec(memory_space=pltpu.VMEM), pl.BlockSpec(memory_space=pltpu.HBM)
    far_in = [isinstance(arg, Far) for arg in args]
    far_out = [isinstance(out, Far) for out in outs]
    args = [arg.value if isinstance(arg, Far) else arg for arg in args]
    outs = [out.value if isinstance(out, Far) else out for out in outs]
    moved = [arg for arg, out_of in zip(args, far_in) if out_of]
    moved += [out for out, out_of in zip(outs, far_out) if out_of]
    count = len(moved)

    def body(*refs):
        ins, rest = refs[: len(args)], refs[len(args) :]
        results, scratch = rest[: len(outs)], rest[len(outs) :]
        at, given, stores = 0, [], []
        for ref, is_far in zip(ins, far_in):
            if is_far:
                ref = Fetch(ref, scratch[at], scratch[count].at[QUARTERS * at])
                at += 1
            given.append(ref)
        for ref, is_far in zip(results, far_out):
            if is_far:
                sems = [scratch[count].at[QUARTERS * at + part] for part in range(QUARTERS)]
                ref = Store(scratch[at], ref, sems)
                stores.append(ref)
                at += 1
            given.append(ref)
        kernel(*given)
        for store in stores:
            for copy in store.copies:
                copy.wait()

    scratch = [pltpu.VMEM(item.shape, item.dtype) for item in moved]
    if count:
        scratch.append(pltpu.SemaphoreType.DMA((count * QUARTERS,)))
    return pl.pallas_call(
        body,
        out_shape=tuple(outs),
        in_specs=[far if is_far else vmem for is_far in far_in],
        out_specs=tuple(far if is_far else vmem for is_far in far_out),
        scratch_shapes=scratch,
        compiler_params=pltpu.CompilerParams(vmem_limit_bytes=LIMIT),
    )(*args)


LIMIT = 28 * 2**20
QUARTERS = 4
GY = ("gh", "gl")
NEAR = ("gx", "gh")
FIELD = shaped(ROWS, NODES)
FACE = shaped(64, 128)
PAIRS = shaped(ROWS, 128)


def neighbours(first, second, axis):
    peers = lax.axis_size(axis)
    pairs = [(i, i ^ 1) for i in range(peers)]
    others = [(i, (i + 2 * (i % 2) - 1) % peers) for i in range(peers)]
    return lax.ppermute(first, axis, pairs), lax.ppermute(second, axis, others)


def surrounded(part, low, high, coeffs, pair=None):
    wide, across = low.shape[1], (EY + 2) * EZ
    below, above = neighbours(low, high, GY)
    gathered = lax.all_to_all(coeffs, NEAR, 0, 0)
    more = () if pair is None else (pair,)
    low, high, spread = run(
        middle_kernel,
        (shaped(across, wide), shaped(across, wide), shaped(lax.axis_size("gl"), 4, 256)),
        part, below, above, gathered, *more,
    )
    left, right = neighbours(low, high, "gx")
    return part, below, above, left, right, lax.all_to_all(spread, "gl", 0, 0)


def per_device(
    forcing, element_order, diffusivity, reaction, leaf_factor, column_factor, top_factor
):
    stiff, shape, loads, spread, rows = build_tables()
    factors = [factor[0, 0] for factor in (leaf_factor, column_factor, top_factor)]
    coarse = (shaped(lax.axis_size(NEAR), 4, 256), shaped(1, 256))
    order = element_order[0]
    part, low, high, coeffs, leaves, pair, *factors = run(
        start_kernel,
        (
            FIELD, shaped(64, NODES + 128), shaped(64, NODES + 128), *coarse, PAIRS,
            *(shaped(item.shape[0] // LEVELS * 24, 256) for item in factors),
        ),
        order, forcing[0, 0], diffusivity[0], reaction[0], *factors, loads,
    )
    *around, gathered = surrounded(part, low, high, coeffs, pair)
    source, search_one, scale, part, low, high, coeffs, leaves = run(
        first_kernel,
        (
            FIELD, FIELD, shaped((EX + 2) * (EY + 2) * EZ, NODES), FIELD, shaped(64, NODES), shaped(64, NODES), *coarse,
        ),
        *around, pair, gathered, leaves, rows, shape, spread, *factors, stiff, loads,
    )
    *around, gathered = surrounded(part, low, high, coeffs)
    image_one, search_two, part, face_left, face_right, face_low, face_high, sums, coeffs = run(
        second_kernel,
        (FIELD, FIELD, FIELD, FACE, FACE, FACE, FACE, shaped(1, 128), shaped(4, 256)),
        *around, pair, gathered, leaves, rows, scale, shape, spread, *factors,
        search_one, source, stiff,
    )
    before_x, after_x = neighbours(face_left, face_right, "gx")
    before_y, after_y = neighbours(face_low, face_high, GY)
    peers = lax.axis_size(("gx", *GY))
    image_two, sums = run(
        last_kernel, (FIELD, shaped(peers, 128)),
        part, after_y, before_y, after_x, before_x, sums, rows,
    )
    sums = lax.all_to_all(sums, ("gx", *GY), 0, 0, tiled=True)
    pressure, residual = run(
        end_kernel, (Far(FIELD), Far(FIELD)),
        sums, coeffs, image_two, order, search_one, search_two, source, image_one,
    )
    return (pressure[None, None], residual[None, None])


def solution(mesh):
    count_x, count_y = mesh.devices.shape
    mesh = Mesh(mesh.devices.reshape(count_x, 2, count_y // 2), ("gx", *GY))
    field = P("gx", GY, None, None)
    row = P("gx", GY, None)
    return jax.shard_map(
        per_device,
        mesh=mesh,
        in_specs=(field, row, row, row, field, field, field),
        out_specs=(field, field),
        check_vma=False,
    )
```
